128 devices in a mesh: frame: 32 (over y, z, core), coil: 4 (over x).
Axes of the slice: x: 4, y: 4, z: 4, core: 2. Of those that a mesh axis runs over, the one named last changes fastest.
Arguments:
- spatial: float32 [8, 2, 320, 320], P(None, None, 'coil', 'frame'), may hold values from -6 to 6
- temporal: float32 [64, 8], P('frame'), may hold values from -2 to 2
- sensitivity: bfloat16 [8, 2, 320, 320], P('coil'), may hold values from -5 to 5
- coil_data: bfloat16 [64, 8, 2, 320, 320], P('frame', 'coil'), may hold values from -6 to 6
- kernel_index: int32 [64, 640, 640], P('frame'), may hold values from 0 to 7
- kernel_level: float32 [64, 8], P('frame'), may hold values from 0.02 to 4
Outputs:
- spatial_next: float32 [8, 2, 320, 320], P(None, None, 'coil', 'frame')
- images: bfloat16 [64, 2, 320, 320], P('frame')
The draws below stay inside these ranges and needn't reach their ends.
All inputs are finite; a program needn't handle non-finite values.
Results may differ from the reference program's by a relative error of at most 0.001.
Values may be sent and summed in bfloat16 or wider, within the bound.
A program may use at most 128 MiB of HBM per device.

```python
import math
import jax
import jax.numpy as jnp
from jax import lax

NX = 320
NY = 320
COILS = 8
RANK = 8
LEVELS = 8
FRAMES = 64
PX = 640
PY = 640


def plant(entries, stream_key, least, largest):
    extent = entries.shape
    place = [jax.random.randint(jax.random.fold_in(stream_key, axis), (), 0, extent[axis]) for axis in range(len(extent))]
    entries = entries.at[tuple(place)].set(least)
    longest = extent.index(max(extent))
    place[longest] = (place[longest] + 1) % extent[longest]
    return entries.at[tuple(place)].set(largest)


def level_of(key, extent, pieces, low, high):
    factor_of = 1.0
    for position, parts in pieces:
        draws = jax.random.uniform(jax.random.fold_in(jax.random.fold_in(key, 6), position), (parts,), jnp.float32, low / len(pieces), high / len(pieces))
        factor_of = factor_of * jnp.repeat(jnp.exp(draws), extent[position] // parts).reshape((-1,) + (1,) * (len(extent) - 1 - position))
    return factor_of


def normal_values(key, shape, scale, bound, split=(), held_as=jnp.bfloat16):
    factor_of = level_of(key, shape, split, -0.22, 0.18) if split else 1.0
    array = jax.random.normal(key, shape, jnp.float32) * scale * factor_of
    return jnp.minimum(jnp.maximum(array, -bound), bound).astype(held_as)


def setup_inputs(seed: int = 0) -> dict:
    seeds = jax.random.split(jax.random.key(seed), 7)
    spatial = normal_values(seeds[0], (RANK, 2, NX, NY), 1.0, 6.0, ((2, 4), (3, 32)), jnp.float32)
    temporal = normal_values(seeds[1], (FRAMES, RANK), RANK ** -0.5, 2.0, ((0, 32),), jnp.float32)
    sensitivity = normal_values(seeds[2], (COILS, 2, NX, NY), 0.35, 5.0, ((0, 4),))
    coil_data = normal_values(seeds[3], (FRAMES, COILS, 2, NX, NY), 1.0, 6.0, ((0, 32), (1, 4)))
    kernel_index = plant(jax.random.randint(seeds[4], (FRAMES, PX, PY), 0, LEVELS), jax.random.fold_in(seeds[4], 1), 0, LEVELS - 1).astype(jnp.int32)
    kernel_level = jnp.clip(jnp.exp(math.log(4.0) - 5.2983174 * jax.random.uniform(seeds[5], (FRAMES, LEVELS), jnp.float32) ** level_of(seeds[5], (FRAMES, LEVELS), ((0, 32),), -0.2, 0.2)), 0.02, 4.0)
    return dict(spatial=spatial, temporal=temporal, sensitivity=sensitivity, coil_data=coil_data, kernel_index=kernel_index, kernel_level=kernel_level)


STEP_SIZE = 0.15


def rebuild(temporal, factors):
    mixed = jnp.einsum('tr,rcxy->tcxy', temporal, factors, precision=lax.Precision.HIGHEST)
    return mixed.astype(jnp.bfloat16)


def reference(spatial, temporal, sensitivity, coil_data, kernel_index, kernel_level):
    images_old = rebuild(temporal, spatial)
    sens_real = sensitivity[:, 0].astype(jnp.float32)
    sens_imag = sensitivity[:, 1].astype(jnp.float32)

    def residual_frame(items):
        image, data, index, level = items
        img = image.astype(jnp.float32)
        coil_real = sens_real * img[0] - sens_imag * img[1]
        coil_imag = sens_real * img[1] + sens_imag * img[0]
        spectrum = jnp.fft.fft2(coil_real + 1j * coil_imag, s=(PX, PY))
        kernel = level[index]
        back = jnp.fft.ifft2(spectrum * kernel)[:, :NX, :NY]
        diff_real = back.real - data[:, 0].astype(jnp.float32)
        diff_imag = back.imag - data[:, 1].astype(jnp.float32)
        res_real = jnp.sum(sens_real * diff_real + sens_imag * diff_imag, axis=0)
        res_imag = jnp.sum(sens_real * diff_imag - sens_imag * diff_real, axis=0)
        return jnp.stack([res_real, res_imag])

    residual = lax.map(residual_frame, (images_old, coil_data, kernel_index, kernel_level))
    gradient = jnp.einsum('tr,tcxy->rcxy', temporal, residual, precision=lax.Precision.HIGHEST)
    spatial_next = spatial - STEP_SIZE * gradient
    images = rebuild(temporal, spatial_next)
    return spatial_next, images
```

```python
import functools
import math

import jax
import jax.numpy as jnp
import ml_dtypes
import numpy as np
from jax import lax
from jax.experimental import pallas as pl
from jax.experimental.pallas import tpu as pltpu
from jax.sharding import PartitionSpec as P

STEP_SIZE = 0.15
BF = jnp.bfloat16
F32 = jnp.float32


def halves(table):
    high = table.astype(ml_dtypes.bfloat16)
    low = (table - high.astype(np.float64)).astype(ml_dtypes.bfloat16)
    return high, low


def make_tables(size):
    half = size // 2
    slots = -(-(size + 1) // 128) * 128
    rows = -(-(size + 1) // 16) * 16
    p = np.arange(half) + 0.5
    k = np.arange(slots)
    valid = (k <= size).astype(np.float64)
    angle = np.pi / size * np.outer(p, k)
    cos, sin = np.cos(angle) * valid, np.sin(angle) * valid
    cos[:, size] = 0.0
    sin[:, 0] = 0.0
    weight = np.where((k == 0) | (k == size), 0.5, 1.0)
    out = {}
    for name, tab in (("c", cos), ("s", sin)):
        hi, lo = halves(tab)
        out["f1" + name] = np.concatenate([hi, lo], axis=1)
        rhi, rlo = hi[:, :rows].T, lo[:, :rows].T
        out["f2" + name] = np.concatenate([rhi, rhi, rlo], axis=1)
        whi, wlo = halves(tab * weight)
        out["i1" + name] = np.concatenate([whi[:, :rows], whi[:, :rows], wlo[:, :rows]], axis=1)
        parts = []
        for j in range(0, slots, 128):
            parts += [whi.T[j:j + 128], whi.T[j:j + 128], wlo.T[j:j + 128]]
        out["i2" + name] = np.concatenate(parts, axis=0)
    wide = -(-half // 128) * 128
    place = np.zeros((size, 2 * wide))
    q = np.arange(half)
    place[half + q, q] = 1
    place[half - 1 - q, wide + q] = 1
    out["place"] = place.astype(ml_dtypes.bfloat16)
    out["unplace"] = place.T.astype(ml_dtypes.bfloat16)
    out["flip"] = np.eye(half)[::-1].astype(ml_dtypes.bfloat16)
    mirror = np.zeros((2 * size, slots))
    kk = np.arange(size + 1)
    mirror[(2 * size - kk) % (2 * size), kk] = 1
    out["mirror"] = mirror.astype(ml_dtypes.bfloat16)
    out["mirror_rows"] = mirror.T[:rows].astype(ml_dtypes.bfloat16)
    return out


TABLES = ("f1c", "f1s", "f2c", "f2s", "i1c", "i1s", "i2c", "i2s", "place", "unplace", "flip", "mirror", "mirror_rows")


def mm(a, b):
    return jnp.dot(a, b, preferred_element_type=F32)


def split(x):
    high = x.astype(BF)
    low = (x - high.astype(F32)).astype(BF)
    return high, low


def normal_kernel(level, image, sens, data, index, f1c, f1s, f2c, f2s, i1c, i1s, i2c, i2s, place, unplace, flip, mirror, mirror_rows, out, kq, sf, imf, res, lc, ls, ge, go, spa, spb, za, zb, lhc, lhs, oc, osn):
    frames, coils = image.shape[0], sens.shape[0]
    size = image.shape[2]
    half = size // 2
    wide = place.shape[1] // 2
    rows = f2c.shape[0]
    slots = mirror.shape[1]
    chunks = slots // 128
    levels = level.shape[1]

    for t in range(frames):
        ib = index[t].astype(F32).astype(BF)
        flipped = mm(ib, mirror[...]).astype(BF)
        low = mm(mirror_rows[...], jnp.concatenate([ib[:, :slots], flipped], axis=1))
        quads = (ib[:rows, :slots].astype(F32), flipped[:rows].astype(F32), low[:, :slots], low[:, slots:])
        for n, quad in enumerate(quads):
            value = jnp.full(quad.shape, level[t, 0], F32)
            for m in range(1, levels):
                value = jnp.where(quad > m - 0.5, level[t, m], value)
            kq[t, n] = value

    def folded(x):
        left = mm(flip[...], x[:half]).astype(BF)
        return mm(jnp.concatenate([x[half:], left], axis=0), place[...])

    for c in range(coils):
        for h in range(2):
            sf[c, h] = folded(sens[c, h])
    for t in range(frames):
        for h in range(2):
            imf[t, h] = folded(image[t, h])
    for t in range(frames):
        for c in range(coils):
            dr, di = folded(data[t, c, 0]), folded(data[t, c, 1])
            sr, si = sf[c, 0], sf[c, 1]
            gr, gi = -(sr * dr + si * di), si * dr - sr * di
            if c:
                gr, gi = res[t, 0] + gr, res[t, 1] + gi
            res[t, 0] = gr
            res[t, 1] = gi

    def pair(q, carry):
        t, c = q // coils, q % coils
        for r in range(0, half, 16):
            parts = {}
            for a, row in (("R", r), ("L", half + r)):
                for b, col in (("R", 0), ("L", wide)):
                    sl = (pl.ds(row, 16), pl.ds(col, half))
                    sr, si = sf[c, 0, sl[0], sl[1]], sf[c, 1, sl[0], sl[1]]
                    ir, ii = imf[t, 0, sl[0], sl[1]], imf[t, 1, sl[0], sl[1]]
                    parts[a + b] = (sr * ir - si * ii, sr * ii + si * ir)
            for h in range(2):
                rr, rl, lr, ll = (parts[n][h] for n in ("RR", "RL", "LR", "LL"))
                re, ro, le, lo = rr + rl, rr - rl, lr + ll, lr - ll
                for k, (xc, xs) in enumerate(((re + le, ro + lo), (re - le, ro - lo))):
                    at = (2 * k + h) * half + r
                    hc, wc = split(xc)
                    hs, ws = split(xs)
                    lc[0, pl.ds(at, 16)] = hc
                    lc[1, pl.ds(at, 16)] = wc
                    ls[0, pl.ds(at, 16)] = hs
                    ls[1, pl.ds(at, 16)] = ws
        for n, (lref, tab) in enumerate(((lc, f1c), (ls, f1s))):
            first = mm(lref[0], tab[:, :slots]) + mm(lref[0], tab[:, slots:]) + mm(lref[1], tab[:, :slots])
            for k, dest in enumerate((ge, go)):
                for h in range(2):
                    part = first[(2 * k + h) * half:(2 * k + h + 1) * half]
                    high, low = split(part)
                    for j in range(chunks):
                        lanes = pl.ds((2 * n + h) * 128, 128)
                        dest[j, pl.ds(0, half), lanes] = high[:, j * 128:(j + 1) * 128]
                        dest[j, pl.ds(half, half), lanes] = low[:, j * 128:(j + 1) * 128]
                        dest[j, pl.ds(2 * half, half), lanes] = high[:, j * 128:(j + 1) * 128]
        for j in range(chunks):
            spa[j] = mm(f2c[...], ge[j])
            spb[j] = mm(f2s[...], go[j])
            for r in range(0, rows, 16):
                rs = pl.ds(r, 16)
                aar, aai, abr, abi = (spa[j, rs, pl.ds(128 * m, 128)] for m in range(4))
                bar, bai, bbr, bbi = (spb[j, rs, pl.ds(128 * m, 128)] for m in range(4))
                kpp, kpm, kmp, kmm = (kq[t, m, rs, pl.ds(128 * j, 128)] for m in range(4))
                ur, ui, vr, vi = aar - bbr, aai - bbi, aar + bbr, aai + bbi
                wr, wi, qr, qi = abr + bar, abi + bai, abr - bar, abi - bai
                ppr, ppi = kpp * (ur + wi), kpp * (ui - wr)
                mmr, mmi = kmm * (ur - wi), kmm * (ui + wr)
                pmr, pmi = kpm * (vr - qi), kpm * (vi + qr)
                mpr, mpi = kmp * (vr + qi), kmp * (vi - qr)
                s1r, s1i, s2r, s2i = ppr + mmr, ppi + mmi, pmr + mpr, pmi + mpi
                d1r, d1i, d2r, d2i = ppr - mmr, ppi - mmi, pmr - mpr, pmi - mpi
                for dest, vals in ((za, (s1r + s2r, s1i + s2i, d2i - d1i, d1r - d2r)), (zb, (-(d1i + d2i), d1r + d2r, s2r - s1r, s2i - s1i))):
                    for m, value in enumerate(vals):
                        high, low = split(value)
                        lanes = pl.ds(128 * m, 128)
                        dest[j, pl.ds(r, 16), lanes] = high
                        dest[j, pl.ds(rows + r, 16), lanes] = low
                        dest[j, pl.ds(2 * rows + r, 16), lanes] = high
            for n, (tab, src) in enumerate(((i1c, za), (i1s, zb))):
                high, low = split(mm(tab[...], src[j]))
                for m in range(4):
                    dest = lhc if m < 2 else lhs
                    rs = pl.ds((2 * n + m % 2) * half, half)
                    for place_at, value in enumerate((high, low, high)):
                        dest[rs, pl.ds(j * 384 + place_at * 128, 128)] = value[:, 128 * m:128 * (m + 1)]
        oc[...] = mm(lhc[...], i2c[...])
        osn[...] = mm(lhs[...], i2s[...])
        for r in range(0, half, 16):
            quad = {}
            for h in range(2):
                ee, oe = oc[pl.ds(h * half + r, 16)], oc[pl.ds((2 + h) * half + r, 16)]
                eo, oo = osn[pl.ds(h * half + r, 16)], osn[pl.ds((2 + h) * half + r, 16)]
                quad["RR", h] = (ee + oe) + (eo + oo)
                quad["RL", h] = (ee + oe) - (eo + oo)
                quad["LR", h] = (ee - oe) + (eo - oo)
                quad["LL", h] = (ee - oe) - (eo - oo)
            for a, row in (("R", r), ("L", half + r)):
                for b, col in (("R", 0), ("L", wide)):
                    sl = (pl.ds(row, 16), pl.ds(col, half))
                    sr, si = sf[c, 0, sl[0], sl[1]], sf[c, 1, sl[0], sl[1]]
                    yr, yi = quad[a + b, 0], quad[a + b, 1]
                    res[t, 0, sl[0], sl[1]] += sr * yr + si * yi
                    res[t, 1, sl[0], sl[1]] += sr * yi - si * yr
        return carry

    lax.fori_loop(0, frames * coils, pair, 0)

    for t in range(frames):
        for h in range(2):
            high, low = split(res[t, h])
            cols = mm(high, unplace[...]) + mm(low, unplace[...])
            out[t, h, pl.ds(half, half)] = cols[:half]
            high, low = split(cols[half:])
            out[t, h, pl.ds(0, half)] = mm(flip[...], high) + mm(flip[...], low)


def partial_residual(images, sensitivity, coil_data, kernel_index, kernel_level):
    frames, _, size, _ = images.shape
    tables = make_tables(size)
    half = size // 2
    wide = tables["place"].shape[1] // 2
    rows = tables["f2c"].shape[0]
    slots = tables["mirror"].shape[1]
    chunks = slots // 128
    coils = sensitivity.shape[0]
    level = kernel_level / (4.0 * size * size)
    vm = pl.BlockSpec(memory_space=pltpu.VMEM)
    return pl.pallas_call(
        normal_kernel,
        out_shape=jax.ShapeDtypeStruct((frames, 2, size, size), F32),
        in_specs=[pl.BlockSpec(memory_space=pltpu.SMEM)] + [vm] * (4 + len(TABLES)),
        out_specs=vm,
        scratch_shapes=[
            pltpu.VMEM((frames, 4, rows, slots), F32),
            pltpu.VMEM((coils, 2, size, 2 * wide), F32),
            pltpu.VMEM((frames, 2, size, 2 * wide), F32),
            pltpu.VMEM((frames, 2, size, 2 * wide), F32),
            pltpu.VMEM((2, 4 * half, half), BF),
            pltpu.VMEM((2, 4 * half, half), BF),
            pltpu.VMEM((chunks, 3 * half, 512), BF),
            pltpu.VMEM((chunks, 3 * half, 512), BF),
            pltpu.VMEM((chunks, rows, 512), F32),
            pltpu.VMEM((chunks, rows, 512), F32),
            pltpu.VMEM((chunks, 3 * rows, 512), BF),
            pltpu.VMEM((chunks, 3 * rows, 512), BF),
            pltpu.VMEM((4 * half, 3 * slots), BF),
            pltpu.VMEM((4 * half, 3 * slots), BF),
            pltpu.VMEM((4 * half, half), F32),
            pltpu.VMEM((4 * half, half), F32),
        ],
        compiler_params=pltpu.CompilerParams(vmem_limit_bytes=60 * 2**20),
    )(level, images, sensitivity, coil_data, kernel_index, *[jnp.asarray(tables[n]) for n in TABLES])


def build_images(factors, temporal):
    mixed = jnp.einsum(
        "tr,rcxy->tcxy",
        temporal,
        lax.all_gather(factors, "frame", axis=3, tiled=True),
        precision=lax.Precision.HIGHEST,
    )
    row_images = mixed.astype(jnp.bfloat16)
    return lax.all_gather(row_images, "coil", axis=2, tiled=True)


def body(spatial, temporal, sensitivity, coil_data, kernel_index, kernel_level):
    full_images = build_images(spatial, temporal)
    partial_value = partial_residual(full_images, sensitivity, coil_data, kernel_index, kernel_level)
    rows_residual = lax.psum_scatter(partial_value, "coil", scatter_dimension=2, tiled=True)
    local_grad = jnp.einsum(
        "tr,tcxy->rcxy", temporal, rows_residual, precision=lax.Precision.HIGHEST
    )
    gradient = lax.psum_scatter(local_grad, "frame", scatter_dimension=3, tiled=True)
    spatial_next = spatial - STEP_SIZE * gradient
    images = build_images(spatial_next, temporal)
    return (spatial_next, images)


def solution(mesh):
    placed = (
        P(None, None, "coil", "frame"),
        P("frame", None),
        P("coil", None, None, None),
        P("frame", "coil", None, None, None),
        P("frame", None, None),
        P("frame", None),
    )
    return jax.shard_map(
        body,
        mesh=mesh,
        in_specs=placed,
        out_specs=(P(None, None, "coil", "frame"), P("frame", None, None, None)),
        check_vma=False,
    )
```

```python
import functools
import math

import jax
import jax.numpy as jnp
import ml_dtypes
import numpy as np
from jax import lax
from jax.experimental import pallas as pl
from jax.experimental.pallas import tpu as pltpu
from jax.sharding import PartitionSpec as P

STEP_SIZE = 0.15
BF = jnp.bfloat16
F32 = jnp.float32


def halves(table):
    high = table.astype(ml_dtypes.bfloat16)
    low = (table - high.astype(np.float64)).astype(ml_dtypes.bfloat16)
    return high, low


def make_tables(size):
    half = size // 2
    slots = -(-(size + 1) // 128) * 128
    rows = -(-(size + 1) // 16) * 16
    p = np.arange(half) + 0.5
    k = np.arange(slots)
    valid = (k <= size).astype(np.float64)
    angle = np.pi / size * np.outer(p, k)
    cos, sin = np.cos(angle) * valid, np.sin(angle) * valid
    cos[:, size] = 0.0
    sin[:, 0] = 0.0
    weight = np.where((k == 0) | (k == size), 0.5, 1.0)
    out = {}
    for name, tab in (("c", cos), ("s", sin)):
        hi, lo = halves(tab)
        out["f1" + name] = np.concatenate([hi, lo], axis=1)
        rhi, rlo = hi[:, :rows].T, lo[:, :rows].T
        out["f2" + name] = np.concatenate([rhi, rhi, rlo], axis=1)
        whi, wlo = halves(tab * weight)
        out["i1" + name] = np.concatenate([whi[:, :rows], whi[:, :rows], wlo[:, :rows]], axis=1)
        parts = []
        for j in range(0, slots, 128):
            parts += [whi.T[j:j + 128], whi.T[j:j + 128], wlo.T[j:j + 128]]
        out["i2" + name] = np.concatenate(parts, axis=0)
    wide = -(-half // 128) * 128
    place = np.zeros((size, 2 * wide))
    q = np.arange(half)
    place[half + q, q] = 1
    place[half - 1 - q, wide + q] = 1
    out["place"] = place.astype(ml_dtypes.bfloat16)
    out["unplace"] = place.T.astype(ml_dtypes.bfloat16)
    out["flip"] = np.eye(half)[::-1].astype(ml_dtypes.bfloat16)
    mirror = np.zeros((2 * size, slots))
    kk = np.arange(size + 1)
    mirror[(2 * size - kk) % (2 * size), kk] = 1
    out["mirror"] = mirror.astype(ml_dtypes.bfloat16)
    out["mirror_rows"] = mirror.T[:rows].astype(ml_dtypes.bfloat16)
    return out


TABLES = ("f1c", "f1s", "f2c", "f2s", "i1c", "i1s", "i2c", "i2s", "place", "unplace", "flip", "mirror", "mirror_rows")


def mm(a, b):
    return jnp.dot(a, b, preferred_element_type=F32)


def split(x):
    high = x.astype(BF)
    low = (x - high.astype(F32)).astype(BF)
    return high, low


def normal_kernel(level, image, sens, data, index, f1c, f1s, f2c, f2s, i1c, i1s, i2c, i2s, place, unplace, flip, mirror, mirror_rows, out, kq, sf, imf, res, lc, ls, ge, go, spa, spb, za, zb, lhc, lhs, oc, osn):
    frames, coils = image.shape[0], sens.shape[0]
    size = image.shape[2]
    half = size // 2
    wide = place.shape[1] // 2
    rows = f2c.shape[0]
    slots = mirror.shape[1]
    chunks = slots // 128
    levels = level.shape[1]

    for t in range(frames):
        ib = index[t].astype(F32).astype(BF)
        flipped = mm(ib, mirror[...]).astype(BF)
        low = mm(mirror_rows[...], jnp.concatenate([ib[:, :slots], flipped], axis=1))
        quads = (ib[:rows, :slots].astype(F32), flipped[:rows].astype(F32), low[:, :slots], low[:, slots:])
        for n, quad in enumerate(quads):
            value = jnp.full(quad.shape, level[t, 0], F32)
            for m in range(1, levels):
                value = jnp.where(quad > m - 0.5, level[t, m], value)
            kq[t, n] = value

    def folded(x):
        left = mm(flip[...], x[:half]).astype(BF)
        return mm(jnp.concatenate([x[half:], left], axis=0), place[...])

    for c in range(coils):
        for h in range(2):
            sf[c, h] = folded(sens[c, h])
    for t in range(frames):
        for h in range(2):
            imf[t, h] = folded(image[t, h])
    for t in range(frames):
        for c in range(coils):
            dr, di = folded(data[t, c, 0]), folded(data[t, c, 1])
            sr, si = sf[c, 0], sf[c, 1]
            gr, gi = -(sr * dr + si * di), si * dr - sr * di
            if c:
                gr, gi = res[t, 0] + gr, res[t, 1] + gi
            res[t, 0] = gr
            res[t, 1] = gi

    def pair(q, carry):
        t, c = q // coils, q % coils
        for r in range(0, half, 16):
            parts = {}
            for a, row in (("R", r), ("L", half + r)):
                for b, col in (("R", 0), ("L", wide)):
                    sl = (pl.ds(row, 16), pl.ds(col, half))
                    sr, si = sf[c, 0, sl[0], sl[1]], sf[c, 1, sl[0], sl[1]]
                    ir, ii = imf[t, 0, sl[0], sl[1]], imf[t, 1, sl[0], sl[1]]
                    parts[a + b] = (sr * ir - si * ii, sr * ii + si * ir)
            for h in range(2):
                rr, rl, lr, ll = (parts[n][h] for n in ("RR", "RL", "LR", "LL"))
                re, ro, le, lo = rr + rl, rr - rl, lr + ll, lr - ll
                for k, (xc, xs) in enumerate(((re + le, ro + lo), (re - le, ro - lo))):
                    at = (2 * k + h) * half + r
                    hc, wc = split(xc)
                    hs, ws = split(xs)
                    lc[0, pl.ds(at, 16)] = hc
                    lc[1, pl.ds(at, 16)] = wc
                    ls[0, pl.ds(at, 16)] = hs
                    ls[1, pl.ds(at, 16)] = ws
        for n, (lref, tab) in enumerate(((lc, f1c), (ls, f1s))):
            first = mm(lref[0], tab[:, :slots]) + mm(lref[0], tab[:, slots:]) + mm(lref[1], tab[:, :slots])
            for k, dest in enumerate((ge, go)):
                for h in range(2):
                    part = first[(2 * k + h) * half:(2 * k + h + 1) * half]
                    high, low = split(part)
                    for j in range(chunks):
                        lanes = pl.ds((2 * n + h) * 128, 128)
                        dest[j, pl.ds(0, half), lanes] = high[:, j * 128:(j + 1) * 128]
                        dest[j, pl.ds(half, half), lanes] = low[:, j * 128:(j + 1) * 128]
                        dest[j, pl.ds(2 * half, half), lanes] = high[:, j * 128:(j + 1) * 128]
        for j in range(chunks):
            spa[j] = mm(f2c[...], ge[j])
            spb[j] = mm(f2s[...], go[j])
            for r in range(0, rows, 16):
                rs = pl.ds(r, 16)
                aar, aai, abr, abi = (spa[j, rs, pl.ds(128 * m, 128)] for m in range(4))
                bar, bai, bbr, bbi = (spb[j, rs, pl.ds(128 * m, 128)] for m in range(4))
                kpp, kpm, kmp, kmm = (kq[t, m, rs, pl.ds(128 * j, 128)] for m in range(4))
                ur, ui, vr, vi = aar - bbr, aai - bbi, aar + bbr, aai + bbi
                wr, wi, qr, qi = abr + bar, abi + bai, abr - bar, abi - bai
                ppr, ppi = kpp * (ur + wi), kpp * (ui - wr)
                mmr, mmi = kmm * (ur - wi), kmm * (ui + wr)
                pmr, pmi = kpm * (vr - qi), kpm * (vi + qr)
                mpr, mpi = kmp * (vr + qi), kmp * (vi - qr)
                s1r, s1i, s2r, s2i = ppr + mmr, ppi + mmi, pmr + mpr, pmi + mpi
                d1r, d1i, d2r, d2i = ppr - mmr, ppi - mmi, pmr - mpr, pmi - mpi
                for dest, vals in ((za, (s1r + s2r, s1i + s2i, d2i - d1i, d1r - d2r)), (zb, (-(d1i + d2i), d1r + d2r, s2r - s1r, s2i - s1i))):
                    for m, value in enumerate(vals):
                        high, low = split(value)
                        lanes = pl.ds(128 * m, 128)
                        dest[j, pl.ds(r, 16), lanes] = high
                        dest[j, pl.ds(rows + r, 16), lanes] = low
                        dest[j, pl.ds(2 * rows + r, 16), lanes] = high
            for n, (tab, src) in enumerate(((i1c, za), (i1s, zb))):
                high, low = split(mm(tab[...], src[j]))
                for m in range(4):
                    dest = lhc if m < 2 else lhs
                    rs = pl.ds((2 * n + m % 2) * half, half)
                    for place_at, value in enumerate((high, low, high)):
                        dest[rs, pl.ds(j * 384 + place_at * 128, 128)] = value[:, 128 * m:128 * (m + 1)]
        oc[...] = mm(lhc[...], i2c[...])
        osn[...] = mm(lhs[...], i2s[...])
        for r in range(0, half, 16):
            quad = {}
            for h in range(2):
                ee, oe = oc[pl.ds(h * half + r, 16)], oc[pl.ds((2 + h) * half + r, 16)]
                eo, oo = osn[pl.ds(h * half + r, 16)], osn[pl.ds((2 + h) * half + r, 16)]
                quad["RR", h] = (ee + oe) + (eo + oo)
                quad["RL", h] = (ee + oe) - (eo + oo)
                quad["LR", h] = (ee - oe) + (eo - oo)
                quad["LL", h] = (ee - oe) - (eo - oo)
            for a, row in (("R", r), ("L", half + r)):
                for b, col in (("R", 0), ("L", wide)):
                    sl = (pl.ds(row, 16), pl.ds(col, half))
                    sr, si = sf[c, 0, sl[0], sl[1]], sf[c, 1, sl[0], sl[1]]
                    yr, yi = quad[a + b, 0], quad[a + b, 1]
                    res[t, 0, sl[0], sl[1]] += sr * yr + si * yi
                    res[t, 1, sl[0], sl[1]] += sr * yi - si * yr
        return carry

    lax.fori_loop(0, frames * coils, pair, 0)

    for t in range(frames):
        for h in range(2):
            high, low = split(res[t, h])
            cols = mm(high, unplace[...]) + mm(low, unplace[...])
            out[t, h, pl.ds(half, half)] = cols[:half]
            high, low = split(cols[half:])
            out[t, h, pl.ds(0, half)] = mm(flip[...], high) + mm(flip[...], low)


def partial_residual(images, sensitivity, coil_data, kernel_index, kernel_level):
    frames, _, size, _ = images.shape
    tables = make_tables(size)
    half = size // 2
    wide = tables["place"].shape[1] // 2
    rows = tables["f2c"].shape[0]
    slots = tables["mirror"].shape[1]
    chunks = slots // 128
    coils = sensitivity.shape[0]
    level = kernel_level / (4.0 * size * size)
    vm = pl.BlockSpec(memory_space=pltpu.VMEM)
    return pl.pallas_call(
        normal_kernel,
        out_shape=jax.ShapeDtypeStruct((frames, 2, size, size), F32),
        in_specs=[pl.BlockSpec(memory_space=pltpu.SMEM)] + [vm] * (4 + len(TABLES)),
        out_specs=vm,
        scratch_shapes=[
            pltpu.VMEM((frames, 4, rows, slots), F32),
            pltpu.VMEM((coils, 2, size, 2 * wide), F32),
            pltpu.VMEM((frames, 2, size, 2 * wide), F32),
            pltpu.VMEM((frames, 2, size, 2 * wide), F32),
            pltpu.VMEM((2, 4 * half, half), BF),
            pltpu.VMEM((2, 4 * half, half), BF),
            pltpu.VMEM((chunks, 3 * half, 512), BF),
            pltpu.VMEM((chunks, 3 * half, 512), BF),
            pltpu.VMEM((chunks, rows, 512), F32),
            pltpu.VMEM((chunks, rows, 512), F32),
            pltpu.VMEM((chunks, 3 * rows, 512), BF),
            pltpu.VMEM((chunks, 3 * rows, 512), BF),
            pltpu.VMEM((4 * half, 3 * slots), BF),
            pltpu.VMEM((4 * half, 3 * slots), BF),
            pltpu.VMEM((4 * half, half), F32),
            pltpu.VMEM((4 * half, half), F32),
        ],
        compiler_params=pltpu.CompilerParams(vmem_limit_bytes=60 * 2**20),
    )(level, images, sensitivity, coil_data, kernel_index, *[jnp.asarray(tables[n]) for n in TABLES])


def plane_shape(sp):
    rank, _, rows, cols = sp.shape
    return rank, rows, rows // 16, cols


def lane_masks(cols, groups):
    lane = lax.broadcasted_iota(jnp.int32, (16, 128), 1)
    return lane


def moves(block, cols, group):
    off, start = group * cols, block * cols
    tile, at = start // 128, start % 128
    first = min(cols, 128 - at)
    out = [(tile, at, off, first)]
    if first < cols:
        out.append((tile + 1, 0, off + first, cols - first))
    return out


def roll(x, shift):
    shift = shift % 128
    return pltpu.roll(x, shift, 1) if shift else x


def enter(peers):
    barrier = pltpu.get_barrier_semaphore()
    frame, coil = lax.axis_index("frame"), lax.axis_index("coil")
    nf, nc = lax.axis_size("frame"), lax.axis_size("coil")

    def greet(i, carry):
        pl.semaphore_signal(barrier, inc=1, device_id={"frame": lax.rem(frame + i, nf)}, device_id_type=pl.DeviceIdType.MESH)
        return carry

    lax.fori_loop(1, nf, greet, 0)
    for step in (1, nc - 1):
        pl.semaphore_signal(barrier, inc=1, device_id={"coil": lax.rem(coil + step, nc)}, device_id_type=pl.DeviceIdType.MESH)
    pl.semaphore_wait(barrier, nf + 1)


def remote(src, dst, send, recv, where):
    return pltpu.make_async_remote_copy(src_ref=src, dst_ref=dst, send_sem=send, recv_sem=recv, device_id=where, device_id_type=pl.DeviceIdType.MESH)


def wait_bytes(ref, sem):
    pltpu.make_async_copy(ref, ref, sem).wait()


def mix_and_send(weights, factors, send_buf, recv_buf, send_sem, recv_sem):
    frame, nf = lax.axis_index("frame"), lax.axis_size("frame")
    rank = factors.shape[0]

    def piece(d, t):
        total = weights[d, t, pl.ds(0, 1)] * factors[0]
        for r in range(1, rank):
            total += weights[d, t, pl.ds(r, 1)] * factors[r]
        return total.astype(BF)

    def step(i, carry):
        d = lax.rem(frame + i, nf)
        for t in range(2):
            send_buf[d, t] = piece(d, t)
        remote(send_buf.at[d], recv_buf.at[frame], send_sem, recv_sem, {"frame": d}).start()
        return carry

    lax.fori_loop(1, nf, step, 0)
    for t in range(2):
        recv_buf[frame, t] = piece(frame, t)


def place_rows(recv_buf, image, t, cols):
    coil, nf = lax.axis_index("coil"), lax.axis_size("frame")
    size = image.shape[2]
    rows = size // lax.axis_size("coil")
    lane = lax.broadcasted_iota(jnp.int32, (16, 128), 1)
    blocks = rows // 16
    for c in range(2):
        for rb in range(blocks):
            tiles = [jnp.zeros((16, 128), F32) for _ in range(-(-size // 128))]
            for f in range(nf):
                value = recv_buf[f, t].astype(F32)
                for tile, at, off, count in moves(f, cols, c * blocks + rb):
                    inside = (lane >= at) & (lane < at + count)
                    tiles[tile] = jnp.where(inside, roll(value, at - off), tiles[tile])
            at_row = pl.multiple_of(coil * rows + rb * 16, 16)
            for n, value in enumerate(tiles):
                width = min(128, size - 128 * n)
                image[t, c, pl.ds(at_row, 16), pl.ds(128 * n, width)] = value.astype(BF)[:, :width]


def spread_rows(image, t, sems):
    send, recv, _, _ = sems
    coil, nc = lax.axis_index("coil"), lax.axis_size("coil")
    rows = image.shape[2] // nc
    mine = pl.ds(pl.multiple_of(coil * rows, 16), rows)
    for way, step in ((0, 1), (1, nc - 1)):
        for c in (way, 1 - way):
            part = image.at[t, c, mine]
            remote(part, part, send.at[t, way, c], recv.at[t, way, c], {"coil": lax.rem(coil + step, nc)}).start()


def forward_rows(image, t, sems):
    send, recv, send2, recv2 = sems
    coil, nc = lax.axis_index("coil"), lax.axis_size("coil")
    rows = image.shape[2] // nc
    for way, step in ((0, 1), (1, nc - 1)):
        source = lax.rem(coil + nc - step, nc)
        part = image.at[t, way, pl.ds(pl.multiple_of(source * rows, 16), rows)]
        wait_bytes(part, recv.at[t, way, way])
        remote(part, part, send2.at[t, way], recv2.at[t, way], {"coil": lax.rem(coil + step, nc)}).start()


def finish_rows(image, t, sems):
    send, recv, send2, recv2 = sems
    coil, nc = lax.axis_index("coil"), lax.axis_size("coil")
    rows = image.shape[2] // nc
    part = image.at[t, 0, pl.ds(0, rows)]
    for way in range(2):
        wait_bytes(part, recv.at[t, way, 1 - way])
        wait_bytes(part, recv2.at[t, way])
        wait_bytes(part, send2.at[t, way])
        for c in range(2):
            wait_bytes(part, send.at[t, way, c])


def share_images(weights, factors, send_buf, recv_buf, image, cols, a2a, rows_sems, between=None):
    nf = lax.axis_size("frame")
    mix_and_send(weights, factors, send_buf, recv_buf, a2a.at[0], a2a.at[1])
    if between is not None:
        between()
    wait_bytes(recv_buf.at[pl.ds(0, nf - 1)], a2a.at[1])
    for t in range(2):
        place_rows(recv_buf, image, t, cols)
        spread_rows(image, t, rows_sems)
    for t in range(2):
        forward_rows(image, t, rows_sems)
    for t in range(2):
        finish_rows(image, t, rows_sems)
    wait_bytes(recv_buf.at[pl.ds(0, nf - 1)], a2a.at[0])


def pack_factors(spatial, factors):
    rank, _, rows, _ = spatial.shape
    cols = 10
    lane = lax.broadcasted_iota(jnp.int32, (16, 128), 1)
    blocks = rows // 16

    def one(r, carry):
        total = jnp.zeros((16, 128), F32)
        for c in range(2):
            for rb in range(blocks):
                off = (c * blocks + rb) * cols
                inside = (lane >= off) & (lane < off + cols)
                total = jnp.where(inside, roll(spatial[r, c, pl.ds(16 * rb, 16)], off), total)
        factors[r] = total
        return carry

    lax.fori_loop(0, rank, one, 0)


def first_kernel(weight, spatial, image, weights, factors, send_buf, recv_buf, wsem, a2a, rs0, rs1, rs2, rs3):
    frame, nf = lax.axis_index("frame"), lax.axis_size("frame")
    enter(None)

    def step(i, carry):
        remote(weight, weights.at[frame], wsem.at[0], wsem.at[1], {"frame": lax.rem(frame + i, nf)}).start()
        return carry

    lax.fori_loop(1, nf, step, 0)
    weights[frame] = weight[...]
    pack_factors(spatial, factors)
    wait_bytes(weights.at[pl.ds(0, nf - 1)], wsem.at[1])
    share_images(weights, factors, send_buf, recv_buf, image, 10, a2a, (rs0, rs1, rs2, rs3))
    wait_bytes(weights.at[pl.ds(0, nf - 1)], wsem.at[0])


def row_sems():
    return [
        pltpu.SemaphoreType.DMA((2, 2, 2)),
        pltpu.SemaphoreType.DMA((2, 2, 2)),
        pltpu.SemaphoreType.DMA((2, 2)),
        pltpu.SemaphoreType.DMA((2, 2)),
    ]


def first_images(spatial, weight, size):
    nf = lax.axis_size("frame")
    rank = spatial.shape[0]
    vm = pl.BlockSpec(memory_space=pltpu.VMEM)
    return pl.pallas_call(
        first_kernel,
        out_shape=(jax.ShapeDtypeStruct((2, 2, size, size), BF), jax.ShapeDtypeStruct((nf, 2, rank, 128), F32)),
        in_specs=[vm, vm],
        out_specs=(vm, vm),
        scratch_shapes=[
            pltpu.VMEM((rank, 16, 128), F32),
            pltpu.VMEM((nf, 2, 16, 128), BF),
            pltpu.VMEM((nf, 2, 16, 128), BF),
            pltpu.SemaphoreType.DMA((2,)),
            pltpu.SemaphoreType.DMA((2,)),
        ] + row_sems(),
        compiler_params=pltpu.CompilerParams(vmem_limit_bytes=40 * 2**20, collective_id=0, has_side_effects=True),
    )(weight, spatial)


def reduce_start(part, t, xa, xd, sems):
    s1, r1, s2, r2, s3, r3 = sems
    coil, nc = lax.axis_index("coil"), lax.axis_size("coil")
    rows = part.shape[2] // nc
    far = pl.ds(pl.multiple_of(lax.rem(coil + 2, nc) * rows, 16), rows)
    for way, step in ((0, 1), (1, nc - 1)):
        to = lax.rem(coil + step, nc)
        near = pl.ds(pl.multiple_of(to * rows, 16), rows)
        remote(part.at[t, way, far], xa.at[t, way], s1.at[t, way], r1.at[t, way], {"coil": to}).start()
        remote(part.at[t, 1 - way, near], xd.at[t, way], s2.at[t, way], r2.at[t, way], {"coil": to}).start()


def reduce_forward(part, t, xa, xsum, xs, sems):
    s1, r1, s2, r2, s3, r3 = sems
    coil, nc = lax.axis_index("coil"), lax.axis_size("coil")
    rows = part.shape[2] // nc
    for way, step in ((0, 1), (1, nc - 1)):
        to = lax.rem(coil + step, nc)
        near = pl.ds(pl.multiple_of(to * rows, 16), rows)
        wait_bytes(xa.at[t, way], r1.at[t, way])
        xsum[t, way] = xa[t, way] + part[t, way, near]
        remote(xsum.at[t, way], xs.at[t, way], s3.at[t, way], r3.at[t, way], {"coil": to}).start()


def reduce_finish(part, t, xd, xs, total, sems):
    s1, r1, s2, r2, s3, r3 = sems
    coil, nc = lax.axis_index("coil"), lax.axis_size("coil")
    size = part.shape[3]
    rows = part.shape[2] // nc
    mine = pl.ds(pl.multiple_of(coil * rows, 16), rows)
    for way in range(2):
        wait_bytes(xs.at[t, way], r3.at[t, way])
        wait_bytes(xd.at[t, 1 - way], r2.at[t, 1 - way])
        total[t, way, :, pl.ds(0, size)] = part[t, way, mine] + xs[t, way] + xd[t, 1 - way]


def send_columns(total, t, send_buf, recv_buf, sems, cols):
    frame, nf = lax.axis_index("frame"), lax.axis_size("frame")
    rows = total.shape[2]
    blocks = rows // 16
    lane = lax.broadcasted_iota(jnp.int32, (16, 128), 1)
    for f in range(nf):
        value = jnp.zeros((16, 128), F32)
        for c in range(2):
            for rb in range(blocks):
                for tile, at, off, count in moves(f, cols, c * blocks + rb):
                    inside = (lane >= off) & (lane < off + count)
                    value = jnp.where(inside, roll(total[t, c, pl.ds(16 * rb, 16), pl.ds(128 * tile, 128)], off - at), value)
        send_buf[t, f] = value

    def step(i, carry):
        d = lax.rem(frame + i, nf)
        remote(send_buf.at[t, d], recv_buf.at[t, frame], sems.at[0, t], sems.at[1, t], {"frame": d}).start()
        return carry

    lax.fori_loop(1, nf, step, 0)
    recv_buf[t, frame] = send_buf[t, frame]


def gradient_step(weights, recv_buf, t, grad):
    nf = lax.axis_size("frame")
    rank = grad.shape[0]

    def step(f, acc):
        value = recv_buf[t, f]
        return tuple(acc[r] + weights[f, t, pl.ds(r, 1)] * value for r in range(rank))

    acc = lax.fori_loop(0, nf, step, tuple(jnp.zeros((16, 128), F32) for _ in range(rank)))
    for r in range(rank):
        grad[r] = acc[r] if t == 0 else grad[r] + acc[r]


def unpack_factors(factors, spatial):
    rank, _, rows, cols = spatial.shape
    blocks = rows // 16

    def one(r, carry):
        value = factors[r]
        for c in range(2):
            for rb in range(blocks):
                spatial[r, c, pl.ds(16 * rb, 16)] = roll(value, -(c * blocks + rb) * cols)[:, :cols]
        return carry

    lax.fori_loop(0, rank, one, 0)


def last_kernel(part, weights, spatial, spatial_next, image, factors, grad, xa, xd, xsum, xs, total, rsend, rrecv, send_buf, recv_buf, a2a, rsem, s1, r1, s2, r2, s3, r3, rs0, rs1, rs2, rs3):
    frame, nf = lax.axis_index("frame"), lax.axis_size("frame")
    cols = spatial_next.shape[3]
    sems = (s1, r1, s2, r2, s3, r3)
    enter(None)
    for t in range(2):
        reduce_start(part, t, xa, xd, sems)
    pack_factors(spatial, factors)
    for t in range(2):
        reduce_forward(part, t, xa, xsum, xs, sems)
    for t in range(2):
        reduce_finish(part, t, xd, xs, total, sems)
        send_columns(total, t, rsend, rrecv, rsem, cols)
    for t in range(2):
        wait_bytes(rrecv.at[t, pl.ds(0, nf - 1)], rsem.at[1, t])
        gradient_step(weights, rrecv, t, grad)
    for r in range(factors.shape[0]):
        factors[r] = factors[r] - STEP_SIZE * grad[r]
    share_images(weights, factors, send_buf, recv_buf, image, cols, a2a, (rs0, rs1, rs2, rs3), lambda: unpack_factors(factors, spatial_next))
    for t in range(2):
        wait_bytes(rrecv.at[t, pl.ds(0, nf - 1)], rsem.at[0, t])
        for way in range(2):
            for sem in (s1, s2, s3):
                wait_bytes(xa.at[t, way], sem.at[t, way])


def update(part, weights, padded, spatial):
    nf = lax.axis_size("frame")
    size = part.shape[2]
    rank, _, rows, cols = spatial.shape
    vm = pl.BlockSpec(memory_space=pltpu.VMEM)
    block = pltpu.VMEM((2, 2, rows, size), F32)
    return pl.pallas_call(
        last_kernel,
        out_shape=(jax.ShapeDtypeStruct(spatial.shape, F32), jax.ShapeDtypeStruct((2, 2, size, size), BF)),
        in_specs=[vm, vm, vm],
        out_specs=(vm, vm),
        scratch_shapes=[
            pltpu.VMEM((rank, 16, 128), F32),
            pltpu.VMEM((rank, 16, 128), F32),
            block, block, block, block,
            pltpu.VMEM((2, 2, rows, -(-size // 128) * 128), F32),
            pltpu.VMEM((2, nf, 16, 128), F32),
            pltpu.VMEM((2, nf, 16, 128), F32),
            pltpu.VMEM((nf, 2, 16, 128), BF),
            pltpu.VMEM((nf, 2, 16, 128), BF),
            pltpu.SemaphoreType.DMA((2,)),
            pltpu.SemaphoreType.DMA((2, 2)),
        ] + [pltpu.SemaphoreType.DMA((2, 2))] * 6 + row_sems(),
        compiler_params=pltpu.CompilerParams(vmem_limit_bytes=40 * 2**20, collective_id=1, has_side_effects=True),
    )(part, weights, padded)


def body(spatial, temporal, sensitivity, coil_data, kernel_index, kernel_level):
    size = sensitivity.shape[2]
    cols = spatial.shape[3]
    padded = jnp.pad(spatial, ((0, 0), (0, 0), (0, 0), (0, 128 - cols)))
    weight = jnp.broadcast_to(temporal[:, :, None], temporal.shape + (128,))
    full_images, weights = first_images(padded, weight, size)
    partial_value = partial_residual(full_images, sensitivity, coil_data, kernel_index, kernel_level)
    return update(partial_value, weights, padded, spatial)


def solution(mesh):
    placed = (
        P(None, None, "coil", "frame"),
        P("frame", None),
        P("coil", None, None, None),
        P("frame", "coil", None, None, None),
        P("frame", None, None),
        P("frame", None),
    )
    return jax.shard_map(
        body,
        mesh=mesh,
        in_specs=placed,
        out_specs=(P(None, None, "coil", "frame"), P("frame", None, None, None)),
        check_vma=False,
    )
```

```python
import types

import jax
import jax.numpy as jnp
import ml_dtypes
import numpy as np
from jax import lax
from jax.experimental import pallas as pl
from jax.experimental.pallas import tpu as pltpu
from jax.sharding import PartitionSpec as P

STEP_SIZE = 0.15
BF = jnp.bfloat16
F32 = jnp.float32


def halves(table):
    high = table.astype(ml_dtypes.bfloat16)
    low = (table - high.astype(np.float64)).astype(ml_dtypes.bfloat16)
    return high, low


def make_tables(size):
    half = size // 2
    slots = -(-(size + 1) // 128) * 128
    rows = -(-(size + 1) // 16) * 16
    p = np.arange(half) + 0.5
    k = np.arange(slots)
    valid = (k <= size).astype(np.float64)
    angle = np.pi / size * np.outer(p, k)
    cos, sin = np.cos(angle) * valid, np.sin(angle) * valid
    cos[:, size] = 0.0
    sin[:, 0] = 0.0
    weight = np.where((k == 0) | (k == size), 0.5, 1.0)
    out = {}
    for name, tab in (("c", cos), ("s", sin)):
        hi, lo = halves(tab)
        out["f1" + name] = np.concatenate([hi, lo], axis=1)
        rhi, rlo = hi[:, :rows].T, lo[:, :rows].T
        out["f2" + name] = np.concatenate([rhi, rhi, rlo], axis=1)
        whi, wlo = halves(tab * weight)
        out["i1" + name] = np.concatenate([whi[:, :rows], whi[:, :rows], wlo[:, :rows]], axis=1)
        parts = []
        for j in range(0, slots, 128):
            parts += [whi.T[j:j + 128], whi.T[j:j + 128], wlo.T[j:j + 128]]
        out["i2" + name] = np.concatenate(parts, axis=0)
    wide = -(-half // 128) * 128
    place = np.zeros((size, 2 * wide))
    q = np.arange(half)
    place[half + q, q] = 1
    place[half - 1 - q, wide + q] = 1
    out["place"] = place.astype(ml_dtypes.bfloat16)
    out["unplace"] = place.T.astype(ml_dtypes.bfloat16)
    out["flip"] = np.eye(half)[::-1].astype(ml_dtypes.bfloat16)
    mirror = np.zeros((2 * size, slots))
    kk = np.arange(size + 1)
    mirror[(2 * size - kk) % (2 * size), kk] = 1
    out["mirror"] = mirror.astype(ml_dtypes.bfloat16)
    out["mirror_rows"] = mirror.T[:rows].astype(ml_dtypes.bfloat16)
    return out


TABLES = ("f1c", "f1s", "f2c", "f2s", "i1c", "i1s", "i2c", "i2s", "place", "unplace", "flip", "mirror", "mirror_rows")


def mm(a, b):
    return jnp.dot(a, b, preferred_element_type=F32)


def split(x):
    high = x.astype(BF)
    low = (x - high.astype(F32)).astype(BF)
    return high, low


def kernel_quads(s, level, t):
    rows = s.f2c.shape[0]
    slots = s.mirror.shape[1]
    ib = s.index[t].astype(F32).astype(BF)
    flipped = mm(ib, s.mirror[...]).astype(BF)
    low = mm(s.mirror_rows[...], jnp.concatenate([ib[:, :slots], flipped], axis=1))
    quads = (ib[:rows, :slots].astype(F32), flipped[:rows].astype(F32), low[:, :slots], low[:, slots:])
    for n, quad in enumerate(quads):
        value = jnp.full(quad.shape, level[t, 0], F32)
        for m in range(1, level.shape[1]):
            value = jnp.where(quad > m - 0.5, level[t, m], value)
        s.kq[t, n] = value


def folded(s, x):
    half = s.flip.shape[0]
    left = mm(s.flip[...], x[:half]).astype(BF)
    return mm(jnp.concatenate([x[half:], left], axis=0), s.place[...])


def fold_data(s, t):
    for c in range(s.sens.shape[0]):
        dr, di = folded(s, s.data[t, c, 0]), folded(s, s.data[t, c, 1])
        sr, si = s.sf[c, 0], s.sf[c, 1]
        gr, gi = -(sr * dr + si * di), si * dr - sr * di
        if c:
            gr, gi = s.res[t, 0] + gr, s.res[t, 1] + gi
        s.res[t, 0] = gr
        s.res[t, 1] = gi


def unfold(s, t):
    half = s.flip.shape[0]
    for h in range(2):
        high, low = split(s.res[t, h])
        cols = mm(high, s.unplace[...]) + mm(low, s.unplace[...])
        s.part[t, h, pl.ds(half, half)] = cols[:half]
        high, low = split(cols[half:])
        s.part[t, h, pl.ds(0, half)] = mm(s.flip[...], high) + mm(s.flip[...], low)


def run_pair(s, t, c):
    half = s.flip.shape[0]
    wide = s.place.shape[1] // 2
    rows = s.f2c.shape[0]
    slots = s.mirror.shape[1]
    chunks = slots // 128
    for r in range(0, half, 16):
        parts = {}
        for a, row in (("R", r), ("L", half + r)):
            for b, col in (("R", 0), ("L", wide)):
                sl = (pl.ds(row, 16), pl.ds(col, half))
                sr, si = s.sf[c, 0, sl[0], sl[1]], s.sf[c, 1, sl[0], sl[1]]
                ir, ii = s.imf[t, 0, sl[0], sl[1]], s.imf[t, 1, sl[0], sl[1]]
                parts[a + b] = (sr * ir - si * ii, sr * ii + si * ir)
        for h in range(2):
            rr, rl, lr, ll = (parts[n][h] for n in ("RR", "RL", "LR", "LL"))
            re, ro, le, lo = rr + rl, rr - rl, lr + ll, lr - ll
            for k, (xc, xs) in enumerate(((re + le, ro + lo), (re - le, ro - lo))):
                at = (2 * k + h) * half + r
                hc, wc = split(xc)
                hs, ws = split(xs)
                s.lc[0, pl.ds(at, 16)] = hc
                s.lc[1, pl.ds(at, 16)] = wc
                s.ls[0, pl.ds(at, 16)] = hs
                s.ls[1, pl.ds(at, 16)] = ws
    for n, (lref, tab) in enumerate(((s.lc, s.f1c), (s.ls, s.f1s))):
        first = mm(lref[0], tab[:, :slots]) + mm(lref[0], tab[:, slots:]) + mm(lref[1], tab[:, :slots])
        for k, dest in enumerate((s.ge, s.go)):
            for h in range(2):
                part = first[(2 * k + h) * half:(2 * k + h + 1) * half]
                high, low = split(part)
                for j in range(chunks):
                    lanes = pl.ds((2 * n + h) * 128, 128)
                    dest[j, pl.ds(0, half), lanes] = high[:, j * 128:(j + 1) * 128]
                    dest[j, pl.ds(half, half), lanes] = low[:, j * 128:(j + 1) * 128]
                    dest[j, pl.ds(2 * half, half), lanes] = high[:, j * 128:(j + 1) * 128]
    for j in range(chunks):
        s.spa[j] = mm(s.f2c[...], s.ge[j])
        s.spb[j] = mm(s.f2s[...], s.go[j])
        for r in range(0, rows, 16):
            rs = pl.ds(r, 16)
            aar, aai, abr, abi = (s.spa[j, rs, pl.ds(128 * m, 128)] for m in range(4))
            bar, bai, bbr, bbi = (s.spb[j, rs, pl.ds(128 * m, 128)] for m in range(4))
            kpp, kpm, kmp, kmm = (s.kq[t, m, rs, pl.ds(128 * j, 128)] for m in range(4))
            ur, ui, vr, vi = aar - bbr, aai - bbi, aar + bbr, aai + bbi
            wr, wi, qr, qi = abr + bar, abi + bai, abr - bar, abi - bai
            ppr, ppi = kpp * (ur + wi), kpp * (ui - wr)
            mmr, mmi = kmm * (ur - wi), kmm * (ui + wr)
            pmr, pmi = kpm * (vr - qi), kpm * (vi + qr)
            mpr, mpi = kmp * (vr + qi), kmp * (vi - qr)
            s1r, s1i, s2r, s2i = ppr + mmr, ppi + mmi, pmr + mpr, pmi + mpi
            d1r, d1i, d2r, d2i = ppr - mmr, ppi - mmi, pmr - mpr, pmi - mpi
            for dest, vals in ((s.za, (s1r + s2r, s1i + s2i, d2i - d1i, d1r - d2r)), (s.zb, (-(d1i + d2i), d1r + d2r, s2r - s1r, s2i - s1i))):
                for m, value in enumerate(vals):
                    high, low = split(value)
                    lanes = pl.ds(128 * m, 128)
                    dest[j, pl.ds(r, 16), lanes] = high
                    dest[j, pl.ds(rows + r, 16), lanes] = low
                    dest[j, pl.ds(2 * rows + r, 16), lanes] = high
        for n, (tab, src) in enumerate(((s.i1c, s.za), (s.i1s, s.zb))):
            high, low = split(mm(tab[...], src[j]))
            for m in range(4):
                dest = s.lhc if m < 2 else s.lhs
                rs = pl.ds((2 * n + m % 2) * half, half)
                for place_at, value in enumerate((high, low, high)):
                    dest[rs, pl.ds(j * 384 + place_at * 128, 128)] = value[:, 128 * m:128 * (m + 1)]
    s.oc[...] = mm(s.lhc[...], s.i2c[...])
    s.osn[...] = mm(s.lhs[...], s.i2s[...])
    for r in range(0, half, 16):
        quad = {}
        for h in range(2):
            ee, oe = s.oc[pl.ds(h * half + r, 16)], s.oc[pl.ds((2 + h) * half + r, 16)]
            eo, oo = s.osn[pl.ds(h * half + r, 16)], s.osn[pl.ds((2 + h) * half + r, 16)]
            quad["RR", h] = (ee + oe) + (eo + oo)
            quad["RL", h] = (ee + oe) - (eo + oo)
            quad["LR", h] = (ee - oe) + (eo - oo)
            quad["LL", h] = (ee - oe) - (eo - oo)
        for a, row in (("R", r), ("L", half + r)):
            for b, col in (("R", 0), ("L", wide)):
                sl = (pl.ds(row, 16), pl.ds(col, half))
                sr, si = s.sf[c, 0, sl[0], sl[1]], s.sf[c, 1, sl[0], sl[1]]
                yr, yi = quad[a + b, 0], quad[a + b, 1]
                s.res[t, 0, sl[0], sl[1]] += sr * yr + si * yi
                s.res[t, 1, sl[0], sl[1]] += sr * yi - si * yr


def plane_shape(sp):
    rank, _, rows, cols = sp.shape
    return rank, rows, rows // 16, cols


def lane_masks(cols, groups):
    lane = lax.broadcasted_iota(jnp.int32, (16, 128), 1)
    return lane


def moves(block, cols, group):
    off, start = group * cols, block * cols
    tile, at = start // 128, start % 128
    first = min(cols, 128 - at)
    out = [(tile, at, off, first)]
    if first < cols:
        out.append((tile + 1, 0, off + first, cols - first))
    return out


def roll(x, shift):
    shift = shift % 128
    return pltpu.roll(x, shift, 1) if shift else x


def enter(peers):
    barrier = pltpu.get_barrier_semaphore()
    frame, coil = lax.axis_index("frame"), lax.axis_index("coil")
    nf, nc = lax.axis_size("frame"), lax.axis_size("coil")

    def greet(i, carry):
        pl.semaphore_signal(barrier, inc=1, device_id={"frame": lax.rem(frame + i, nf)}, device_id_type=pl.DeviceIdType.MESH)
        return carry

    lax.fori_loop(1, nf, greet, 0)
    for step in (1, nc - 1):
        pl.semaphore_signal(barrier, inc=1, device_id={"coil": lax.rem(coil + step, nc)}, device_id_type=pl.DeviceIdType.MESH)
    pl.semaphore_wait(barrier, nf + 1)


def remote(src, dst, send, recv, where):
    return pltpu.make_async_remote_copy(src_ref=src, dst_ref=dst, send_sem=send, recv_sem=recv, device_id=where, device_id_type=pl.DeviceIdType.MESH)


def wait_bytes(ref, sem):
    pltpu.make_async_copy(ref, ref, sem).wait()


def mix_and_send(weights, factors, send_buf, recv_buf, send_sem, recv_sem):
    frame, nf = lax.axis_index("frame"), lax.axis_size("frame")
    rank = factors.shape[0]

    def piece(d, t):
        total = weights[d, t, pl.ds(0, 1)] * factors[0]
        for r in range(1, rank):
            total += weights[d, t, pl.ds(r, 1)] * factors[r]
        return total.astype(BF)

    def step(i, carry):
        d = lax.rem(frame + i, nf)
        for t in range(2):
            send_buf[d, t] = piece(d, t)
        remote(send_buf.at[d], recv_buf.at[frame], send_sem, recv_sem, {"frame": d}).start()
        return carry

    lax.fori_loop(1, nf, step, 0)
    for t in range(2):
        recv_buf[frame, t] = piece(frame, t)


def place_rows(recv_buf, image, t, cols):
    coil, nf = lax.axis_index("coil"), lax.axis_size("frame")
    size = image.shape[2]
    rows = size // lax.axis_size("coil")
    lane = lax.broadcasted_iota(jnp.int32, (16, 128), 1)
    blocks = rows // 16
    for c in range(2):
        for rb in range(blocks):
            tiles = [jnp.zeros((16, 128), F32) for _ in range(-(-size // 128))]
            for f in range(nf):
                value = recv_buf[f, t].astype(F32)
                for tile, at, off, count in moves(f, cols, c * blocks + rb):
                    inside = (lane >= at) & (lane < at + count)
                    tiles[tile] = jnp.where(inside, roll(value, at - off), tiles[tile])
            at_row = pl.multiple_of(coil * rows + rb * 16, 16)
            for n, value in enumerate(tiles):
                width = min(128, size - 128 * n)
                image[t, c, pl.ds(at_row, 16), pl.ds(128 * n, width)] = value.astype(BF)[:, :width]


def spread_rows(image, t, sems):
    send, recv, _, _ = sems
    coil, nc = lax.axis_index("coil"), lax.axis_size("coil")
    rows = image.shape[2] // nc
    mine = pl.ds(pl.multiple_of(coil * rows, 16), rows)
    for way, step in ((0, 1), (1, nc - 1)):
        for c in (way, 1 - way):
            part = image.at[t, c, mine]
            remote(part, part, send.at[t, way, c], recv.at[t, way, c], {"coil": lax.rem(coil + step, nc)}).start()


def forward_rows(image, t, sems):
    send, recv, send2, recv2 = sems
    coil, nc = lax.axis_index("coil"), lax.axis_size("coil")
    rows = image.shape[2] // nc
    for way, step in ((0, 1), (1, nc - 1)):
        source = lax.rem(coil + nc - step, nc)
        part = image.at[t, way, pl.ds(pl.multiple_of(source * rows, 16), rows)]
        wait_bytes(part, recv.at[t, way, way])
        remote(part, part, send2.at[t, way], recv2.at[t, way], {"coil": lax.rem(coil + step, nc)}).start()


def finish_rows(image, t, sems):
    send, recv, send2, recv2 = sems
    coil, nc = lax.axis_index("coil"), lax.axis_size("coil")
    rows = image.shape[2] // nc
    part = image.at[t, 0, pl.ds(0, rows)]
    for way in range(2):
        wait_bytes(part, recv.at[t, way, 1 - way])
        wait_bytes(part, recv2.at[t, way])
        wait_bytes(part, send2.at[t, way])
        for c in range(2):
            wait_bytes(part, send.at[t, way, c])


def share_images(weights, factors, send_buf, recv_buf, image, cols, a2a, rows_sems, between=None):
    nf = lax.axis_size("frame")
    mix_and_send(weights, factors, send_buf, recv_buf, a2a.at[0], a2a.at[1])
    if between is not None:
        between()
    wait_bytes(recv_buf.at[pl.ds(0, nf - 1)], a2a.at[1])
    for t in range(2):
        place_rows(recv_buf, image, t, cols)
        spread_rows(image, t, rows_sems)
    for t in range(2):
        forward_rows(image, t, rows_sems)
    for t in range(2):
        finish_rows(image, t, rows_sems)
    wait_bytes(recv_buf.at[pl.ds(0, nf - 1)], a2a.at[0])


def pack_factors(spatial, factors):
    rank, _, rows, _ = spatial.shape
    cols = 10
    lane = lax.broadcasted_iota(jnp.int32, (16, 128), 1)
    blocks = rows // 16

    def one(r, carry):
        total = jnp.zeros((16, 128), F32)
        for c in range(2):
            for rb in range(blocks):
                off = (c * blocks + rb) * cols
                inside = (lane >= off) & (lane < off + cols)
                total = jnp.where(inside, roll(spatial[r, c, pl.ds(16 * rb, 16)], off), total)
        factors[r] = total
        return carry

    lax.fori_loop(0, rank, one, 0)


def row_sems():
    return [
        pltpu.SemaphoreType.DMA((2, 2, 2)),
        pltpu.SemaphoreType.DMA((2, 2, 2)),
        pltpu.SemaphoreType.DMA((2, 2)),
        pltpu.SemaphoreType.DMA((2, 2)),
    ]


def reduce_start(part, t, xa, xd, sems):
    s1, r1, s2, r2, s3, r3 = sems
    coil, nc = lax.axis_index("coil"), lax.axis_size("coil")
    rows = part.shape[2] // nc
    far = pl.ds(pl.multiple_of(lax.rem(coil + 2, nc) * rows, 16), rows)
    for way, step in ((0, 1), (1, nc - 1)):
        to = lax.rem(coil + step, nc)
        near = pl.ds(pl.multiple_of(to * rows, 16), rows)
        remote(part.at[t, way, far], xa.at[t, way], s1.at[t, way], r1.at[t, way], {"coil": to}).start()
        remote(part.at[t, 1 - way, near], xd.at[t, way], s2.at[t, way], r2.at[t, way], {"coil": to}).start()


def reduce_forward(part, t, xa, xsum, xs, sems):
    s1, r1, s2, r2, s3, r3 = sems
    coil, nc = lax.axis_index("coil"), lax.axis_size("coil")
    rows = part.shape[2] // nc
    for way, step in ((0, 1), (1, nc - 1)):
        to = lax.rem(coil + step, nc)
        near = pl.ds(pl.multiple_of(to * rows, 16), rows)
        wait_bytes(xa.at[t, way], r1.at[t, way])
        xsum[t, way] = xa[t, way] + part[t, way, near]
        remote(xsum.at[t, way], xs.at[t, way], s3.at[t, way], r3.at[t, way], {"coil": to}).start()


def reduce_finish(part, t, xd, xs, total, sems):
    s1, r1, s2, r2, s3, r3 = sems
    coil, nc = lax.axis_index("coil"), lax.axis_size("coil")
    size = part.shape[3]
    rows = part.shape[2] // nc
    mine = pl.ds(pl.multiple_of(coil * rows, 16), rows)
    for way in range(2):
        wait_bytes(xs.at[t, way], r3.at[t, way])
        wait_bytes(xd.at[t, 1 - way], r2.at[t, 1 - way])
        total[t, way, :, pl.ds(0, size)] = part[t, way, mine] + xs[t, way] + xd[t, 1 - way]


def send_columns(total, t, send_buf, recv_buf, sems, cols):
    frame, nf = lax.axis_index("frame"), lax.axis_size("frame")
    rows = total.shape[2]
    blocks = rows // 16
    lane = lax.broadcasted_iota(jnp.int32, (16, 128), 1)
    for f in range(nf):
        value = jnp.zeros((16, 128), F32)
        for c in range(2):
            for rb in range(blocks):
                for tile, at, off, count in moves(f, cols, c * blocks + rb):
                    inside = (lane >= off) & (lane < off + count)
                    value = jnp.where(inside, roll(total[t, c, pl.ds(16 * rb, 16), pl.ds(128 * tile, 128)], off - at), value)
        send_buf[t, f] = value

    def step(i, carry):
        d = lax.rem(frame + i, nf)
        remote(send_buf.at[t, d], recv_buf.at[t, frame], sems.at[0, t], sems.at[1, t], {"frame": d}).start()
        return carry

    lax.fori_loop(1, nf, step, 0)
    recv_buf[t, frame] = send_buf[t, frame]


def gradient_step(weights, recv_buf, t, grad):
    nf = lax.axis_size("frame")
    rank = grad.shape[0]

    def step(f, acc):
        value = recv_buf[t, f]
        return tuple(acc[r] + weights[f, t, pl.ds(r, 1)] * value for r in range(rank))

    acc = lax.fori_loop(0, nf, step, tuple(jnp.zeros((16, 128), F32) for _ in range(rank)))
    for r in range(rank):
        grad[r] = acc[r] if t == 0 else grad[r] + acc[r]


def unpack_factors(factors, spatial):
    rank, _, rows, cols = spatial.shape
    blocks = rows // 16

    def one(r, carry):
        value = factors[r]
        for c in range(2):
            for rb in range(blocks):
                spatial[r, c, pl.ds(16 * rb, 16)] = roll(value, -(c * blocks + rb) * cols)[:, :cols]
        return carry

    lax.fori_loop(0, rank, one, 0)


LOCAL = ("spatial", "index", "sens", "data") + TABLES


def whole_kernel(weight, level, *refs, **scratch):
    s = types.SimpleNamespace(**scratch)
    sources, (spatial_next, image) = refs[:len(LOCAL)], refs[len(LOCAL):]
    frame, nf = lax.axis_index("frame"), lax.axis_size("frame")
    cols = spatial_next.shape[3]
    copies = {}
    for n, (name, source) in enumerate(zip(LOCAL, sources)):
        copies[name] = pltpu.make_async_copy(source, scratch[name], s.lsem.at[n])
        copies[name].start()

    def ready(*names):
        for name in names:
            copies[name].wait()

    enter(None)

    def exchange(i, carry):
        remote(weight, s.weights.at[frame], s.wsem.at[0], s.wsem.at[1], {"frame": lax.rem(frame + i, nf)}).start()
        return carry

    lax.fori_loop(1, nf, exchange, 0)
    s.weights[frame] = weight[...]
    ready("spatial")
    pack_factors(s.spatial, s.factors)
    ready("index", *TABLES)
    kernel_quads(s, level, 0)
    wait_bytes(s.weights.at[pl.ds(0, nf - 1)], s.wsem.at[1])
    mix_and_send(s.weights, s.factors, s.send1, s.recv1, s.asem.at[0], s.asem.at[1])
    kernel_quads(s, level, 1)
    ready("sens", "data")
    for c in range(s.sens.shape[0]):
        for h in range(2):
            s.sf[c, h] = folded(s, s.sens[c, h])
    wait_bytes(s.recv1.at[pl.ds(0, nf - 1)], s.asem.at[1])
    rows1 = (s.p0, s.p1, s.p2, s.p3)
    for t in range(2):
        place_rows(s.recv1, s.old, t, cols)
        spread_rows(s.old, t, rows1)
    fold_data(s, 0)
    for t in range(2):
        forward_rows(s.old, t, rows1)
    fold_data(s, 1)
    finish_rows(s.old, 0, rows1)
    for h in range(2):
        s.imf[0, h] = folded(s, s.old[0, h])
    sems = (s.s1, s.r1, s.s2, s.r2, s.s3, s.r3)
    coils = s.sens.shape[0]

    def pair(q, carry):
        run_pair(s, q // coils, q % coils)

        @pl.when(q == coils - 1)
        def _():
            unfold(s, 0)
            reduce_start(s.part, 0, s.xa, s.xd, sems)
            finish_rows(s.old, 1, rows1)
            for h in range(2):
                s.imf[1, h] = folded(s, s.old[1, h])

        @pl.when(q == coils)
        def _():
            reduce_forward(s.part, 0, s.xa, s.xsum, s.xs, sems)

        return carry

    lax.fori_loop(0, 2 * coils, pair, 0)
    unfold(s, 1)
    reduce_start(s.part, 1, s.xa, s.xd, sems)
    reduce_finish(s.part, 0, s.xd, s.xs, s.total, sems)
    send_columns(s.total, 0, s.rsend, s.rrecv, s.rsem, cols)
    reduce_forward(s.part, 1, s.xa, s.xsum, s.xs, sems)
    wait_bytes(s.rrecv.at[0, pl.ds(0, nf - 1)], s.rsem.at[1, 0])
    gradient_step(s.weights, s.rrecv, 0, s.grad)
    reduce_finish(s.part, 1, s.xd, s.xs, s.total, sems)
    send_columns(s.total, 1, s.rsend, s.rrecv, s.rsem, cols)
    wait_bytes(s.rrecv.at[1, pl.ds(0, nf - 1)], s.rsem.at[1, 1])
    gradient_step(s.weights, s.rrecv, 1, s.grad)
    for r in range(s.factors.shape[0]):
        s.factors[r] = s.factors[r] - STEP_SIZE * s.grad[r]
    share_images(s.weights, s.factors, s.send2, s.recv2, image, cols, s.bsem, (s.q0, s.q1, s.q2, s.q3), lambda: unpack_factors(s.factors, spatial_next))
    wait_bytes(s.weights.at[pl.ds(0, nf - 1)], s.wsem.at[0])
    wait_bytes(s.recv1.at[pl.ds(0, nf - 1)], s.asem.at[0])
    for t in range(2):
        wait_bytes(s.rrecv.at[t, pl.ds(0, nf - 1)], s.rsem.at[0, t])
        for way in range(2):
            for sem in (s.s1, s.s2, s.s3):
                wait_bytes(s.xa.at[t, way], sem.at[t, way])


def body(spatial, temporal, sensitivity, coil_data, kernel_index, kernel_level):
    size = sensitivity.shape[2]
    rank, _, rows_mine, cols = spatial.shape
    frames, coils = coil_data.shape[:2]
    nf = lax.axis_size("frame")
    padded = jnp.pad(spatial, ((0, 0), (0, 0), (0, 0), (0, 128 - cols)))
    weight = jnp.broadcast_to(temporal[:, :, None], temporal.shape + (128,))
    level = kernel_level / (4.0 * size * size)
    tables = make_tables(size)
    half = size // 2
    wide = tables["place"].shape[1] // 2
    rows = tables["f2c"].shape[0]
    slots = tables["mirror"].shape[1]
    chunks = slots // 128
    operands = dict(spatial=padded, index=kernel_index, sens=sensitivity, data=coil_data)
    operands.update({n: jnp.asarray(tables[n]) for n in TABLES})
    vm = pl.BlockSpec(memory_space=pltpu.VMEM)
    block = pltpu.VMEM((frames, 2, rows_mine, size), F32)
    dma = pltpu.SemaphoreType.DMA
    scratch = {n: pltpu.VMEM(x.shape, x.dtype) for n, x in operands.items()}
    scratch.update(
        kq=pltpu.VMEM((frames, 4, rows, slots), F32),
        sf=pltpu.VMEM((coils, 2, size, 2 * wide), F32),
        imf=pltpu.VMEM((frames, 2, size, 2 * wide), F32),
        res=pltpu.VMEM((frames, 2, size, 2 * wide), F32),
        lc=pltpu.VMEM((2, 4 * half, half), BF),
        ls=pltpu.VMEM((2, 4 * half, half), BF),
        ge=pltpu.VMEM((chunks, 3 * half, 512), BF),
        go=pltpu.VMEM((chunks, 3 * half, 512), BF),
        spa=pltpu.VMEM((chunks, rows, 512), F32),
        spb=pltpu.VMEM((chunks, rows, 512), F32),
        za=pltpu.VMEM((chunks, 3 * rows, 512), BF),
        zb=pltpu.VMEM((chunks, 3 * rows, 512), BF),
        lhc=pltpu.VMEM((4 * half, 3 * slots), BF),
        lhs=pltpu.VMEM((4 * half, 3 * slots), BF),
        oc=pltpu.VMEM((4 * half, half), F32),
        osn=pltpu.VMEM((4 * half, half), F32),
        part=pltpu.VMEM((frames, 2, size, size), F32),
        old=pltpu.VMEM((frames, 2, size, size), BF),
        weights=pltpu.VMEM((nf, frames, rank, 128), F32),
        factors=pltpu.VMEM((rank, 16, 128), F32),
        grad=pltpu.VMEM((rank, 16, 128), F32),
        send1=pltpu.VMEM((nf, frames, 16, 128), BF),
        recv1=pltpu.VMEM((nf, frames, 16, 128), BF),
        send2=pltpu.VMEM((nf, frames, 16, 128), BF),
        recv2=pltpu.VMEM((nf, frames, 16, 128), BF),
        rsend=pltpu.VMEM((frames, nf, 16, 128), F32),
        rrecv=pltpu.VMEM((frames, nf, 16, 128), F32),
        xa=block, xd=block, xsum=block, xs=block,
        total=pltpu.VMEM((frames, 2, rows_mine, -(-size // 128) * 128), F32),
        lsem=dma((len(LOCAL),)),
        wsem=dma((2,)), asem=dma((2,)), bsem=dma((2,)), rsem=dma((2, 2)),
        s1=dma((2, 2)), r1=dma((2, 2)), s2=dma((2, 2)), r2=dma((2, 2)), s3=dma((2, 2)), r3=dma((2, 2)),
    )
    for first in "pq":
        scratch.update({first + str(n): sem for n, sem in enumerate(row_sems())})
    return pl.pallas_call(
        whole_kernel,
        out_shape=(jax.ShapeDtypeStruct(spatial.shape, F32), jax.ShapeDtypeStruct((frames, 2, size, size), BF)),
        in_specs=[vm, pl.BlockSpec(memory_space=pltpu.SMEM)] + [pl.BlockSpec(memory_space=pl.ANY)] * len(LOCAL),
        out_specs=(vm, vm),
        scratch_shapes=scratch,
        compiler_params=pltpu.CompilerParams(vmem_limit_bytes=60 * 2**20, collective_id=0, has_side_effects=True),
    )(weight, level, *[operands[n] for n in LOCAL])


def solution(mesh):
    placed = (
        P(None, None, "coil", "frame"),
        P("frame", None),
        P("coil", None, None, None),
        P("frame", "coil", None, None, None),
        P("frame", None, None),
        P("frame", None),
    )
    return jax.shard_map(
        body,
        mesh=mesh,
        in_specs=placed,
        out_specs=(P(None, None, "coil", "frame"), P("frame", None, None, None)),
        check_vma=False,
    )
```

```python
import types

import jax
import jax.numpy as jnp
import ml_dtypes
import numpy as np
from jax import lax
from jax.experimental import pallas as pl
from jax.experimental.pallas import tpu as pltpu
from jax.sharding import PartitionSpec as P

STEP_SIZE = 0.15
BF = jnp.bfloat16
F32 = jnp.float32


def halves(table):
    high = table.astype(ml_dtypes.bfloat16)
    low = (table - high.astype(np.float64)).astype(ml_dtypes.bfloat16)
    return high, low


def make_tables(size, blocks, cols):
    half = size // 2
    slots = -(-(size + 1) // 128) * 128
    rows = -(-(size + 1) // 16) * 16
    p = np.arange(half) + 0.5
    k = np.arange(slots)
    valid = (k <= size).astype(np.float64)
    angle = np.pi / size * np.outer(p, k)
    cos, sin = np.cos(angle) * valid, np.sin(angle) * valid
    cos[:, size] = 0.0
    sin[:, 0] = 0.0
    weight = np.where((k == 0) | (k == size), 0.5, 1.0)
    out = {}
    for name, tab in (("c", cos), ("s", sin)):
        hi, lo = halves(tab)
        out["f1" + name] = np.concatenate([hi, lo], axis=1)
        rhi, rlo = hi[:, :rows].T, lo[:, :rows].T
        out["f2" + name] = np.concatenate([rhi, rhi, rlo], axis=1)
        whi, wlo = halves(tab * weight)
        out["i1" + name] = np.concatenate([whi[:, :rows], whi[:, :rows], wlo[:, :rows]], axis=1)
        parts = []
        for j in range(0, slots, 128):
            parts += [whi.T[j:j + 128], whi.T[j:j + 128], wlo.T[j:j + 128]]
        out["i2" + name] = np.concatenate(parts, axis=0)
    wide = -(-half // 128) * 128
    place = np.zeros((size, 2 * wide))
    q = np.arange(half)
    place[half + q, q] = 1
    place[half - 1 - q, wide + q] = 1
    out["place"] = place.astype(ml_dtypes.bfloat16)
    out["unplace"] = place.T.astype(ml_dtypes.bfloat16)
    out["flip"] = np.eye(half)[::-1].astype(ml_dtypes.bfloat16)
    mirror = np.zeros((2 * size, slots))
    kk = np.arange(size + 1)
    mirror[(2 * size - kk) % (2 * size), kk] = 1
    out["mirror"] = mirror.astype(ml_dtypes.bfloat16)
    out["mirror_rows"] = mirror.T[:rows].astype(ml_dtypes.bfloat16)
    spread = np.zeros((32, 128))
    for c in range(2):
        for rb in range(blocks):
            for j in range(cols):
                spread[2 * j + c, (c * blocks + rb) * cols + j] = 1
    out["spread"] = spread.astype(ml_dtypes.bfloat16)
    return out


TABLES = ("f1c", "f1s", "f2c", "f2s", "i1c", "i1s", "i2c", "i2s", "place", "unplace", "flip", "mirror", "mirror_rows", "spread")


def mm(a, b):
    return jnp.dot(a, b, preferred_element_type=F32)


def split(x):
    high = x.astype(BF)
    low = (x - high.astype(F32)).astype(BF)
    return high, low


def kernel_quads(s, level, t):
    rows = s.f2c.shape[0]
    slots = s.mirror.shape[1]
    size = 2 * s.flip.shape[0]
    values = [level[t, m] * (0.25 / (size * size)) for m in range(level.shape[1])]
    ib = s.index[t].astype(F32).astype(BF)
    flipped = mm(ib, s.mirror[...]).astype(BF)
    low = mm(s.mirror_rows[...], jnp.concatenate([ib[:, :slots], flipped], axis=1))
    quads = (ib[:rows, :slots].astype(F32), flipped[:rows].astype(F32), low[:, :slots], low[:, slots:])
    for n, quad in enumerate(quads):
        value = jnp.full(quad.shape, values[0], F32)
        for m in range(1, len(values)):
            value = jnp.where(quad > m - 0.5, values[m], value)
        s.kq[t, n] = value


def folded(s, x):
    half = s.flip.shape[0]
    left = mm(s.flip[...], x[:half]).astype(BF)
    return mm(jnp.concatenate([x[half:], left], axis=0), s.place[...])


def fold_data(s, t):
    for c in range(s.sens.shape[0]):
        dr, di = folded(s, s.data[t, c, 0]), folded(s, s.data[t, c, 1])
        sr, si = s.sf[c, 0], s.sf[c, 1]
        gr, gi = -(sr * dr + si * di), si * dr - sr * di
        if c:
            gr, gi = s.res[t, 0] + gr, s.res[t, 1] + gi
        s.res[t, 0] = gr
        s.res[t, 1] = gi


def unfold(s, t):
    half = s.flip.shape[0]
    for h in range(2):
        high, low = split(s.res[t, h])
        cols = mm(high, s.unplace[...]) + mm(low, s.unplace[...])
        s.part[t, h, pl.ds(half, half)] = cols[:half]
        high, low = split(cols[half:])
        s.part[t, h, pl.ds(0, half)] = mm(s.flip[...], high) + mm(s.flip[...], low)


def run_pair(s, t, c):
    half = s.flip.shape[0]
    wide = s.place.shape[1] // 2
    rows = s.f2c.shape[0]
    slots = s.mirror.shape[1]
    chunks = slots // 128
    for r in range(0, half, 16):
        parts = {}
        for a, row in (("R", r), ("L", half + r)):
            for b, col in (("R", 0), ("L", wide)):
                sl = (pl.ds(row, 16), pl.ds(col, half))
                sr, si = s.sf[c, 0, sl[0], sl[1]], s.sf[c, 1, sl[0], sl[1]]
                ir, ii = s.imf[t, 0, sl[0], sl[1]], s.imf[t, 1, sl[0], sl[1]]
                parts[a + b] = (sr * ir - si * ii, sr * ii + si * ir)
        for h in range(2):
            rr, rl, lr, ll = (parts[n][h] for n in ("RR", "RL", "LR", "LL"))
            re, ro, le, lo = rr + rl, rr - rl, lr + ll, lr - ll
            for k, (xc, xs) in enumerate(((re + le, ro + lo), (re - le, ro - lo))):
                at = (2 * k + h) * half + r
                hc, wc = split(xc)
                hs, ws = split(xs)
                s.lc[0, pl.ds(at, 16)] = hc
                s.lc[1, pl.ds(at, 16)] = wc
                s.ls[0, pl.ds(at, 16)] = hs
                s.ls[1, pl.ds(at, 16)] = ws
    for n, (lref, tab) in enumerate(((s.lc, s.f1c), (s.ls, s.f1s))):
        first = mm(lref[0], tab[:, :slots]) + mm(lref[0], tab[:, slots:]) + mm(lref[1], tab[:, :slots])
        for k, dest in enumerate((s.ge, s.go)):
            for h in range(2):
                part = first[(2 * k + h) * half:(2 * k + h + 1) * half]
                high, low = split(part)
                for j in range(chunks):
                    lanes = pl.ds((2 * n + h) * 128, 128)
                    dest[j, pl.ds(0, half), lanes] = high[:, j * 128:(j + 1) * 128]
                    dest[j, pl.ds(half, half), lanes] = low[:, j * 128:(j + 1) * 128]
                    dest[j, pl.ds(2 * half, half), lanes] = high[:, j * 128:(j + 1) * 128]
    for j in range(chunks):
        s.spa[j] = mm(s.f2c[...], s.ge[j])
        s.spb[j] = mm(s.f2s[...], s.go[j])
    for j in range(chunks):
        for r in range(0, rows, 16):
            rs = pl.ds(r, 16)
            aar, aai, abr, abi = (s.spa[j, rs, pl.ds(128 * m, 128)] for m in range(4))
            bar, bai, bbr, bbi = (s.spb[j, rs, pl.ds(128 * m, 128)] for m in range(4))
            kpp, kpm, kmp, kmm = (s.kq[t, m, rs, pl.ds(128 * j, 128)] for m in range(4))
            ur, ui, vr, vi = aar - bbr, aai - bbi, aar + bbr, aai + bbi
            wr, wi, qr, qi = abr + bar, abi + bai, abr - bar, abi - bai
            ppr, ppi = kpp * (ur + wi), kpp * (ui - wr)
            mmr, mmi = kmm * (ur - wi), kmm * (ui + wr)
            pmr, pmi = kpm * (vr - qi), kpm * (vi + qr)
            mpr, mpi = kmp * (vr + qi), kmp * (vi - qr)
            s1r, s1i, s2r, s2i = ppr + mmr, ppi + mmi, pmr + mpr, pmi + mpi
            d1r, d1i, d2r, d2i = ppr - mmr, ppi - mmi, pmr - mpr, pmi - mpi
            for dest, vals in ((s.za, (s1r + s2r, s1i + s2i, d2i - d1i, d1r - d2r)), (s.zb, (-(d1i + d2i), d1r + d2r, s2r - s1r, s2i - s1i))):
                for m, value in enumerate(vals):
                    high, low = split(value)
                    lanes = pl.ds(128 * m, 128)
                    dest[j, pl.ds(r, 16), lanes] = high
                    dest[j, pl.ds(rows + r, 16), lanes] = low
                    dest[j, pl.ds(2 * rows + r, 16), lanes] = high
    for j in range(chunks):
        for n, (tab, src) in enumerate(((s.i1c, s.za), (s.i1s, s.zb))):
            high, low = split(mm(tab[...], src[j]))
            for m in range(4):
                dest = s.lhc if m < 2 else s.lhs
                rs = pl.ds((2 * n + m % 2) * half, half)
                for place_at, value in enumerate((high, low, high)):
                    dest[rs, pl.ds(j * 384 + place_at * 128, 128)] = value[:, 128 * m:128 * (m + 1)]
    s.oc[...] = mm(s.lhc[...], s.i2c[...])
    s.osn[...] = mm(s.lhs[...], s.i2s[...])
    for r in range(0, half, 16):
        quad = {}
        for h in range(2):
            ee, oe = s.oc[pl.ds(h * half + r, 16)], s.oc[pl.ds((2 + h) * half + r, 16)]
            eo, oo = s.osn[pl.ds(h * half + r, 16)], s.osn[pl.ds((2 + h) * half + r, 16)]
            quad["RR", h] = (ee + oe) + (eo + oo)
            quad["RL", h] = (ee + oe) - (eo + oo)
            quad["LR", h] = (ee - oe) + (eo - oo)
            quad["LL", h] = (ee - oe) - (eo - oo)
        for a, row in (("R", r), ("L", half + r)):
            for b, col in (("R", 0), ("L", wide)):
                sl = (pl.ds(row, 16), pl.ds(col, half))
                sr, si = s.sf[c, 0, sl[0], sl[1]], s.sf[c, 1, sl[0], sl[1]]
                yr, yi = quad[a + b, 0], quad[a + b, 1]
                s.res[t, 0, sl[0], sl[1]] += sr * yr + si * yi
                s.res[t, 1, sl[0], sl[1]] += sr * yi - si * yr


def plane_shape(sp):
    rank, _, rows, cols = sp.shape
    return rank, rows, rows // 16, cols


def lane_masks(cols, groups):
    lane = lax.broadcasted_iota(jnp.int32, (16, 128), 1)
    return lane


def moves(block, cols, group):
    off, start = group * cols, block * cols
    tile, at = start // 128, start % 128
    first = min(cols, 128 - at)
    out = [(tile, at, off, first)]
    if first < cols:
        out.append((tile + 1, 0, off + first, cols - first))
    return out


def roll(x, shift):
    shift = shift % 128
    return pltpu.roll(x, shift, 1) if shift else x


def enter(peers):
    barrier = pltpu.get_barrier_semaphore()
    frame, coil = lax.axis_index("frame"), lax.axis_index("coil")
    nf, nc = lax.axis_size("frame"), lax.axis_size("coil")

    def greet(i, carry):
        pl.semaphore_signal(barrier, inc=1, device_id={"frame": lax.rem(frame + i, nf)}, device_id_type=pl.DeviceIdType.MESH)
        return carry

    lax.fori_loop(1, nf, greet, 0)
    for step in (1, nc - 1):
        pl.semaphore_signal(barrier, inc=1, device_id={"coil": lax.rem(coil + step, nc)}, device_id_type=pl.DeviceIdType.MESH)
    pl.semaphore_wait(barrier, nf + 1)


def remote(src, dst, send, recv, where):
    return pltpu.make_async_remote_copy(src_ref=src, dst_ref=dst, send_sem=send, recv_sem=recv, device_id=where, device_id_type=pl.DeviceIdType.MESH)


def wait_bytes(ref, sem):
    pltpu.make_async_copy(ref, ref, sem).wait()


def mix_and_send(weights, factors, t, send_buf, recv_buf, sems):
    frame, nf = lax.axis_index("frame"), lax.axis_size("frame")
    rank = factors.shape[0]

    def piece(d):
        total = weights[d, t, pl.ds(0, 1)] * factors[0]
        for r in range(1, rank):
            total += weights[d, t, pl.ds(r, 1)] * factors[r]
        return total.astype(BF)

    def step(i, carry):
        d = lax.rem(frame + i, nf)
        send_buf[t, d] = piece(d)
        remote(send_buf.at[t, d], recv_buf.at[t, frame], sems.at[0, t], sems.at[1, t], {"frame": d}).start()
        return carry

    lax.fori_loop(1, nf, step, 0)
    recv_buf[t, frame] = piece(frame)


def wait_frames(buf, t, sem):
    wait_bytes(buf.at[t, pl.ds(0, buf.shape[1] - 1)], sem)


def place_rows(recv_buf, image, t, cols):
    coil, nf = lax.axis_index("coil"), lax.axis_size("frame")
    size = image.shape[2]
    rows = size // lax.axis_size("coil")
    lane = lax.broadcasted_iota(jnp.int32, (16, 128), 1)
    blocks = rows // 16
    for c in range(2):
        for rb in range(blocks):
            tiles = [jnp.zeros((16, 128), F32) for _ in range(-(-size // 128))]
            for f in range(nf):
                value = recv_buf[t, f].astype(F32)
                for tile, at, off, count in moves(f, cols, c * blocks + rb):
                    inside = (lane >= at) & (lane < at + count)
                    tiles[tile] = jnp.where(inside, roll(value, at - off), tiles[tile])
            at_row = pl.multiple_of(coil * rows + rb * 16, 16)
            for n, value in enumerate(tiles):
                width = min(128, size - 128 * n)
                image[t, c, pl.ds(at_row, 16), pl.ds(128 * n, width)] = value.astype(BF)[:, :width]


def spread_rows(image, t, sems):
    send, recv, _, _ = sems
    coil, nc = lax.axis_index("coil"), lax.axis_size("coil")
    rows = image.shape[2] // nc
    mine = pl.ds(pl.multiple_of(coil * rows, 16), rows)
    for way, step in ((0, 1), (1, nc - 1)):
        for c in (way, 1 - way):
            part = image.at[t, c, mine]
            remote(part, part, send.at[t, way, c], recv.at[t, way, c], {"coil": lax.rem(coil + step, nc)}).start()


def forward_rows(image, t, sems):
    send, recv, send2, recv2 = sems
    coil, nc = lax.axis_index("coil"), lax.axis_size("coil")
    rows = image.shape[2] // nc
    for way, step in ((0, 1), (1, nc - 1)):
        source = lax.rem(coil + nc - step, nc)
        part = image.at[t, way, pl.ds(pl.multiple_of(source * rows, 16), rows)]
        wait_bytes(part, recv.at[t, way, way])
        remote(part, part, send2.at[t, way], recv2.at[t, way], {"coil": lax.rem(coil + step, nc)}).start()


def finish_rows(image, t, sems):
    send, recv, send2, recv2 = sems
    coil, nc = lax.axis_index("coil"), lax.axis_size("coil")
    rows = image.shape[2] // nc
    part = image.at[t, 0, pl.ds(0, rows)]
    for way in range(2):
        wait_bytes(part, recv.at[t, way, 1 - way])
        wait_bytes(part, recv2.at[t, way])
        wait_bytes(part, send2.at[t, way])
        for c in range(2):
            wait_bytes(part, send.at[t, way, c])


def share_images(s, image, cols, sems, between):
    for t in range(2):
        mix_and_send(s.weights, s.factors, t, s.send2, s.recv2, s.bsem)
    between()
    for t in range(2):
        wait_frames(s.recv2, t, s.bsem.at[1, t])
        place_rows(s.recv2, image, t, cols)
        spread_rows(image, t, sems)
    for t in range(2):
        forward_rows(image, t, sems)
    for t in range(2):
        finish_rows(image, t, sems)
        wait_frames(s.send2, t, s.bsem.at[0, t])


def thirds(x):
    high, low = split(x)
    rest = (x - high.astype(F32)) - low.astype(F32)
    return high, low, rest.astype(BF)


def group_mask(rb, blocks, cols):
    lane = lax.broadcasted_iota(jnp.int32, (16, 128), 1)
    first, second = rb * cols, (blocks + rb) * cols
    return ((lane >= first) & (lane < first + cols)) | ((lane >= second) & (lane < second + cols))


def pack_factors(s):
    rank, cols, _, rows = s.spatial.shape
    blocks = rows // 16
    s.flat[...] = jnp.zeros(s.flat.shape, F32)
    for r in range(rank):
        for j in range(cols):
            s.flat[pl.ds(2 * j, 2), pl.ds(128 * r, rows)] = s.spatial[r, j]
    turned = sum(lax.dot_general(x, s.spread[...], (((0,), (0,)), ((), ())), preferred_element_type=F32) for x in thirds(s.flat[...]))
    for r in range(rank):
        total = jnp.zeros((16, 128), F32)
        for rb in range(blocks):
            at = 128 * r + 16 * rb
            total = jnp.where(group_mask(rb, blocks, cols), turned[at:at + 16], total)
        s.factors[r] = total


def unpack_factors(s, spatial_next):
    rank, cols, _, rows = spatial_next.shape
    blocks = rows // 16
    s.wide[...] = jnp.zeros(s.wide.shape, F32)
    for r in range(rank):
        value = s.factors[r]
        for rb in range(blocks):
            s.wide[pl.ds(128 * r + 16 * rb, 16)] = jnp.where(group_mask(rb, blocks, cols), value, 0.0)
    turned = sum(lax.dot_general(s.spread[...], x, (((1,), (1,)), ((), ())), preferred_element_type=F32) for x in thirds(s.wide[...]))
    for r in range(rank):
        for j in range(cols):
            spatial_next[r, j] = turned[2 * j:2 * j + 2, 128 * r:128 * r + rows]


def widen_weights(s):
    nf, frames, rank = s.raw.shape
    one = lax.broadcasted_iota(jnp.int32, (rank, rank), 0) == lax.broadcasted_iota(jnp.int32, (rank, rank), 1)

    def step(d, carry):
        for t in range(frames):
            row = jnp.broadcast_to(s.raw[d, pl.ds(t, 1)], (rank, rank))
            column = jnp.sum(jnp.where(one, row, 0.0), axis=1, keepdims=True)
            s.weights[d, t] = jnp.broadcast_to(column, (rank, 128))
        return carry

    lax.fori_loop(0, nf, step, 0, unroll=8)


def row_sems():
    return [
        pltpu.SemaphoreType.DMA((2, 2, 2)),
        pltpu.SemaphoreType.DMA((2, 2, 2)),
        pltpu.SemaphoreType.DMA((2, 2)),
        pltpu.SemaphoreType.DMA((2, 2)),
    ]


def reduce_start(part, t, xa, xd, sems):
    s1, r1, s2, r2, s3, r3 = sems
    coil, nc = lax.axis_index("coil"), lax.axis_size("coil")
    rows = part.shape[2] // nc
    far = pl.ds(pl.multiple_of(lax.rem(coil + 2, nc) * rows, 16), rows)
    for way, step in ((0, 1), (1, nc - 1)):
        to = lax.rem(coil + step, nc)
        near = pl.ds(pl.multiple_of(to * rows, 16), rows)
        remote(part.at[t, way, far], xa.at[t, way], s1.at[t, way], r1.at[t, way], {"coil": to}).start()
        remote(part.at[t, 1 - way, near], xd.at[t, way], s2.at[t, way], r2.at[t, way], {"coil": to}).start()


def reduce_forward(part, t, xa, xsum, xs, sems):
    s1, r1, s2, r2, s3, r3 = sems
    coil, nc = lax.axis_index("coil"), lax.axis_size("coil")
    rows = part.shape[2] // nc
    for way, step in ((0, 1), (1, nc - 1)):
        to = lax.rem(coil + step, nc)
        near = pl.ds(pl.multiple_of(to * rows, 16), rows)
        wait_bytes(xa.at[t, way], r1.at[t, way])
        xsum[t, way] = xa[t, way] + part[t, way, near]
        remote(xsum.at[t, way], xs.at[t, way], s3.at[t, way], r3.at[t, way], {"coil": to}).start()


def reduce_finish(part, t, xd, xs, total, sems):
    s1, r1, s2, r2, s3, r3 = sems
    coil, nc = lax.axis_index("coil"), lax.axis_size("coil")
    size = part.shape[3]
    rows = part.shape[2] // nc
    mine = pl.ds(pl.multiple_of(coil * rows, 16), rows)
    for way in range(2):
        wait_bytes(xs.at[t, way], r3.at[t, way])
        wait_bytes(xd.at[t, 1 - way], r2.at[t, 1 - way])
        total[t, way, :, pl.ds(0, size)] = part[t, way, mine] + xs[t, way] + xd[t, 1 - way]


def send_columns(total, t, send_buf, recv_buf, sems, cols):
    frame, nf = lax.axis_index("frame"), lax.axis_size("frame")
    rows = total.shape[2]
    blocks = rows // 16
    lane = lax.broadcasted_iota(jnp.int32, (16, 128), 1)
    for f in range(nf):
        value = jnp.zeros((16, 128), F32)
        for c in range(2):
            for rb in range(blocks):
                for tile, at, off, count in moves(f, cols, c * blocks + rb):
                    inside = (lane >= off) & (lane < off + count)
                    value = jnp.where(inside, roll(total[t, c, pl.ds(16 * rb, 16), pl.ds(128 * tile, 128)], off - at), value)
        send_buf[t, f] = value

    def step(i, carry):
        d = lax.rem(frame + i, nf)
        remote(send_buf.at[t, d], recv_buf.at[t, frame], sems.at[0, t], sems.at[1, t], {"frame": d}).start()
        return carry

    lax.fori_loop(1, nf, step, 0)
    recv_buf[t, frame] = send_buf[t, frame]


def gradient_step(weights, recv_buf, t, grad):
    nf = lax.axis_size("frame")
    rank = grad.shape[0]

    def step(f, acc):
        value = recv_buf[t, f]
        return tuple(acc[r] + weights[f, t, pl.ds(r, 1)] * value for r in range(rank))

    acc = lax.fori_loop(0, nf, step, tuple(jnp.zeros((16, 128), F32) for _ in range(rank)))
    for r in range(rank):
        grad[r] = acc[r] if t == 0 else grad[r] + acc[r]


LOCAL = ("spatial", "index", "sens", "data") + TABLES


def whole_kernel(weight, level, *refs, **scratch):
    s = types.SimpleNamespace(**scratch)
    sources, (spatial_next, image) = refs[:len(LOCAL)], refs[len(LOCAL):]
    frame, nf = lax.axis_index("frame"), lax.axis_size("frame")
    cols = spatial_next.shape[1]
    copies = {}
    for n, (name, source) in enumerate(zip(LOCAL, sources)):
        copies[name] = pltpu.make_async_copy(source, scratch[name], s.lsem.at[n])
        copies[name].start()

    def ready(*names):
        for name in names:
            copies[name].wait()

    enter(None)

    def exchange(i, carry):
        remote(weight, s.raw.at[frame], s.wsem.at[0], s.wsem.at[1], {"frame": lax.rem(frame + i, nf)}).start()
        return carry

    lax.fori_loop(1, nf, exchange, 0)
    s.raw[frame] = weight[...]
    ready("spatial", "spread")
    pack_factors(s)
    ready("index", *(n for n in TABLES if n != "spread"))
    kernel_quads(s, level, 0)
    wait_bytes(s.raw.at[pl.ds(0, nf - 1)], s.wsem.at[1])
    widen_weights(s)
    for t in range(2):
        mix_and_send(s.weights, s.factors, t, s.send1, s.recv1, s.asem)
    kernel_quads(s, level, 1)
    ready("sens", "data")
    for c in range(s.sens.shape[0]):
        for h in range(2):
            s.sf[c, h] = folded(s, s.sens[c, h])
    rows1 = (s.p0, s.p1, s.p2, s.p3)
    for t in range(2):
        wait_frames(s.recv1, t, s.asem.at[1, t])
        place_rows(s.recv1, s.old, t, cols)
        spread_rows(s.old, t, rows1)
    fold_data(s, 0)
    for t in range(2):
        forward_rows(s.old, t, rows1)
    fold_data(s, 1)
    finish_rows(s.old, 0, rows1)
    for h in range(2):
        s.imf[0, h] = folded(s, s.old[0, h])
    sems = (s.s1, s.r1, s.s2, s.r2, s.s3, s.r3)
    coils = s.sens.shape[0]

    def pair(q, carry):
        run_pair(s, q // coils, q % coils)

        @pl.when(q == coils - 1)
        def _():
            unfold(s, 0)
            reduce_start(s.part, 0, s.xa, s.xd, sems)
            finish_rows(s.old, 1, rows1)
            for h in range(2):
                s.imf[1, h] = folded(s, s.old[1, h])

        @pl.when(q == coils)
        def _():
            reduce_forward(s.part, 0, s.xa, s.xsum, s.xs, sems)

        return carry

    lax.fori_loop(0, 2 * coils, pair, 0)
    unfold(s, 1)
    reduce_start(s.part, 1, s.xa, s.xd, sems)
    reduce_finish(s.part, 0, s.xd, s.xs, s.total, sems)
    send_columns(s.total, 0, s.rsend, s.rrecv, s.rsem, cols)
    reduce_forward(s.part, 1, s.xa, s.xsum, s.xs, sems)
    wait_bytes(s.rrecv.at[0, pl.ds(0, nf - 1)], s.rsem.at[1, 0])
    gradient_step(s.weights, s.rrecv, 0, s.grad)
    reduce_finish(s.part, 1, s.xd, s.xs, s.total, sems)
    send_columns(s.total, 1, s.rsend, s.rrecv, s.rsem, cols)
    wait_bytes(s.rrecv.at[1, pl.ds(0, nf - 1)], s.rsem.at[1, 1])
    gradient_step(s.weights, s.rrecv, 1, s.grad)
    for r in range(s.factors.shape[0]):
        s.factors[r] = s.factors[r] - STEP_SIZE * s.grad[r]
    share_images(s, image, cols, (s.q0, s.q1, s.q2, s.q3), lambda: unpack_factors(s, spatial_next))
    wait_bytes(s.raw.at[pl.ds(0, nf - 1)], s.wsem.at[0])
    for t in range(2):
        wait_frames(s.send1, t, s.asem.at[0, t])
    for t in range(2):
        wait_bytes(s.rrecv.at[t, pl.ds(0, nf - 1)], s.rsem.at[0, t])
        for way in range(2):
            for sem in (s.s1, s.s2, s.s3):
                wait_bytes(s.xa.at[t, way], sem.at[t, way])


def body(spatial, temporal, sensitivity, coil_data, kernel_index, kernel_level):
    size = sensitivity.shape[2]
    rank, _, rows_mine, cols = spatial.shape
    frames, coils = coil_data.shape[:2]
    nf = lax.axis_size("frame")
    tables = make_tables(size, rows_mine // 16, cols)
    half = size // 2
    wide = tables["place"].shape[1] // 2
    rows = tables["f2c"].shape[0]
    slots = tables["mirror"].shape[1]
    chunks = slots // 128
    operands = dict(spatial=spatial.transpose(0, 3, 1, 2), index=kernel_index, sens=sensitivity, data=coil_data)
    operands.update({n: jnp.asarray(tables[n]) for n in TABLES})
    vm = pl.BlockSpec(memory_space=pltpu.VMEM)
    block = pltpu.VMEM((frames, 2, rows_mine, size), F32)
    dma = pltpu.SemaphoreType.DMA
    scratch = {n: pltpu.VMEM(x.shape, x.dtype) for n, x in operands.items()}
    scratch.update(
        kq=pltpu.VMEM((frames, 4, rows, slots), F32),
        sf=pltpu.VMEM((coils, 2, size, 2 * wide), F32),
        imf=pltpu.VMEM((frames, 2, size, 2 * wide), F32),
        res=pltpu.VMEM((frames, 2, size, 2 * wide), F32),
        lc=pltpu.VMEM((2, 4 * half, half), BF),
        ls=pltpu.VMEM((2, 4 * half, half), BF),
        ge=pltpu.VMEM((chunks, 3 * half, 512), BF),
        go=pltpu.VMEM((chunks, 3 * half, 512), BF),
        spa=pltpu.VMEM((chunks, rows, 512), F32),
        spb=pltpu.VMEM((chunks, rows, 512), F32),
        za=pltpu.VMEM((chunks, 3 * rows, 512), BF),
        zb=pltpu.VMEM((chunks, 3 * rows, 512), BF),
        lhc=pltpu.VMEM((4 * half, 3 * slots), BF),
        lhs=pltpu.VMEM((4 * half, 3 * slots), BF),
        oc=pltpu.VMEM((4 * half, half), F32),
        osn=pltpu.VMEM((4 * half, half), F32),
        part=pltpu.VMEM((frames, 2, size, size), F32),
        old=pltpu.VMEM((frames, 2, size, size), BF),
        raw=pltpu.VMEM((nf, frames, rank), F32),
        flat=pltpu.VMEM((32, 128 * rank), F32),
        wide=pltpu.VMEM((128 * rank, 128), F32),
        weights=pltpu.VMEM((nf, frames, rank, 128), F32),
        factors=pltpu.VMEM((rank, 16, 128), F32),
        grad=pltpu.VMEM((rank, 16, 128), F32),
        send1=pltpu.VMEM((frames, nf, 16, 128), BF),
        recv1=pltpu.VMEM((frames, nf, 16, 128), BF),
        send2=pltpu.VMEM((frames, nf, 16, 128), BF),
        recv2=pltpu.VMEM((frames, nf, 16, 128), BF),
        rsend=pltpu.VMEM((frames, nf, 16, 128), F32),
        rrecv=pltpu.VMEM((frames, nf, 16, 128), F32),
        xa=block, xd=block, xsum=block, xs=block,
        total=pltpu.VMEM((frames, 2, rows_mine, -(-size // 128) * 128), F32),
        lsem=dma((len(LOCAL),)),
        wsem=dma((2,)), asem=dma((2, 2)), bsem=dma((2, 2)), rsem=dma((2, 2)),
        s1=dma((2, 2)), r1=dma((2, 2)), s2=dma((2, 2)), r2=dma((2, 2)), s3=dma((2, 2)), r3=dma((2, 2)),
    )
    for first in "pq":
        scratch.update({first + str(n): sem for n, sem in enumerate(row_sems())})
    result, images = pl.pallas_call(
        whole_kernel,
        out_shape=(jax.ShapeDtypeStruct((rank, cols, 2, rows_mine), F32), jax.ShapeDtypeStruct((frames, 2, size, size), BF)),
        in_specs=[vm, pl.BlockSpec(memory_space=pltpu.SMEM)] + [pl.BlockSpec(memory_space=pl.ANY)] * len(LOCAL),
        out_specs=(vm, vm),
        scratch_shapes=scratch,
        compiler_params=pltpu.CompilerParams(vmem_limit_bytes=60 * 2**20, collective_id=0, has_side_effects=True),
    )(temporal, kernel_level, *[operands[n] for n in LOCAL])
    return result.transpose(0, 2, 3, 1), images


def solution(mesh):
    placed = (
        P(None, None, "coil", "frame"),
        P("frame", None),
        P("coil", None, None, None),
        P("frame", "coil", None, None, None),
        P("frame", None, None),
        P("frame", None),
    )
    return jax.shard_map(
        body,
        mesh=mesh,
        in_specs=placed,
        out_specs=(P(None, None, "coil", "frame"), P("frame", None, None, None)),
        check_vma=False,
    )
```

```python
import types

import jax
import jax.numpy as jnp
import ml_dtypes
import numpy as np
from jax import lax
from jax.experimental import pallas as pl
from jax.experimental.pallas import tpu as pltpu
from jax.sharding import PartitionSpec as P

STEP_SIZE = 0.15
BF = jnp.bfloat16
F32 = jnp.float32


def halves(table):
    high = table.astype(ml_dtypes.bfloat16)
    low = (table - high.astype(np.float64)).astype(ml_dtypes.bfloat16)
    return high, low


def make_tables(size, blocks, cols):
    half = size // 2
    slots = -(-(size + 1) // 128) * 128
    rows = -(-(size + 1) // 16) * 16
    p = np.arange(half) + 0.5
    k = np.arange(slots)
    valid = (k <= size).astype(np.float64)
    angle = np.pi / size * np.outer(p, k)
    cos, sin = np.cos(angle) * valid, np.sin(angle) * valid
    cos[:, size] = 0.0
    sin[:, 0] = 0.0
    weight = np.where((k == 0) | (k == size), 0.5, 1.0)
    out = {}
    for name, tab in (("c", cos), ("s", sin)):
        hi, lo = halves(tab)
        out["f1" + name] = np.concatenate([hi, lo], axis=1)
        rhi, rlo = hi[:, :rows].T, lo[:, :rows].T
        out["f2" + name] = np.concatenate([rhi, rhi, rlo], axis=1)
        whi, wlo = halves(tab * weight)
        out["i1" + name] = np.concatenate([whi[:, :rows], whi[:, :rows], wlo[:, :rows]], axis=1)
        parts = []
        for j in range(0, slots, 128):
            parts += [whi.T[j:j + 128], whi.T[j:j + 128], wlo.T[j:j + 128]]
        out["i2" + name] = np.concatenate(parts, axis=0)
    wide = -(-half // 128) * 128
    place = np.zeros((size, 2 * wide))
    q = np.arange(half)
    place[half + q, q] = 1
    place[half - 1 - q, wide + q] = 1
    out["place"] = place.astype(ml_dtypes.bfloat16)
    out["unplace"] = place.T.astype(ml_dtypes.bfloat16)
    out["flip"] = np.eye(half)[::-1].astype(ml_dtypes.bfloat16)
    mirror = np.zeros((2 * size, slots))
    kk = np.arange(size + 1)
    mirror[(2 * size - kk) % (2 * size), kk] = 1
    out["mirror"] = mirror.astype(ml_dtypes.bfloat16)
    out["mirror_rows"] = mirror.T[:rows].astype(ml_dtypes.bfloat16)
    spread = np.zeros((32, 128))
    for c in range(2):
        for rb in range(blocks):
            for j in range(cols):
                spread[2 * j + c, (c * blocks + rb) * cols + j] = 1
    out["spread"] = spread.astype(ml_dtypes.bfloat16)
    return out


TABLES = ("f1c", "f1s", "f2c", "f2s", "i1c", "i1s", "i2c", "i2s", "place", "unplace", "flip", "mirror", "mirror_rows", "spread")


def mm(a, b):
    return jnp.dot(a, b, preferred_element_type=F32)


def split(x):
    high = x.astype(BF)
    low = (x - high.astype(F32)).astype(BF)
    return high, low


def kernel_quads(s, level, t):
    rows = s.f2c.shape[0]
    slots = s.mirror.shape[1]
    size = 2 * s.flip.shape[0]
    values = [level[t, m] * (0.25 / (size * size)) for m in range(level.shape[1])]
    ib = s.index[t].astype(F32).astype(BF)
    flipped = mm(ib, s.mirror[...]).astype(BF)
    low = mm(s.mirror_rows[...], jnp.concatenate([ib[:, :slots], flipped], axis=1))
    quads = (ib[:rows, :slots].astype(F32), flipped[:rows].astype(F32), low[:, :slots], low[:, slots:])
    for n, quad in enumerate(quads):
        value = jnp.full(quad.shape, values[0], F32)
        for m in range(1, len(values)):
            value = jnp.where(quad > m - 0.5, values[m], value)
        s.kq[t, n] = value


def folded(s, x):
    half = s.flip.shape[0]
    left = mm(s.flip[...], x[:half]).astype(BF)
    return mm(jnp.concatenate([x[half:], left], axis=0), s.place[...])


def fold_data(s, t):
    for c in range(s.sens.shape[0]):
        dr, di = folded(s, s.data[t, c, 0]), folded(s, s.data[t, c, 1])
        sr, si = s.sf[c, 0], s.sf[c, 1]
        gr, gi = -(sr * dr + si * di), si * dr - sr * di
        if c:
            gr, gi = s.res[t, 0] + gr, s.res[t, 1] + gi
        s.res[t, 0] = gr
        s.res[t, 1] = gi


def unfold(s, t):
    half = s.flip.shape[0]
    for h in range(2):
        high, low = split(s.res[t, h])
        cols = mm(high, s.unplace[...]) + mm(low, s.unplace[...])
        s.part[t, h, pl.ds(half, half)] = cols[:half]
        high, low = split(cols[half:])
        s.part[t, h, pl.ds(0, half)] = mm(s.flip[...], high) + mm(s.flip[...], low)


def run_pair(s, t, c):
    half = s.flip.shape[0]
    wide = s.place.shape[1] // 2
    rows = s.f2c.shape[0]
    slots = s.mirror.shape[1]
    chunks = slots // 128
    for r in range(0, half, 16):
        parts = {}
        for a, row in (("R", r), ("L", half + r)):
            for b, col in (("R", 0), ("L", wide)):
                sl = (pl.ds(row, 16), pl.ds(col, half))
                sr, si = s.sf[c, 0, sl[0], sl[1]], s.sf[c, 1, sl[0], sl[1]]
                ir, ii = s.imf[t, 0, sl[0], sl[1]], s.imf[t, 1, sl[0], sl[1]]
                parts[a + b] = (sr * ir - si * ii, sr * ii + si * ir)
        for h in range(2):
            rr, rl, lr, ll = (parts[n][h] for n in ("RR", "RL", "LR", "LL"))
            re, ro, le, lo = rr + rl, rr - rl, lr + ll, lr - ll
            for k, (xc, xs) in enumerate(((re + le, ro + lo), (re - le, ro - lo))):
                at = (2 * k + h) * half + r
                hc, wc = split(xc)
                hs, ws = split(xs)
                s.lc[0, pl.ds(at, 16)] = hc
                s.lc[1, pl.ds(at, 16)] = wc
                s.ls[0, pl.ds(at, 16)] = hs
                s.ls[1, pl.ds(at, 16)] = ws
    for n, (lref, tab) in enumerate(((s.lc, s.f1c), (s.ls, s.f1s))):
        both = mm(lref[0], tab[...])
        first = both[:, :slots] + both[:, slots:] + mm(lref[1], tab[:, :slots])
        for k, dest in enumerate((s.ge, s.go)):
            for h in range(2):
                part = first[(2 * k + h) * half:(2 * k + h + 1) * half]
                high, low = split(part)
                for j in range(chunks):
                    lanes = pl.ds((2 * n + h) * 128, 128)
                    dest[j, pl.ds(0, half), lanes] = high[:, j * 128:(j + 1) * 128]
                    dest[j, pl.ds(half, half), lanes] = low[:, j * 128:(j + 1) * 128]
                    dest[j, pl.ds(2 * half, half), lanes] = high[:, j * 128:(j + 1) * 128]
    even = [mm(s.f2c[...], s.ge[j]) for j in range(chunks)]
    odd = [mm(s.f2s[...], s.go[j]) for j in range(chunks)]
    for j in range(chunks):
        for r in range(0, rows, 16):
            rs = pl.ds(r, 16)
            aar, aai, abr, abi = (even[j][r:r + 16, 128 * m:128 * m + 128] for m in range(4))
            bar, bai, bbr, bbi = (odd[j][r:r + 16, 128 * m:128 * m + 128] for m in range(4))
            kpp, kpm, kmp, kmm = (s.kq[t, m, rs, pl.ds(128 * j, 128)] for m in range(4))
            ur, ui, vr, vi = aar - bbr, aai - bbi, aar + bbr, aai + bbi
            wr, wi, qr, qi = abr + bar, abi + bai, abr - bar, abi - bai
            ppr, ppi = kpp * (ur + wi), kpp * (ui - wr)
            mmr, mmi = kmm * (ur - wi), kmm * (ui + wr)
            pmr, pmi = kpm * (vr - qi), kpm * (vi + qr)
            mpr, mpi = kmp * (vr + qi), kmp * (vi - qr)
            s1r, s1i, s2r, s2i = ppr + mmr, ppi + mmi, pmr + mpr, pmi + mpi
            d1r, d1i, d2r, d2i = ppr - mmr, ppi - mmi, pmr - mpr, pmi - mpi
            for dest, vals in ((s.za, (s1r + s2r, s1i + s2i, d2i - d1i, d1r - d2r)), (s.zb, (-(d1i + d2i), d1r + d2r, s2r - s1r, s2i - s1i))):
                for m, value in enumerate(vals):
                    high, low = split(value)
                    lanes = pl.ds(128 * m, 128)
                    dest[j, pl.ds(r, 16), lanes] = high
                    dest[j, pl.ds(rows + r, 16), lanes] = low
                    dest[j, pl.ds(2 * rows + r, 16), lanes] = high
    for j in range(chunks):
        for n, (tab, src) in enumerate(((s.i1c, s.za), (s.i1s, s.zb))):
            high, low = split(mm(tab[...], src[j]))
            for m in range(4):
                dest = s.lhc if m < 2 else s.lhs
                rs = pl.ds((2 * n + m % 2) * half, half)
                for place_at, value in enumerate((high, low, high)):
                    dest[rs, pl.ds(j * 384 + place_at * 128, 128)] = value[:, 128 * m:128 * (m + 1)]
    s.oc[...] = mm(s.lhc[...], s.i2c[...])
    s.osn[...] = mm(s.lhs[...], s.i2s[...])
    for r in range(0, half, 16):
        quad = {}
        for h in range(2):
            ee, oe = s.oc[pl.ds(h * half + r, 16)], s.oc[pl.ds((2 + h) * half + r, 16)]
            eo, oo = s.osn[pl.ds(h * half + r, 16)], s.osn[pl.ds((2 + h) * half + r, 16)]
            quad["RR", h] = (ee + oe) + (eo + oo)
            quad["RL", h] = (ee + oe) - (eo + oo)
            quad["LR", h] = (ee - oe) + (eo - oo)
            quad["LL", h] = (ee - oe) - (eo - oo)
        for a, row in (("R", r), ("L", half + r)):
            for b, col in (("R", 0), ("L", wide)):
                sl = (pl.ds(row, 16), pl.ds(col, half))
                sr, si = s.sf[c, 0, sl[0], sl[1]], s.sf[c, 1, sl[0], sl[1]]
                yr, yi = quad[a + b, 0], quad[a + b, 1]
                s.res[t, 0, sl[0], sl[1]] += sr * yr + si * yi
                s.res[t, 1, sl[0], sl[1]] += sr * yi - si * yr


def plane_shape(sp):
    rank, _, rows, cols = sp.shape
    return rank, rows, rows // 16, cols


def lane_masks(cols, groups):
    lane = lax.broadcasted_iota(jnp.int32, (16, 128), 1)
    return lane


def moves(block, cols, group):
    off, start = group * cols, block * cols
    tile, at = start // 128, start % 128
    first = min(cols, 128 - at)
    out = [(tile, at, off, first)]
    if first < cols:
        out.append((tile + 1, 0, off + first, cols - first))
    return out


def roll(x, shift):
    shift = shift % 128
    return pltpu.roll(x, shift, 1) if shift else x


def enter(peers):
    barrier = pltpu.get_barrier_semaphore()
    frame, coil = lax.axis_index("frame"), lax.axis_index("coil")
    nf, nc = lax.axis_size("frame"), lax.axis_size("coil")

    def greet(i, carry):
        pl.semaphore_signal(barrier, inc=1, device_id={"frame": lax.rem(frame + i, nf)}, device_id_type=pl.DeviceIdType.MESH)
        return carry

    lax.fori_loop(1, nf, greet, 0)
    for step in (1, nc - 1):
        pl.semaphore_signal(barrier, inc=1, device_id={"coil": lax.rem(coil + step, nc)}, device_id_type=pl.DeviceIdType.MESH)
    pl.semaphore_wait(barrier, nf + 1)


def remote(src, dst, send, recv, where):
    return pltpu.make_async_remote_copy(src_ref=src, dst_ref=dst, send_sem=send, recv_sem=recv, device_id=where, device_id_type=pl.DeviceIdType.MESH)


def wait_bytes(ref, sem):
    pltpu.make_async_copy(ref, ref, sem).wait()


def mix_and_send(weights, factors, t, send_buf, recv_buf, sems):
    frame, nf = lax.axis_index("frame"), lax.axis_size("frame")
    rank = factors.shape[0]

    def piece(d):
        total = weights[d, t, pl.ds(0, 1)] * factors[0]
        for r in range(1, rank):
            total += weights[d, t, pl.ds(r, 1)] * factors[r]
        return total.astype(BF)

    def step(i, carry):
        d = lax.rem(frame + i, nf)
        send_buf[t, d] = piece(d)
        remote(send_buf.at[t, d], recv_buf.at[t, frame], sems.at[0, t], sems.at[1, t], {"frame": d}).start()
        return carry

    lax.fori_loop(1, nf, step, 0)
    recv_buf[t, frame] = piece(frame)


def wait_frames(buf, t, sem):
    wait_bytes(buf.at[t, pl.ds(0, buf.shape[1] - 1)], sem)


def place_rows(recv_buf, image, t, cols):
    coil, nf = lax.axis_index("coil"), lax.axis_size("frame")
    size = image.shape[2]
    rows = size // lax.axis_size("coil")
    lane = lax.broadcasted_iota(jnp.int32, (16, 128), 1)
    blocks = rows // 16
    for c in range(2):
        for rb in range(blocks):
            tiles = [jnp.zeros((16, 128), F32) for _ in range(-(-size // 128))]
            for f in range(nf):
                value = recv_buf[t, f].astype(F32)
                for tile, at, off, count in moves(f, cols, c * blocks + rb):
                    inside = (lane >= at) & (lane < at + count)
                    tiles[tile] = jnp.where(inside, roll(value, at - off), tiles[tile])
            at_row = pl.multiple_of(coil * rows + rb * 16, 16)
            for n, value in enumerate(tiles):
                width = min(128, size - 128 * n)
                image[t, c, pl.ds(at_row, 16), pl.ds(128 * n, width)] = value.astype(BF)[:, :width]


def spread_rows(image, t, sems):
    send, recv, _, _ = sems
    coil, nc = lax.axis_index("coil"), lax.axis_size("coil")
    rows = image.shape[2] // nc
    mine = pl.ds(pl.multiple_of(coil * rows, 16), rows)
    for way, step in ((0, 1), (1, nc - 1)):
        for c in (way, 1 - way):
            part = image.at[t, c, mine]
            remote(part, part, send.at[t, way, c], recv.at[t, way, c], {"coil": lax.rem(coil + step, nc)}).start()


def forward_rows(image, t, sems):
    send, recv, send2, recv2 = sems
    coil, nc = lax.axis_index("coil"), lax.axis_size("coil")
    rows = image.shape[2] // nc
    for way, step in ((0, 1), (1, nc - 1)):
        source = lax.rem(coil + nc - step, nc)
        part = image.at[t, way, pl.ds(pl.multiple_of(source * rows, 16), rows)]
        wait_bytes(part, recv.at[t, way, way])
        remote(part, part, send2.at[t, way], recv2.at[t, way], {"coil": lax.rem(coil + step, nc)}).start()


def finish_rows(image, t, sems):
    send, recv, send2, recv2 = sems
    coil, nc = lax.axis_index("coil"), lax.axis_size("coil")
    rows = image.shape[2] // nc
    part = image.at[t, 0, pl.ds(0, rows)]
    for way in range(2):
        wait_bytes(part, recv.at[t, way, 1 - way])
        wait_bytes(part, recv2.at[t, way])
        wait_bytes(part, send2.at[t, way])
        for c in range(2):
            wait_bytes(part, send.at[t, way, c])


def share_images(s, image, cols, sems, between):
    for t in range(2):
        mix_and_send(s.weights, s.factors, t, s.send2, s.recv2, s.bsem)
    between()
    for t in range(2):
        wait_frames(s.recv2, t, s.bsem.at[1, t])
        place_rows(s.recv2, image, t, cols)
        spread_rows(image, t, sems)
    for t in range(2):
        forward_rows(image, t, sems)
    for t in range(2):
        finish_rows(image, t, sems)
        wait_frames(s.send2, t, s.bsem.at[0, t])


def thirds(x):
    high, low = split(x)
    rest = (x - high.astype(F32)) - low.astype(F32)
    return high, low, rest.astype(BF)


def group_mask(rb, blocks, cols):
    lane = lax.broadcasted_iota(jnp.int32, (16, 128), 1)
    first, second = rb * cols, (blocks + rb) * cols
    return ((lane >= first) & (lane < first + cols)) | ((lane >= second) & (lane < second + cols))


def pack_factors(s):
    rank, cols, _, rows = s.spatial.shape
    blocks = rows // 16
    s.flat[...] = jnp.zeros(s.flat.shape, F32)
    for r in range(rank):
        for j in range(cols):
            s.flat[pl.ds(2 * j, 2), pl.ds(128 * r, rows)] = s.spatial[r, j]
    turned = sum(lax.dot_general(x, s.spread[...], (((0,), (0,)), ((), ())), preferred_element_type=F32) for x in thirds(s.flat[...]))
    for r in range(rank):
        total = jnp.zeros((16, 128), F32)
        for rb in range(blocks):
            at = 128 * r + 16 * rb
            total = jnp.where(group_mask(rb, blocks, cols), turned[at:at + 16], total)
        s.factors[r] = total


def unpack_factors(s, spatial_next):
    rank, cols, _, rows = spatial_next.shape
    blocks = rows // 16
    s.wide[...] = jnp.zeros(s.wide.shape, F32)
    for r in range(rank):
        value = s.factors[r]
        for rb in range(blocks):
            s.wide[pl.ds(128 * r + 16 * rb, 16)] = jnp.where(group_mask(rb, blocks, cols), value, 0.0)
    turned = sum(lax.dot_general(s.spread[...], x, (((1,), (1,)), ((), ())), preferred_element_type=F32) for x in thirds(s.wide[...]))
    for r in range(rank):
        for j in range(cols):
            spatial_next[r, j] = turned[2 * j:2 * j + 2, 128 * r:128 * r + rows]


def widen_weights(s):
    nf, frames, rank = s.raw.shape
    one = lax.broadcasted_iota(jnp.int32, (rank, rank), 0) == lax.broadcasted_iota(jnp.int32, (rank, rank), 1)

    def step(d, carry):
        for t in range(frames):
            row = jnp.broadcast_to(s.raw[d, pl.ds(t, 1)], (rank, rank))
            column = jnp.sum(jnp.where(one, row, 0.0), axis=1, keepdims=True)
            s.weights[d, t] = jnp.broadcast_to(column, (rank, 128))
        return carry

    lax.fori_loop(0, nf, step, 0, unroll=8)


def row_sems():
    return [
        pltpu.SemaphoreType.DMA((2, 2, 2)),
        pltpu.SemaphoreType.DMA((2, 2, 2)),
        pltpu.SemaphoreType.DMA((2, 2)),
        pltpu.SemaphoreType.DMA((2, 2)),
    ]


def reduce_start(part, t, xa, xd, sems):
    s1, r1, s2, r2, s3, r3 = sems
    coil, nc = lax.axis_index("coil"), lax.axis_size("coil")
    rows = part.shape[2] // nc
    far = pl.ds(pl.multiple_of(lax.rem(coil + 2, nc) * rows, 16), rows)
    for way, step in ((0, 1), (1, nc - 1)):
        to = lax.rem(coil + step, nc)
        near = pl.ds(pl.multiple_of(to * rows, 16), rows)
        remote(part.at[t, way, far], xa.at[t, way], s1.at[t, way], r1.at[t, way], {"coil": to}).start()
        remote(part.at[t, 1 - way, near], xd.at[t, way], s2.at[t, way], r2.at[t, way], {"coil": to}).start()


def reduce_forward(part, t, xa, xsum, xs, sems):
    s1, r1, s2, r2, s3, r3 = sems
    coil, nc = lax.axis_index("coil"), lax.axis_size("coil")
    rows = part.shape[2] // nc
    for way, step in ((0, 1), (1, nc - 1)):
        to = lax.rem(coil + step, nc)
        near = pl.ds(pl.multiple_of(to * rows, 16), rows)
        wait_bytes(xa.at[t, way], r1.at[t, way])
        xsum[t, way] = xa[t, way] + part[t, way, near]
        remote(xsum.at[t, way], xs.at[t, way], s3.at[t, way], r3.at[t, way], {"coil": to}).start()


def reduce_finish(part, t, xd, xs, total, sems):
    s1, r1, s2, r2, s3, r3 = sems
    coil, nc = lax.axis_index("coil"), lax.axis_size("coil")
    size = part.shape[3]
    rows = part.shape[2] // nc
    mine = pl.ds(pl.multiple_of(coil * rows, 16), rows)
    for way in range(2):
        wait_bytes(xs.at[t, way], r3.at[t, way])
        wait_bytes(xd.at[t, 1 - way], r2.at[t, 1 - way])
        total[t, way, :, pl.ds(0, size)] = part[t, way, mine] + xs[t, way] + xd[t, 1 - way]


def send_columns(total, t, send_buf, recv_buf, sems, cols):
    frame, nf = lax.axis_index("frame"), lax.axis_size("frame")
    rows = total.shape[2]
    blocks = rows // 16
    lane = lax.broadcasted_iota(jnp.int32, (16, 128), 1)
    for f in range(nf):
        value = jnp.zeros((16, 128), F32)
        for c in range(2):
            for rb in range(blocks):
                for tile, at, off, count in moves(f, cols, c * blocks + rb):
                    inside = (lane >= off) & (lane < off + count)
                    value = jnp.where(inside, roll(total[t, c, pl.ds(16 * rb, 16), pl.ds(128 * tile, 128)], off - at), value)
        send_buf[t, f] = value

    def step(i, carry):
        d = lax.rem(frame + i, nf)
        remote(send_buf.at[t, d], recv_buf.at[t, frame], sems.at[0, t], sems.at[1, t], {"frame": d}).start()
        return carry

    lax.fori_loop(1, nf, step, 0)
    recv_buf[t, frame] = send_buf[t, frame]


def gradient_step(weights, recv_buf, t, grad):
    nf = lax.axis_size("frame")
    rank = grad.shape[0]

    def step(f, acc):
        value = recv_buf[t, f]
        return tuple(acc[r] + weights[f, t, pl.ds(r, 1)] * value for r in range(rank))

    acc = lax.fori_loop(0, nf, step, tuple(jnp.zeros((16, 128), F32) for _ in range(rank)))
    for r in range(rank):
        grad[r] = acc[r] if t == 0 else grad[r] + acc[r]


LOCAL = ("spatial", "index", "sens", "data") + TABLES


def whole_kernel(weight, level, *refs, **scratch):
    s = types.SimpleNamespace(**scratch)
    sources, (spatial_next, image) = refs[:len(LOCAL)], refs[len(LOCAL):]
    frame, nf = lax.axis_index("frame"), lax.axis_size("frame")
    cols = spatial_next.shape[1]
    copies = {}
    for n, (name, source) in enumerate(zip(LOCAL, sources)):
        copies[name] = pltpu.make_async_copy(source, scratch[name], s.lsem.at[n])
        copies[name].start()

    def ready(*names):
        for name in names:
            copies[name].wait()

    enter(None)

    def exchange(i, carry):
        remote(weight, s.raw.at[frame], s.wsem.at[0], s.wsem.at[1], {"frame": lax.rem(frame + i, nf)}).start()
        return carry

    lax.fori_loop(1, nf, exchange, 0)
    s.raw[frame] = weight[...]
    ready("spatial", "spread")
    pack_factors(s)
    ready("index", *(n for n in TABLES if n != "spread"))
    kernel_quads(s, level, 0)
    wait_bytes(s.raw.at[pl.ds(0, nf - 1)], s.wsem.at[1])
    widen_weights(s)
    for t in range(2):
        mix_and_send(s.weights, s.factors, t, s.send1, s.recv1, s.asem)
    kernel_quads(s, level, 1)
    ready("sens", "data")
    for c in range(s.sens.shape[0]):
        for h in range(2):
            s.sf[c, h] = folded(s, s.sens[c, h])
    rows1 = (s.p0, s.p1, s.p2, s.p3)
    wait_frames(s.recv1, 0, s.asem.at[1, 0])
    place_rows(s.recv1, s.old, 0, cols)
    spread_rows(s.old, 0, rows1)
    wait_frames(s.recv1, 1, s.asem.at[1, 1])
    place_rows(s.recv1, s.old, 1, cols)
    fold_data(s, 0)
    forward_rows(s.old, 0, rows1)
    spread_rows(s.old, 1, rows1)
    fold_data(s, 1)
    finish_rows(s.old, 0, rows1)
    for h in range(2):
        s.imf[0, h] = folded(s, s.old[0, h])
    sems = (s.s1, s.r1, s.s2, s.r2, s.s3, s.r3)
    coils = s.sens.shape[0]

    def pair(q, carry):
        run_pair(s, q // coils, q % coils)

        @pl.when(q == 0)
        def _():
            forward_rows(s.old, 1, rows1)

        @pl.when(q == coils - 1)
        def _():
            unfold(s, 0)
            reduce_start(s.part, 0, s.xa, s.xd, sems)
            finish_rows(s.old, 1, rows1)
            for h in range(2):
                s.imf[1, h] = folded(s, s.old[1, h])

        @pl.when(q == coils)
        def _():
            reduce_forward(s.part, 0, s.xa, s.xsum, s.xs, sems)

        return carry

    lax.fori_loop(0, 2 * coils, pair, 0)
    unfold(s, 1)
    reduce_start(s.part, 1, s.xa, s.xd, sems)
    reduce_finish(s.part, 0, s.xd, s.xs, s.total, sems)
    send_columns(s.total, 0, s.rsend, s.rrecv, s.rsem, cols)
    reduce_forward(s.part, 1, s.xa, s.xsum, s.xs, sems)
    wait_bytes(s.rrecv.at[0, pl.ds(0, nf - 1)], s.rsem.at[1, 0])
    gradient_step(s.weights, s.rrecv, 0, s.grad)
    reduce_finish(s.part, 1, s.xd, s.xs, s.total, sems)
    send_columns(s.total, 1, s.rsend, s.rrecv, s.rsem, cols)
    wait_bytes(s.rrecv.at[1, pl.ds(0, nf - 1)], s.rsem.at[1, 1])
    gradient_step(s.weights, s.rrecv, 1, s.grad)
    for r in range(s.factors.shape[0]):
        s.factors[r] = s.factors[r] - STEP_SIZE * s.grad[r]
    share_images(s, image, cols, (s.q0, s.q1, s.q2, s.q3), lambda: unpack_factors(s, spatial_next))
    wait_bytes(s.raw.at[pl.ds(0, nf - 1)], s.wsem.at[0])
    for t in range(2):
        wait_frames(s.send1, t, s.asem.at[0, t])
    for t in range(2):
        wait_bytes(s.rrecv.at[t, pl.ds(0, nf - 1)], s.rsem.at[0, t])
        for way in range(2):
            for sem in (s.s1, s.s2, s.s3):
                wait_bytes(s.xa.at[t, way], sem.at[t, way])


def settle_kernel(result, images, result_out, images_out, sems):
    copies = [pltpu.make_async_copy(result, result_out, sems.at[0])]
    frames, parts = images.shape[:2]
    for t in range(frames):
        for h in range(parts):
            copies.append(pltpu.make_async_copy(images.at[t, h], images_out.at[t, h], sems.at[1 + parts * t + h]))
    for copy in copies:
        copy.start()
    for copy in copies:
        copy.wait()


def settle(result, images):
    anywhere = pl.BlockSpec(memory_space=pl.ANY)
    return pl.pallas_call(
        settle_kernel,
        out_shape=(jax.ShapeDtypeStruct(result.shape, result.dtype), jax.ShapeDtypeStruct(images.shape, images.dtype)),
        in_specs=[anywhere, anywhere],
        out_specs=(anywhere, anywhere),
        scratch_shapes=[pltpu.SemaphoreType.DMA((1 + images.shape[0] * images.shape[1],))],
    )(result, images)


def body(spatial, temporal, sensitivity, coil_data, kernel_index, kernel_level):
    size = sensitivity.shape[2]
    rank, _, rows_mine, cols = spatial.shape
    frames, coils = coil_data.shape[:2]
    nf = lax.axis_size("frame")
    tables = make_tables(size, rows_mine // 16, cols)
    half = size // 2
    wide = tables["place"].shape[1] // 2
    rows = tables["f2c"].shape[0]
    slots = tables["mirror"].shape[1]
    chunks = slots // 128
    operands = dict(spatial=spatial.transpose(0, 3, 1, 2), index=kernel_index, sens=sensitivity, data=coil_data)
    operands.update({n: jnp.asarray(tables[n]) for n in TABLES})
    vm = pl.BlockSpec(memory_space=pltpu.VMEM)
    block = pltpu.VMEM((frames, 2, rows_mine, size), F32)
    dma = pltpu.SemaphoreType.DMA
    scratch = {n: pltpu.VMEM(x.shape, x.dtype) for n, x in operands.items()}
    scratch.update(
        kq=pltpu.VMEM((frames, 4, rows, slots), F32),
        sf=pltpu.VMEM((coils, 2, size, 2 * wide), F32),
        imf=pltpu.VMEM((frames, 2, size, 2 * wide), F32),
        res=pltpu.VMEM((frames, 2, size, 2 * wide), F32),
        lc=pltpu.VMEM((2, 4 * half, half), BF),
        ls=pltpu.VMEM((2, 4 * half, half), BF),
        ge=pltpu.VMEM((chunks, 3 * half, 512), BF),
        go=pltpu.VMEM((chunks, 3 * half, 512), BF),
        za=pltpu.VMEM((chunks, 3 * rows, 512), BF),
        zb=pltpu.VMEM((chunks, 3 * rows, 512), BF),
        lhc=pltpu.VMEM((4 * half, 3 * slots), BF),
        lhs=pltpu.VMEM((4 * half, 3 * slots), BF),
        oc=pltpu.VMEM((4 * half, half), F32),
        osn=pltpu.VMEM((4 * half, half), F32),
        part=pltpu.VMEM((frames, 2, size, size), F32),
        old=pltpu.VMEM((frames, 2, size, size), BF),
        raw=pltpu.VMEM((nf, frames, rank), F32),
        flat=pltpu.VMEM((32, 128 * rank), F32),
        wide=pltpu.VMEM((128 * rank, 128), F32),
        weights=pltpu.VMEM((nf, frames, rank, 128), F32),
        factors=pltpu.VMEM((rank, 16, 128), F32),
        grad=pltpu.VMEM((rank, 16, 128), F32),
        send1=pltpu.VMEM((frames, nf, 16, 128), BF),
        recv1=pltpu.VMEM((frames, nf, 16, 128), BF),
        send2=pltpu.VMEM((frames, nf, 16, 128), BF),
        recv2=pltpu.VMEM((frames, nf, 16, 128), BF),
        rsend=pltpu.VMEM((frames, nf, 16, 128), F32),
        rrecv=pltpu.VMEM((frames, nf, 16, 128), F32),
        xa=block, xd=block, xsum=block, xs=block,
        total=pltpu.VMEM((frames, 2, rows_mine, -(-size // 128) * 128), F32),
        lsem=dma((len(LOCAL),)),
        wsem=dma((2,)), asem=dma((2, 2)), bsem=dma((2, 2)), rsem=dma((2, 2)),
        s1=dma((2, 2)), r1=dma((2, 2)), s2=dma((2, 2)), r2=dma((2, 2)), s3=dma((2, 2)), r3=dma((2, 2)),
    )
    for first in "pq":
        scratch.update({first + str(n): sem for n, sem in enumerate(row_sems())})
    result, images = settle(*pl.pallas_call(
        whole_kernel,
        out_shape=(jax.ShapeDtypeStruct((rank, cols, 2, rows_mine), F32), jax.ShapeDtypeStruct((frames, 2, size, size), BF)),
        in_specs=[vm, pl.BlockSpec(memory_space=pltpu.SMEM)] + [pl.BlockSpec(memory_space=pl.ANY)] * len(LOCAL),
        out_specs=(vm, vm),
        scratch_shapes=scratch,
        compiler_params=pltpu.CompilerParams(vmem_limit_bytes=60 * 2**20, collective_id=0, has_side_effects=True),
    )(temporal, kernel_level, *[operands[n] for n in LOCAL]))
    return result.transpose(0, 2, 3, 1), images


def solution(mesh):
    placed = (
        P(None, None, "coil", "frame"),
        P("frame", None),
        P("coil", None, None, None),
        P("frame", "coil", None, None, None),
        P("frame", None, None),
        P("frame", None),
    )
    return jax.shard_map(
        body,
        mesh=mesh,
        in_specs=placed,
        out_specs=(P(None, None, "coil", "frame"), P("frame", None, None, None)),
        check_vma=False,
    )
```

```python
import types

import jax
import jax.numpy as jnp
import ml_dtypes
import numpy as np
from jax import lax
from jax.experimental import pallas as pl
from jax.experimental.pallas import tpu as pltpu
from jax.sharding import PartitionSpec as P

STEP_SIZE = 0.15
BF = jnp.bfloat16
F32 = jnp.float32


def halves(table):
    high = table.astype(ml_dtypes.bfloat16)
    low = (table - high.astype(np.float64)).astype(ml_dtypes.bfloat16)
    return high, low


def make_tables(size, blocks, cols):
    half = size // 2
    slots = -(-(size + 1) // 128) * 128
    rows = -(-(size + 1) // 16) * 16
    p = np.arange(half) + 0.5
    k = np.arange(slots)
    valid = (k <= size).astype(np.float64)
    angle = np.pi / size * np.outer(p, k)
    cos, sin = np.cos(angle) * valid, np.sin(angle) * valid
    cos[:, size] = 0.0
    sin[:, 0] = 0.0
    weight = np.where((k == 0) | (k == size), 0.5, 1.0)
    out = {}
    for name, tab in (("c", cos), ("s", sin)):
        hi, lo = halves(tab)
        out["f1" + name] = np.concatenate([hi, lo], axis=1)
        rhi, rlo = hi[:, :rows].T, lo[:, :rows].T
        out["f2" + name] = np.concatenate([rhi, rhi, rlo], axis=1)
        whi, wlo = halves(tab * weight)
        out["i1" + name] = np.concatenate([whi[:, :rows], whi[:, :rows], wlo[:, :rows]], axis=1)
        parts = []
        for j in range(0, slots, 128):
            parts += [whi.T[j:j + 128], whi.T[j:j + 128], wlo.T[j:j + 128]]
        out["i2" + name] = np.concatenate(parts, axis=0)
    wide = -(-half // 128) * 128
    place = np.zeros((size, 2 * wide))
    q = np.arange(half)
    place[half + q, q] = 1
    place[half - 1 - q, wide + q] = 1
    out["place"] = place.astype(ml_dtypes.bfloat16)
    out["unplace"] = place.T.astype(ml_dtypes.bfloat16)
    out["flip"] = np.eye(half)[::-1].astype(ml_dtypes.bfloat16)
    mirror = np.zeros((2 * size, slots))
    kk = np.arange(size + 1)
    mirror[(2 * size - kk) % (2 * size), kk] = 1
    out["mirror"] = mirror.astype(ml_dtypes.bfloat16)
    out["mirror_rows"] = mirror.T[:rows].astype(ml_dtypes.bfloat16)
    spread = np.zeros((32, 128))
    for c in range(2):
        for rb in range(blocks):
            for j in range(cols):
                spread[2 * j + c, (c * blocks + rb) * cols + j] = 1
    out["spread"] = spread.astype(ml_dtypes.bfloat16)
    return out


TABLES = ("f1c", "f1s", "f2c", "f2s", "i1c", "i1s", "i2c", "i2s", "place", "unplace", "flip", "mirror", "mirror_rows", "spread")


def mm(a, b):
    return jnp.dot(a, b, preferred_element_type=F32)


def split(x):
    high = x.astype(BF)
    low = (x - high.astype(F32)).astype(BF)
    return high, low


def kernel_quads(s, level, t):
    rows = s.f2c.shape[0]
    slots = s.mirror.shape[1]
    size = 2 * s.flip.shape[0]
    values = [level[t, m] * (0.25 / (size * size)) for m in range(level.shape[1])]
    ib = s.index[t].astype(F32).astype(BF)
    flipped = mm(ib, s.mirror[...]).astype(BF)
    low = mm(s.mirror_rows[...], jnp.concatenate([ib[:, :slots], flipped], axis=1))
    quads = (ib[:rows, :slots].astype(F32), flipped[:rows].astype(F32), low[:, :slots], low[:, slots:])
    for n, quad in enumerate(quads):
        value = jnp.full(quad.shape, values[0], F32)
        for m in range(1, len(values)):
            value = jnp.where(quad > m - 0.5, values[m], value)
        s.kq[t, n] = value


def folded(s, x):
    half = s.flip.shape[0]
    left = mm(s.flip[...], x[:half]).astype(BF)
    return mm(jnp.concatenate([x[half:], left], axis=0), s.place[...])


def fold_data(s, t):
    for c in range(s.sens.shape[0]):
        dr, di = folded(s, s.data[t, c, 0]), folded(s, s.data[t, c, 1])
        sr, si = s.sf[c, 0], s.sf[c, 1]
        gr, gi = -(sr * dr + si * di), si * dr - sr * di
        if c:
            gr, gi = s.res[t, 0] + gr, s.res[t, 1] + gi
        s.res[t, 0] = gr
        s.res[t, 1] = gi


def unfold(s, t):
    half = s.flip.shape[0]
    for h in range(2):
        high, low = split(s.res[t, h])
        cols = mm(high, s.unplace[...]) + mm(low, s.unplace[...])
        s.part[t, h, pl.ds(half, half)] = cols[:half]
        high, low = split(cols[half:])
        s.part[t, h, pl.ds(0, half)] = mm(s.flip[...], high) + mm(s.flip[...], low)


def fold_pair(s, t, c):
    half = s.flip.shape[0]
    wide = s.place.shape[1] // 2
    for r in range(0, half, 16):
        parts = {}
        for a, row in (("R", r), ("L", half + r)):
            for b, col in (("R", 0), ("L", wide)):
                sl = (pl.ds(row, 16), pl.ds(col, half))
                sr, si = s.sf[c, 0, sl[0], sl[1]], s.sf[c, 1, sl[0], sl[1]]
                ir, ii = s.imf[t, 0, sl[0], sl[1]], s.imf[t, 1, sl[0], sl[1]]
                parts[a + b] = (sr * ir - si * ii, sr * ii + si * ir)
        for h in range(2):
            rr, rl, lr, ll = (parts[n][h] for n in ("RR", "RL", "LR", "LL"))
            re, ro, le, lo = rr + rl, rr - rl, lr + ll, lr - ll
            for k, (xc, xs) in enumerate(((re + le, ro + lo), (re - le, ro - lo))):
                at = (2 * k + h) * half + r
                hc, wc = split(xc)
                hs, ws = split(xs)
                s.lc[0, pl.ds(at, 16)] = hc
                s.lc[1, pl.ds(at, 16)] = wc
                s.ls[0, pl.ds(at, 16)] = hs
                s.ls[1, pl.ds(at, 16)] = ws


def run_pair(s, t, c):
    half = s.flip.shape[0]
    wide = s.place.shape[1] // 2
    rows = s.f2c.shape[0]
    slots = s.mirror.shape[1]
    chunks = slots // 128
    for n, (lref, tab) in enumerate(((s.lc, s.f1c), (s.ls, s.f1s))):
        both = mm(lref[0], tab[...])
        first = both[:, :slots] + both[:, slots:] + mm(lref[1], tab[:, :slots])
        for k, dest in enumerate((s.ge, s.go)):
            for h in range(2):
                part = first[(2 * k + h) * half:(2 * k + h + 1) * half]
                high, low = split(part)
                for j in range(chunks):
                    lanes = pl.ds((2 * n + h) * 128, 128)
                    dest[j, pl.ds(0, half), lanes] = high[:, j * 128:(j + 1) * 128]
                    dest[j, pl.ds(half, half), lanes] = low[:, j * 128:(j + 1) * 128]
                    dest[j, pl.ds(2 * half, half), lanes] = high[:, j * 128:(j + 1) * 128]
    even = [mm(s.f2c[...], s.ge[j]) for j in range(chunks)]
    odd = [mm(s.f2s[...], s.go[j]) for j in range(chunks)]
    for j in range(chunks):
        for r in range(0, rows, 16):
            rs = pl.ds(r, 16)
            aar, aai, abr, abi = (even[j][r:r + 16, 128 * m:128 * m + 128] for m in range(4))
            bar, bai, bbr, bbi = (odd[j][r:r + 16, 128 * m:128 * m + 128] for m in range(4))
            kpp, kpm, kmp, kmm = (s.kq[t, m, rs, pl.ds(128 * j, 128)] for m in range(4))
            ur, ui, vr, vi = aar - bbr, aai - bbi, aar + bbr, aai + bbi
            wr, wi, qr, qi = abr + bar, abi + bai, abr - bar, abi - bai
            ppr, ppi = kpp * (ur + wi), kpp * (ui - wr)
            mmr, mmi = kmm * (ur - wi), kmm * (ui + wr)
            pmr, pmi = kpm * (vr - qi), kpm * (vi + qr)
            mpr, mpi = kmp * (vr + qi), kmp * (vi - qr)
            s1r, s1i, s2r, s2i = ppr + mmr, ppi + mmi, pmr + mpr, pmi + mpi
            d1r, d1i, d2r, d2i = ppr - mmr, ppi - mmi, pmr - mpr, pmi - mpi
            for dest, vals in ((s.za, (s1r + s2r, s1i + s2i, d2i - d1i, d1r - d2r)), (s.zb, (-(d1i + d2i), d1r + d2r, s2r - s1r, s2i - s1i))):
                for m, value in enumerate(vals):
                    high, low = split(value)
                    lanes = pl.ds(128 * m, 128)
                    dest[j, pl.ds(r, 16), lanes] = high
                    dest[j, pl.ds(rows + r, 16), lanes] = low
                    dest[j, pl.ds(2 * rows + r, 16), lanes] = high
    for j in range(chunks):
        for n, (tab, src) in enumerate(((s.i1c, s.za), (s.i1s, s.zb))):
            high, low = split(mm(tab[...], src[j]))
            for m in range(4):
                dest = s.lhc if m < 2 else s.lhs
                rs = pl.ds((2 * n + m % 2) * half, half)
                for place_at, value in enumerate((high, low, high)):
                    dest[rs, pl.ds(j * 384 + place_at * 128, 128)] = value[:, 128 * m:128 * (m + 1)]
    following = lax.rem(t * s.sens.shape[0] + c + 1, s.res.shape[0] * s.sens.shape[0])
    fold_pair(s, following // s.sens.shape[0], following % s.sens.shape[0])
    s.oc[...] = mm(s.lhc[...], s.i2c[...])
    s.osn[...] = mm(s.lhs[...], s.i2s[...])
    for r in range(0, half, 16):
        quad = {}
        for h in range(2):
            ee, oe = s.oc[pl.ds(h * half + r, 16)], s.oc[pl.ds((2 + h) * half + r, 16)]
            eo, oo = s.osn[pl.ds(h * half + r, 16)], s.osn[pl.ds((2 + h) * half + r, 16)]
            quad["RR", h] = (ee + oe) + (eo + oo)
            quad["RL", h] = (ee + oe) - (eo + oo)
            quad["LR", h] = (ee - oe) + (eo - oo)
            quad["LL", h] = (ee - oe) - (eo - oo)
        for a, row in (("R", r), ("L", half + r)):
            for b, col in (("R", 0), ("L", wide)):
                sl = (pl.ds(row, 16), pl.ds(col, half))
                sr, si = s.sf[c, 0, sl[0], sl[1]], s.sf[c, 1, sl[0], sl[1]]
                yr, yi = quad[a + b, 0], quad[a + b, 1]
                s.res[t, 0, sl[0], sl[1]] += sr * yr + si * yi
                s.res[t, 1, sl[0], sl[1]] += sr * yi - si * yr


def plane_shape(sp):
    rank, _, rows, cols = sp.shape
    return rank, rows, rows // 16, cols


def lane_masks(cols, groups):
    lane = lax.broadcasted_iota(jnp.int32, (16, 128), 1)
    return lane


def moves(block, cols, group):
    off, start = group * cols, block * cols
    tile, at = start // 128, start % 128
    first = min(cols, 128 - at)
    out = [(tile, at, off, first)]
    if first < cols:
        out.append((tile + 1, 0, off + first, cols - first))
    return out


def roll(x, shift):
    shift = shift % 128
    return pltpu.roll(x, shift, 1) if shift else x


def enter(peers):
    barrier = pltpu.get_barrier_semaphore()
    frame, coil = lax.axis_index("frame"), lax.axis_index("coil")
    nf, nc = lax.axis_size("frame"), lax.axis_size("coil")

    def greet(i, carry):
        pl.semaphore_signal(barrier, inc=1, device_id={"frame": lax.rem(frame + i, nf)}, device_id_type=pl.DeviceIdType.MESH)
        return carry

    lax.fori_loop(1, nf, greet, 0)
    for step in (1, nc - 1):
        pl.semaphore_signal(barrier, inc=1, device_id={"coil": lax.rem(coil + step, nc)}, device_id_type=pl.DeviceIdType.MESH)
    pl.semaphore_wait(barrier, nf + 1)


def remote(src, dst, send, recv, where):
    return pltpu.make_async_remote_copy(src_ref=src, dst_ref=dst, send_sem=send, recv_sem=recv, device_id=where, device_id_type=pl.DeviceIdType.MESH)


def wait_bytes(ref, sem):
    pltpu.make_async_copy(ref, ref, sem).wait()


def mix_and_send(weights, factors, t, send_buf, recv_buf, sems):
    frame, nf = lax.axis_index("frame"), lax.axis_size("frame")
    rank = factors.shape[0]

    def piece(d):
        total = weights[d, t, pl.ds(0, 1)] * factors[0]
        for r in range(1, rank):
            total += weights[d, t, pl.ds(r, 1)] * factors[r]
        return total.astype(BF)

    def step(i, carry):
        d = lax.rem(frame + i, nf)
        send_buf[t, d] = piece(d)
        remote(send_buf.at[t, d], recv_buf.at[t, frame], sems.at[0, t], sems.at[1, t], {"frame": d}).start()
        return carry

    lax.fori_loop(1, nf, step, 0)
    recv_buf[t, frame] = piece(frame)


def wait_frames(buf, t, sem):
    wait_bytes(buf.at[t, pl.ds(0, buf.shape[1] - 1)], sem)


def place_rows(recv_buf, image, t, cols):
    coil, nf = lax.axis_index("coil"), lax.axis_size("frame")
    size = image.shape[2]
    rows = size // lax.axis_size("coil")
    lane = lax.broadcasted_iota(jnp.int32, (16, 128), 1)
    blocks = rows // 16
    for c in range(2):
        for rb in range(blocks):
            tiles = [jnp.zeros((16, 128), F32) for _ in range(-(-size // 128))]
            for f in range(nf):
                value = recv_buf[t, f].astype(F32)
                for tile, at, off, count in moves(f, cols, c * blocks + rb):
                    inside = (lane >= at) & (lane < at + count)
                    tiles[tile] = jnp.where(inside, roll(value, at - off), tiles[tile])
            at_row = pl.multiple_of(coil * rows + rb * 16, 16)
            for n, value in enumerate(tiles):
                width = min(128, size - 128 * n)
                image[t, c, pl.ds(at_row, 16), pl.ds(128 * n, width)] = value.astype(BF)[:, :width]


def spread_rows(image, t, sems):
    send, recv, _, _ = sems
    coil, nc = lax.axis_index("coil"), lax.axis_size("coil")
    rows = image.shape[2] // nc
    mine = pl.ds(pl.multiple_of(coil * rows, 16), rows)
    for way, step in ((0, 1), (1, nc - 1)):
        for c in (way, 1 - way):
            part = image.at[t, c, mine]
            remote(part, part, send.at[t, way, c], recv.at[t, way, c], {"coil": lax.rem(coil + step, nc)}).start()


def forward_rows(image, t, sems):
    send, recv, send2, recv2 = sems
    coil, nc = lax.axis_index("coil"), lax.axis_size("coil")
    rows = image.shape[2] // nc
    for way, step in ((0, 1), (1, nc - 1)):
        source = lax.rem(coil + nc - step, nc)
        part = image.at[t, way, pl.ds(pl.multiple_of(source * rows, 16), rows)]
        wait_bytes(part, recv.at[t, way, way])
        remote(part, part, send2.at[t, way], recv2.at[t, way], {"coil": lax.rem(coil + step, nc)}).start()


def finish_rows(image, t, sems):
    send, recv, send2, recv2 = sems
    coil, nc = lax.axis_index("coil"), lax.axis_size("coil")
    rows = image.shape[2] // nc
    part = image.at[t, 0, pl.ds(0, rows)]
    for way in range(2):
        wait_bytes(part, recv.at[t, way, 1 - way])
        wait_bytes(part, recv2.at[t, way])
        wait_bytes(part, send2.at[t, way])
        for c in range(2):
            wait_bytes(part, send.at[t, way, c])


def share_images(s, image, cols, sems, between):
    for t in range(2):
        mix_and_send(s.weights, s.factors, t, s.send2, s.recv2, s.bsem)
    between()
    for t in range(2):
        wait_frames(s.recv2, t, s.bsem.at[1, t])
        place_rows(s.recv2, image, t, cols)
        spread_rows(image, t, sems)
    for t in range(2):
        forward_rows(image, t, sems)
    for t in range(2):
        finish_rows(image, t, sems)
        wait_frames(s.send2, t, s.bsem.at[0, t])


def thirds(x):
    high, low = split(x)
    rest = (x - high.astype(F32)) - low.astype(F32)
    return high, low, rest.astype(BF)


def group_mask(rb, blocks, cols):
    lane = lax.broadcasted_iota(jnp.int32, (16, 128), 1)
    first, second = rb * cols, (blocks + rb) * cols
    return ((lane >= first) & (lane < first + cols)) | ((lane >= second) & (lane < second + cols))


def pack_factors(s):
    rank, cols, _, rows = s.spatial.shape
    blocks = rows // 16
    s.flat[...] = jnp.zeros(s.flat.shape, F32)
    for r in range(rank):
        for j in range(cols):
            s.flat[pl.ds(2 * j, 2), pl.ds(128 * r, rows)] = s.spatial[r, j]
    turned = sum(lax.dot_general(x, s.spread[...], (((0,), (0,)), ((), ())), preferred_element_type=F32) for x in thirds(s.flat[...]))
    for r in range(rank):
        total = jnp.zeros((16, 128), F32)
        for rb in range(blocks):
            at = 128 * r + 16 * rb
            total = jnp.where(group_mask(rb, blocks, cols), turned[at:at + 16], total)
        s.factors[r] = total


def unpack_factors(s, spatial_next):
    rank, cols, _, rows = spatial_next.shape
    blocks = rows // 16
    s.wide[...] = jnp.zeros(s.wide.shape, F32)
    for r in range(rank):
        value = s.factors[r]
        for rb in range(blocks):
            s.wide[pl.ds(128 * r + 16 * rb, 16)] = jnp.where(group_mask(rb, blocks, cols), value, 0.0)
    turned = sum(lax.dot_general(s.spread[...], x, (((1,), (1,)), ((), ())), preferred_element_type=F32) for x in thirds(s.wide[...]))
    for r in range(rank):
        for j in range(cols):
            spatial_next[r, j] = turned[2 * j:2 * j + 2, 128 * r:128 * r + rows]


def widen_weights(s):
    nf, frames, rank = s.raw.shape
    one = lax.broadcasted_iota(jnp.int32, (rank, rank), 0) == lax.broadcasted_iota(jnp.int32, (rank, rank), 1)

    def step(d, carry):
        for t in range(frames):
            row = jnp.broadcast_to(s.raw[d, pl.ds(t, 1)], (rank, rank))
            column = jnp.sum(jnp.where(one, row, 0.0), axis=1, keepdims=True)
            s.weights[d, t] = jnp.broadcast_to(column, (rank, 128))
        return carry

    lax.fori_loop(0, nf, step, 0, unroll=8)


def row_sems():
    return [
        pltpu.SemaphoreType.DMA((2, 2, 2)),
        pltpu.SemaphoreType.DMA((2, 2, 2)),
        pltpu.SemaphoreType.DMA((2, 2)),
        pltpu.SemaphoreType.DMA((2, 2)),
    ]


def reduce_start(part, t, xa, xd, sems):
    s1, r1, s2, r2, s3, r3 = sems
    coil, nc = lax.axis_index("coil"), lax.axis_size("coil")
    rows = part.shape[2] // nc
    far = pl.ds(pl.multiple_of(lax.rem(coil + 2, nc) * rows, 16), rows)
    for way, step in ((0, 1), (1, nc - 1)):
        to = lax.rem(coil + step, nc)
        near = pl.ds(pl.multiple_of(to * rows, 16), rows)
        remote(part.at[t, way, far], xa.at[t, way], s1.at[t, way], r1.at[t, way], {"coil": to}).start()
        remote(part.at[t, 1 - way, near], xd.at[t, way], s2.at[t, way], r2.at[t, way], {"coil": to}).start()


def reduce_forward(part, t, xa, xsum, xs, sems):
    s1, r1, s2, r2, s3, r3 = sems
    coil, nc = lax.axis_index("coil"), lax.axis_size("coil")
    rows = part.shape[2] // nc
    for way, step in ((0, 1), (1, nc - 1)):
        to = lax.rem(coil + step, nc)
        near = pl.ds(pl.multiple_of(to * rows, 16), rows)
        wait_bytes(xa.at[t, way], r1.at[t, way])
        xsum[t, way] = xa[t, way] + part[t, way, near]
        remote(xsum.at[t, way], xs.at[t, way], s3.at[t, way], r3.at[t, way], {"coil": to}).start()


def reduce_finish(part, t, xd, xs, total, sems):
    s1, r1, s2, r2, s3, r3 = sems
    coil, nc = lax.axis_index("coil"), lax.axis_size("coil")
    size = part.shape[3]
    rows = part.shape[2] // nc
    mine = pl.ds(pl.multiple_of(coil * rows, 16), rows)
    for way in range(2):
        wait_bytes(xs.at[t, way], r3.at[t, way])
        wait_bytes(xd.at[t, 1 - way], r2.at[t, 1 - way])
        total[t, way, :, pl.ds(0, size)] = part[t, way, mine] + xs[t, way] + xd[t, 1 - way]


def send_columns(total, t, send_buf, recv_buf, sems, cols):
    frame, nf = lax.axis_index("frame"), lax.axis_size("frame")
    rows = total.shape[2]
    blocks = rows // 16
    lane = lax.broadcasted_iota(jnp.int32, (16, 128), 1)
    for f in range(nf):
        value = jnp.zeros((16, 128), F32)
        for c in range(2):
            for rb in range(blocks):
                for tile, at, off, count in moves(f, cols, c * blocks + rb):
                    inside = (lane >= off) & (lane < off + count)
                    value = jnp.where(inside, roll(total[t, c, pl.ds(16 * rb, 16), pl.ds(128 * tile, 128)], off - at), value)
        send_buf[t, f] = value

    def step(i, carry):
        d = lax.rem(frame + i, nf)
        remote(send_buf.at[t, d], recv_buf.at[t, frame], sems.at[0, t], sems.at[1, t], {"frame": d}).start()
        return carry

    lax.fori_loop(1, nf, step, 0)
    recv_buf[t, frame] = send_buf[t, frame]


def gradient_step(weights, recv_buf, t, grad):
    nf = lax.axis_size("frame")
    rank = grad.shape[0]

    def step(f, acc):
        value = recv_buf[t, f]
        return tuple(acc[r] + weights[f, t, pl.ds(r, 1)] * value for r in range(rank))

    acc = lax.fori_loop(0, nf, step, tuple(jnp.zeros((16, 128), F32) for _ in range(rank)))
    for r in range(rank):
        grad[r] = acc[r] if t == 0 else grad[r] + acc[r]


LOCAL = ("spatial", "index", "sens", "data") + TABLES


def whole_kernel(weight, level, *refs, **scratch):
    s = types.SimpleNamespace(**scratch)
    sources, (spatial_next, image) = refs[:len(LOCAL)], refs[len(LOCAL):]
    frame, nf = lax.axis_index("frame"), lax.axis_size("frame")
    cols = spatial_next.shape[1]
    copies = {}
    for n, (name, source) in enumerate(zip(LOCAL, sources)):
        copies[name] = pltpu.make_async_copy(source, scratch[name], s.lsem.at[n])
        copies[name].start()

    def ready(*names):
        for name in names:
            copies[name].wait()

    enter(None)

    def exchange(i, carry):
        remote(weight, s.raw.at[frame], s.wsem.at[0], s.wsem.at[1], {"frame": lax.rem(frame + i, nf)}).start()
        return carry

    lax.fori_loop(1, nf, exchange, 0)
    s.raw[frame] = weight[...]
    ready("spatial", "spread")
    pack_factors(s)
    ready("index", *(n for n in TABLES if n != "spread"))
    kernel_quads(s, level, 0)
    wait_bytes(s.raw.at[pl.ds(0, nf - 1)], s.wsem.at[1])
    widen_weights(s)
    for t in range(2):
        mix_and_send(s.weights, s.factors, t, s.send1, s.recv1, s.asem)
    kernel_quads(s, level, 1)
    ready("sens", "data")
    for c in range(s.sens.shape[0]):
        for h in range(2):
            s.sf[c, h] = folded(s, s.sens[c, h])
    rows1 = (s.p0, s.p1, s.p2, s.p3)
    wait_frames(s.recv1, 0, s.asem.at[1, 0])
    place_rows(s.recv1, s.old, 0, cols)
    spread_rows(s.old, 0, rows1)
    wait_frames(s.recv1, 1, s.asem.at[1, 1])
    place_rows(s.recv1, s.old, 1, cols)
    fold_data(s, 0)
    forward_rows(s.old, 0, rows1)
    spread_rows(s.old, 1, rows1)
    fold_data(s, 1)
    finish_rows(s.old, 0, rows1)
    for h in range(2):
        s.imf[0, h] = folded(s, s.old[0, h])
    sems = (s.s1, s.r1, s.s2, s.r2, s.s3, s.r3)
    coils = s.sens.shape[0]

    fold_pair(s, 0, 0)

    def pair(q, carry):
        @pl.when(q == coils - 1)
        def _():
            finish_rows(s.old, 1, rows1)
            for h in range(2):
                s.imf[1, h] = folded(s, s.old[1, h])

        run_pair(s, q // coils, q % coils)

        @pl.when(q == 0)
        def _():
            forward_rows(s.old, 1, rows1)

        @pl.when(q == coils - 1)
        def _():
            unfold(s, 0)
            reduce_start(s.part, 0, s.xa, s.xd, sems)

        @pl.when(q == coils)
        def _():
            reduce_forward(s.part, 0, s.xa, s.xsum, s.xs, sems)

        return carry

    lax.fori_loop(0, 2 * coils, pair, 0)
    unfold(s, 1)
    reduce_start(s.part, 1, s.xa, s.xd, sems)
    reduce_finish(s.part, 0, s.xd, s.xs, s.total, sems)
    send_columns(s.total, 0, s.rsend, s.rrecv, s.rsem, cols)
    reduce_forward(s.part, 1, s.xa, s.xsum, s.xs, sems)
    wait_bytes(s.rrecv.at[0, pl.ds(0, nf - 1)], s.rsem.at[1, 0])
    gradient_step(s.weights, s.rrecv, 0, s.grad)
    reduce_finish(s.part, 1, s.xd, s.xs, s.total, sems)
    send_columns(s.total, 1, s.rsend, s.rrecv, s.rsem, cols)
    wait_bytes(s.rrecv.at[1, pl.ds(0, nf - 1)], s.rsem.at[1, 1])
    gradient_step(s.weights, s.rrecv, 1, s.grad)
    for r in range(s.factors.shape[0]):
        s.factors[r] = s.factors[r] - STEP_SIZE * s.grad[r]
    share_images(s, image, cols, (s.q0, s.q1, s.q2, s.q3), lambda: unpack_factors(s, spatial_next))
    wait_bytes(s.raw.at[pl.ds(0, nf - 1)], s.wsem.at[0])
    for t in range(2):
        wait_frames(s.send1, t, s.asem.at[0, t])
    for t in range(2):
        wait_bytes(s.rrecv.at[t, pl.ds(0, nf - 1)], s.rsem.at[0, t])
        for way in range(2):
            for sem in (s.s1, s.s2, s.s3):
                wait_bytes(s.xa.at[t, way], sem.at[t, way])


def settle_kernel(result, images, result_out, images_out, small, large, sems):
    frames, parts = images.shape[:2]
    legs = [(result, small, result_out)]
    legs += [(images.at[t, h], large.at[t, h], images_out.at[t, h]) for t in range(frames) for h in range(parts)]
    into = [pltpu.make_async_copy(src, mid, sems.at[0, n]) for n, (src, mid, _) in enumerate(legs)]
    out = [pltpu.make_async_copy(mid, dst, sems.at[1, n]) for n, (_, mid, dst) in enumerate(legs)]
    for copy in into:
        copy.start()
    for first, second in zip(into, out):
        first.wait()
        second.start()
    for copy in out:
        copy.wait()


def settle(result, images):
    anywhere = pl.BlockSpec(memory_space=pl.ANY)
    return pl.pallas_call(
        settle_kernel,
        out_shape=(jax.ShapeDtypeStruct(result.shape, result.dtype), jax.ShapeDtypeStruct(images.shape, images.dtype)),
        in_specs=[anywhere, anywhere],
        out_specs=(anywhere, anywhere),
        scratch_shapes=[
            pltpu.VMEM(result.shape, result.dtype),
            pltpu.VMEM(images.shape, images.dtype),
            pltpu.SemaphoreType.DMA((2, 1 + images.shape[0] * images.shape[1])),
        ],
    )(result, images)


def body(spatial, temporal, sensitivity, coil_data, kernel_index, kernel_level):
    size = sensitivity.shape[2]
    rank, _, rows_mine, cols = spatial.shape
    frames, coils = coil_data.shape[:2]
    nf = lax.axis_size("frame")
    tables = make_tables(size, rows_mine // 16, cols)
    half = size // 2
    wide = tables["place"].shape[1] // 2
    rows = tables["f2c"].shape[0]
    slots = tables["mirror"].shape[1]
    chunks = slots // 128
    operands = dict(spatial=spatial.transpose(0, 3, 1, 2), index=kernel_index, sens=sensitivity, data=coil_data)
    operands.update({n: jnp.asarray(tables[n]) for n in TABLES})
    vm = pl.BlockSpec(memory_space=pltpu.VMEM)
    block = pltpu.VMEM((frames, 2, rows_mine, size), F32)
    dma = pltpu.SemaphoreType.DMA
    scratch = {n: pltpu.VMEM(x.shape, x.dtype) for n, x in operands.items()}
    scratch.update(
        kq=pltpu.VMEM((frames, 4, rows, slots), F32),
        sf=pltpu.VMEM((coils, 2, size, 2 * wide), F32),
        imf=pltpu.VMEM((frames, 2, size, 2 * wide), F32),
        res=pltpu.VMEM((frames, 2, size, 2 * wide), F32),
        lc=pltpu.VMEM((2, 4 * half, half), BF),
        ls=pltpu.VMEM((2, 4 * half, half), BF),
        ge=pltpu.VMEM((chunks, 3 * half, 512), BF),
        go=pltpu.VMEM((chunks, 3 * half, 512), BF),
        za=pltpu.VMEM((chunks, 3 * rows, 512), BF),
        zb=pltpu.VMEM((chunks, 3 * rows, 512), BF),
        lhc=pltpu.VMEM((4 * half, 3 * slots), BF),
        lhs=pltpu.VMEM((4 * half, 3 * slots), BF),
        oc=pltpu.VMEM((4 * half, half), F32),
        osn=pltpu.VMEM((4 * half, half), F32),
        part=pltpu.VMEM((frames, 2, size, size), F32),
        old=pltpu.VMEM((frames, 2, size, size), BF),
        raw=pltpu.VMEM((nf, frames, rank), F32),
        flat=pltpu.VMEM((32, 128 * rank), F32),
        wide=pltpu.VMEM((128 * rank, 128), F32),
        weights=pltpu.VMEM((nf, frames, rank, 128), F32),
        factors=pltpu.VMEM((rank, 16, 128), F32),
        grad=pltpu.VMEM((rank, 16, 128), F32),
        send1=pltpu.VMEM((frames, nf, 16, 128), BF),
        recv1=pltpu.VMEM((frames, nf, 16, 128), BF),
        send2=pltpu.VMEM((frames, nf, 16, 128), BF),
        recv2=pltpu.VMEM((frames, nf, 16, 128), BF),
        rsend=pltpu.VMEM((frames, nf, 16, 128), F32),
        rrecv=pltpu.VMEM((frames, nf, 16, 128), F32),
        xa=block, xd=block, xsum=block, xs=block,
        total=pltpu.VMEM((frames, 2, rows_mine, -(-size // 128) * 128), F32),
        lsem=dma((len(LOCAL),)),
        wsem=dma((2,)), asem=dma((2, 2)), bsem=dma((2, 2)), rsem=dma((2, 2)),
        s1=dma((2, 2)), r1=dma((2, 2)), s2=dma((2, 2)), r2=dma((2, 2)), s3=dma((2, 2)), r3=dma((2, 2)),
    )
    for first in "pq":
        scratch.update({first + str(n): sem for n, sem in enumerate(row_sems())})
    result, images = settle(*pl.pallas_call(
        whole_kernel,
        out_shape=(jax.ShapeDtypeStruct((rank, cols, 2, rows_mine), F32), jax.ShapeDtypeStruct((frames, 2, size, size), BF)),
        in_specs=[vm, pl.BlockSpec(memory_space=pltpu.SMEM)] + [pl.BlockSpec(memory_space=pl.ANY)] * len(LOCAL),
        out_specs=(vm, vm),
        scratch_shapes=scratch,
        compiler_params=pltpu.CompilerParams(vmem_limit_bytes=60 * 2**20, collective_id=0, has_side_effects=True),
    )(temporal, kernel_level, *[operands[n] for n in LOCAL]))
    return result.transpose(0, 2, 3, 1), images


def solution(mesh):
    placed = (
        P(None, None, "coil", "frame"),
        P("frame", None),
        P("coil", None, None, None),
        P("frame", "coil", None, None, None),
        P("frame", None, None),
        P("frame", None),
    )
    return jax.shard_map(
        body,
        mesh=mesh,
        in_specs=placed,
        out_specs=(P(None, None, "coil", "frame"), P("frame", None, None, None)),
        check_vma=False,
    )
```

```python
import types

import jax
import jax.numpy as jnp
import ml_dtypes
import numpy as np
from jax import lax
from jax.experimental import pallas as pl
from jax.experimental.pallas import tpu as pltpu
from jax.sharding import PartitionSpec as P

STEP_SIZE = 0.15
BF = jnp.bfloat16
F32 = jnp.float32


def halves(table):
    high = table.astype(ml_dtypes.bfloat16)
    low = (table - high.astype(np.float64)).astype(ml_dtypes.bfloat16)
    return high, low


def make_tables(size, blocks, cols):
    half = size // 2
    slots = -(-(size + 1) // 128) * 128
    rows = -(-(size + 1) // 16) * 16
    p = np.arange(half) + 0.5
    k = np.arange(slots)
    valid = (k <= size).astype(np.float64)
    angle = np.pi / size * np.outer(p, k)
    cos, sin = np.cos(angle) * valid, np.sin(angle) * valid
    cos[:, size] = 0.0
    sin[:, 0] = 0.0
    weight = np.where((k == 0) | (k == size), 0.5, 1.0)
    out = {}
    for name, tab in (("c", cos), ("s", sin)):
        hi, lo = halves(tab)
        out["f1" + name] = np.concatenate([hi, lo], axis=1)
        rhi, rlo = hi[:, :rows].T, lo[:, :rows].T
        out["f2" + name] = np.concatenate([rhi, rhi, rlo], axis=1)
        whi, wlo = halves(tab * weight)
        out["i1" + name] = np.concatenate([whi[:, :rows], whi[:, :rows], wlo[:, :rows]], axis=1)
        parts = []
        for j in range(0, slots, 128):
            parts += [whi.T[j:j + 128], whi.T[j:j + 128], wlo.T[j:j + 128]]
        out["i2" + name] = np.concatenate(parts, axis=0)
    wide = -(-half // 128) * 128
    place = np.zeros((size, 2 * wide))
    q = np.arange(half)
    place[half + q, q] = 1
    place[half - 1 - q, wide + q] = 1
    out["place"] = place.astype(ml_dtypes.bfloat16)
    out["unplace"] = place.T.astype(ml_dtypes.bfloat16)
    out["flip"] = np.eye(half)[::-1].astype(ml_dtypes.bfloat16)
    mirror = np.zeros((2 * size, slots))
    kk = np.arange(size + 1)
    mirror[(2 * size - kk) % (2 * size), kk] = 1
    out["mirror"] = mirror.astype(ml_dtypes.bfloat16)
    out["mirror_rows"] = mirror.T[:rows].astype(ml_dtypes.bfloat16)
    spread = np.zeros((32, 128))
    for c in range(2):
        for rb in range(blocks):
            for j in range(cols):
                spread[2 * j + c, (c * blocks + rb) * cols + j] = 1
    out["spread"] = spread.astype(ml_dtypes.bfloat16)
    return out


TABLES = ("f1c", "f1s", "f2c", "f2s", "i1c", "i1s", "i2c", "i2s", "place", "unplace", "flip", "mirror", "mirror_rows", "spread")


def mm(a, b):
    return jnp.dot(a, b, preferred_element_type=F32)


def split(x):
    high = x.astype(BF)
    low = (x - high.astype(F32)).astype(BF)
    return high, low


def kernel_quads(s, level, t):
    rows = s.f2c.shape[0]
    slots = s.mirror.shape[1]
    size = 2 * s.flip.shape[0]
    values = [level[t, m] * (0.25 / (size * size)) for m in range(level.shape[1])]
    ib = s.index[t].astype(F32).astype(BF)
    flipped = mm(ib, s.mirror[...]).astype(BF)
    low = mm(s.mirror_rows[...], jnp.concatenate([ib[:, :slots], flipped], axis=1))
    quads = (ib[:rows, :slots].astype(F32), flipped[:rows].astype(F32), low[:, :slots], low[:, slots:])
    for n, quad in enumerate(quads):
        value = jnp.full(quad.shape, values[0], F32)
        for m in range(1, len(values)):
            value = jnp.where(quad > m - 0.5, values[m], value)
        s.kq[t, n] = value


def folded(s, x):
    half = s.flip.shape[0]
    left = mm(s.flip[...], x[:half]).astype(BF)
    return mm(jnp.concatenate([x[half:], left], axis=0), s.place[...])


def fold_data(s, t):
    for c in range(s.sens.shape[0]):
        dr, di = folded(s, s.data[t, c, 0]), folded(s, s.data[t, c, 1])
        sr, si = s.sf[c, 0], s.sf[c, 1]
        gr, gi = -(sr * dr + si * di), si * dr - sr * di
        if c:
            gr, gi = s.res[t, 0] + gr, s.res[t, 1] + gi
        s.res[t, 0] = gr
        s.res[t, 1] = gi


def unfold(s, t):
    half = s.flip.shape[0]
    for h in range(2):
        high, low = split(s.res[t, h])
        cols = mm(high, s.unplace[...]) + mm(low, s.unplace[...])
        s.part[t, h, pl.ds(half, half)] = cols[:half]
        high, low = split(cols[half:])
        s.part[t, h, pl.ds(0, half)] = mm(s.flip[...], high) + mm(s.flip[...], low)


def run_pair(s, t, c):
    half = s.flip.shape[0]
    wide = s.place.shape[1] // 2
    rows = s.f2c.shape[0]
    slots = s.mirror.shape[1]
    chunks = slots // 128
    for r in range(0, half, 16):
        parts = {}
        for a, row in (("R", r), ("L", half + r)):
            for b, col in (("R", 0), ("L", wide)):
                sl = (pl.ds(row, 16), pl.ds(col, half))
                sr, si = s.sf[c, 0, sl[0], sl[1]], s.sf[c, 1, sl[0], sl[1]]
                ir, ii = s.imf[t, 0, sl[0], sl[1]], s.imf[t, 1, sl[0], sl[1]]
                parts[a + b] = (sr * ir - si * ii, sr * ii + si * ir)
        for h in range(2):
            rr, rl, lr, ll = (parts[n][h] for n in ("RR", "RL", "LR", "LL"))
            re, ro, le, lo = rr + rl, rr - rl, lr + ll, lr - ll
            for k, (xc, xs) in enumerate(((re + le, ro + lo), (re - le, ro - lo))):
                at = (2 * k + h) * half + r
                hc, wc = split(xc)
                hs, ws = split(xs)
                s.lc[0, pl.ds(at, 16)] = hc
                s.lc[1, pl.ds(at, 16)] = wc
                s.ls[0, pl.ds(at, 16)] = hs
                s.ls[1, pl.ds(at, 16)] = ws
    for n, (lref, tab) in enumerate(((s.lc, s.f1c), (s.ls, s.f1s))):
        both = mm(lref[0], tab[...])
        first = both[:, :slots] + both[:, slots:] + mm(lref[1], tab[:, :slots])
        for k, dest in enumerate((s.ge, s.go)):
            for h in range(2):
                part = first[(2 * k + h) * half:(2 * k + h + 1) * half]
                high, low = split(part)
                for j in range(chunks):
                    lanes = pl.ds((2 * n + h) * 128, 128)
                    dest[j, pl.ds(0, half), lanes] = high[:, j * 128:(j + 1) * 128]
                    dest[j, pl.ds(half, half), lanes] = low[:, j * 128:(j + 1) * 128]
                    dest[j, pl.ds(2 * half, half), lanes] = high[:, j * 128:(j + 1) * 128]
    even = [mm(s.f2c[...], s.ge[j]) for j in range(chunks)]
    odd = [mm(s.f2s[...], s.go[j]) for j in range(chunks)]
    for j in range(chunks):
        for r in range(0, rows, 16):
            rs = pl.ds(r, 16)
            aar, aai, abr, abi = (even[j][r:r + 16, 128 * m:128 * m + 128] for m in range(4))
            bar, bai, bbr, bbi = (odd[j][r:r + 16, 128 * m:128 * m + 128] for m in range(4))
            kpp, kpm, kmp, kmm = (s.kq[t, m, rs, pl.ds(128 * j, 128)] for m in range(4))
            ur, ui, vr, vi = aar - bbr, aai - bbi, aar + bbr, aai + bbi
            wr, wi, qr, qi = abr + bar, abi + bai, abr - bar, abi - bai
            ppr, ppi = kpp * (ur + wi), kpp * (ui - wr)
            mmr, mmi = kmm * (ur - wi), kmm * (ui + wr)
            pmr, pmi = kpm * (vr - qi), kpm * (vi + qr)
            mpr, mpi = kmp * (vr + qi), kmp * (vi - qr)
            s1r, s1i, s2r, s2i = ppr + mmr, ppi + mmi, pmr + mpr, pmi + mpi
            d1r, d1i, d2r, d2i = ppr - mmr, ppi - mmi, pmr - mpr, pmi - mpi
            for dest, vals in ((s.za, (s1r + s2r, s1i + s2i, d2i - d1i, d1r - d2r)), (s.zb, (-(d1i + d2i), d1r + d2r, s2r - s1r, s2i - s1i))):
                for m, value in enumerate(vals):
                    high, low = split(value)
                    lanes = pl.ds(128 * m, 128)
                    dest[j, pl.ds(r, 16), lanes] = high
                    dest[j, pl.ds(rows + r, 16), lanes] = low
                    dest[j, pl.ds(2 * rows + r, 16), lanes] = high
    for j in range(chunks):
        for n, (tab, src) in enumerate(((s.i1c, s.za), (s.i1s, s.zb))):
            high, low = split(mm(tab[...], src[j]))
            for m in range(4):
                dest = s.lhc if m < 2 else s.lhs
                rs = pl.ds((2 * n + m % 2) * half, half)
                for place_at, value in enumerate((high, low, high)):
                    dest[rs, pl.ds(j * 384 + place_at * 128, 128)] = value[:, 128 * m:128 * (m + 1)]
    s.oc[...] = mm(s.lhc[...], s.i2c[...])
    s.osn[...] = mm(s.lhs[...], s.i2s[...])
    for r in range(0, half, 16):
        quad = {}
        for h in range(2):
            ee, oe = s.oc[pl.ds(h * half + r, 16)], s.oc[pl.ds((2 + h) * half + r, 16)]
            eo, oo = s.osn[pl.ds(h * half + r, 16)], s.osn[pl.ds((2 + h) * half + r, 16)]
            quad["RR", h] = (ee + oe) + (eo + oo)
            quad["RL", h] = (ee + oe) - (eo + oo)
            quad["LR", h] = (ee - oe) + (eo - oo)
            quad["LL", h] = (ee - oe) - (eo - oo)
        for a, row in (("R", r), ("L", half + r)):
            for b, col in (("R", 0), ("L", wide)):
                sl = (pl.ds(row, 16), pl.ds(col, half))
                sr, si = s.sf[c, 0, sl[0], sl[1]], s.sf[c, 1, sl[0], sl[1]]
                yr, yi = quad[a + b, 0], quad[a + b, 1]
                s.res[t, 0, sl[0], sl[1]] += sr * yr + si * yi
                s.res[t, 1, sl[0], sl[1]] += sr * yi - si * yr


def plane_shape(sp):
    rank, _, rows, cols = sp.shape
    return rank, rows, rows // 16, cols


def lane_masks(cols, groups):
    lane = lax.broadcasted_iota(jnp.int32, (16, 128), 1)
    return lane


def moves(block, cols, group):
    off, start = group * cols, block * cols
    tile, at = start // 128, start % 128
    first = min(cols, 128 - at)
    out = [(tile, at, off, first)]
    if first < cols:
        out.append((tile + 1, 0, off + first, cols - first))
    return out


def roll(x, shift):
    shift = shift % 128
    return pltpu.roll(x, shift, 1) if shift else x


def enter(peers):
    barrier = pltpu.get_barrier_semaphore()
    frame, coil = lax.axis_index("frame"), lax.axis_index("coil")
    nf, nc = lax.axis_size("frame"), lax.axis_size("coil")

    def greet(i, carry):
        pl.semaphore_signal(barrier, inc=1, device_id={"frame": lax.rem(frame + i, nf)}, device_id_type=pl.DeviceIdType.MESH)
        return carry

    lax.fori_loop(1, nf, greet, 0)
    for step in (1, nc - 1):
        pl.semaphore_signal(barrier, inc=1, device_id={"coil": lax.rem(coil + step, nc)}, device_id_type=pl.DeviceIdType.MESH)
    pl.semaphore_wait(barrier, nf + 1)


def remote(src, dst, send, recv, where):
    return pltpu.make_async_remote_copy(src_ref=src, dst_ref=dst, send_sem=send, recv_sem=recv, device_id=where, device_id_type=pl.DeviceIdType.MESH)


def wait_bytes(ref, sem):
    pltpu.make_async_copy(ref, ref, sem).wait()


def mix_and_send(weights, factors, t, send_buf, recv_buf, sems):
    frame, nf = lax.axis_index("frame"), lax.axis_size("frame")
    rank = factors.shape[0]

    def piece(d):
        total = weights[d, t, pl.ds(0, 1)] * factors[0]
        for r in range(1, rank):
            total += weights[d, t, pl.ds(r, 1)] * factors[r]
        return total.astype(BF)

    def step(i, carry):
        d = lax.rem(frame + i, nf)
        send_buf[t, d] = piece(d)
        remote(send_buf.at[t, d], recv_buf.at[t, frame], sems.at[0, t], sems.at[1, t], {"frame": d}).start()
        return carry

    lax.fori_loop(1, nf, step, 0)
    recv_buf[t, frame] = piece(frame)


def wait_frames(buf, t, sem):
    wait_bytes(buf.at[t, pl.ds(0, buf.shape[1] - 1)], sem)


def place_rows(recv_buf, image, t, cols):
    coil, nf = lax.axis_index("coil"), lax.axis_size("frame")
    size = image.shape[2]
    rows = size // lax.axis_size("coil")
    lane = lax.broadcasted_iota(jnp.int32, (16, 128), 1)
    blocks = rows // 16
    for c in range(2):
        for rb in range(blocks):
            tiles = [jnp.zeros((16, 128), F32) for _ in range(-(-size // 128))]
            for f in range(nf):
                value = recv_buf[t, f].astype(F32)
                for tile, at, off, count in moves(f, cols, c * blocks + rb):
                    inside = (lane >= at) & (lane < at + count)
                    tiles[tile] = jnp.where(inside, roll(value, at - off), tiles[tile])
            at_row = pl.multiple_of(coil * rows + rb * 16, 16)
            for n, value in enumerate(tiles):
                width = min(128, size - 128 * n)
                image[t, c, pl.ds(at_row, 16), pl.ds(128 * n, width)] = value.astype(BF)[:, :width]


def spread_rows(image, t, sems):
    send, recv, _, _ = sems
    coil, nc = lax.axis_index("coil"), lax.axis_size("coil")
    rows = image.shape[2] // nc
    mine = pl.ds(pl.multiple_of(coil * rows, 16), rows)
    for way, step in ((0, 1), (1, nc - 1)):
        for c in (way, 1 - way):
            part = image.at[t, c, mine]
            remote(part, part, send.at[t, way, c], recv.at[t, way, c], {"coil": lax.rem(coil + step, nc)}).start()


def forward_rows(image, t, sems):
    send, recv, send2, recv2 = sems
    coil, nc = lax.axis_index("coil"), lax.axis_size("coil")
    rows = image.shape[2] // nc
    for way, step in ((0, 1), (1, nc - 1)):
        source = lax.rem(coil + nc - step, nc)
        part = image.at[t, way, pl.ds(pl.multiple_of(source * rows, 16), rows)]
        wait_bytes(part, recv.at[t, way, way])
        remote(part, part, send2.at[t, way], recv2.at[t, way], {"coil": lax.rem(coil + step, nc)}).start()


def finish_rows(image, t, sems):
    send, recv, send2, recv2 = sems
    coil, nc = lax.axis_index("coil"), lax.axis_size("coil")
    rows = image.shape[2] // nc
    part = image.at[t, 0, pl.ds(0, rows)]
    for way in range(2):
        wait_bytes(part, recv.at[t, way, 1 - way])
        wait_bytes(part, recv2.at[t, way])
        wait_bytes(part, send2.at[t, way])
        for c in range(2):
            wait_bytes(part, send.at[t, way, c])


def share_images(s, image, cols, sems, between):
    for t in range(2):
        mix_and_send(s.weights, s.factors, t, s.send2, s.recv2, s.bsem)
    between()
    for t in range(2):
        wait_frames(s.recv2, t, s.bsem.at[1, t])
        place_rows(s.recv2, image, t, cols)
        spread_rows(image, t, sems)
    for t in range(2):
        forward_rows(image, t, sems)
    for t in range(2):
        finish_rows(image, t, sems)
        wait_frames(s.send2, t, s.bsem.at[0, t])


def thirds(x):
    high, low = split(x)
    rest = (x - high.astype(F32)) - low.astype(F32)
    return high, low, rest.astype(BF)


def group_mask(rb, blocks, cols):
    lane = lax.broadcasted_iota(jnp.int32, (16, 128), 1)
    first, second = rb * cols, (blocks + rb) * cols
    return ((lane >= first) & (lane < first + cols)) | ((lane >= second) & (lane < second + cols))


def pack_factors(s):
    rank, cols, _, rows = s.spatial.shape
    blocks = rows // 16
    s.flat[...] = jnp.zeros(s.flat.shape, F32)
    for r in range(rank):
        for j in range(cols):
            s.flat[pl.ds(2 * j, 2), pl.ds(128 * r, rows)] = s.spatial[r, j]
    turned = sum(lax.dot_general(x, s.spread[...], (((0,), (0,)), ((), ())), preferred_element_type=F32) for x in thirds(s.flat[...]))
    for r in range(rank):
        total = jnp.zeros((16, 128), F32)
        for rb in range(blocks):
            at = 128 * r + 16 * rb
            total = jnp.where(group_mask(rb, blocks, cols), turned[at:at + 16], total)
        s.factors[r] = total


def unpack_factors(s, spatial_next):
    rank, cols, _, rows = spatial_next.shape
    blocks = rows // 16
    s.wide[...] = jnp.zeros(s.wide.shape, F32)
    for r in range(rank):
        value = s.factors[r]
        for rb in range(blocks):
            s.wide[pl.ds(128 * r + 16 * rb, 16)] = jnp.where(group_mask(rb, blocks, cols), value, 0.0)
    turned = sum(lax.dot_general(s.spread[...], x, (((1,), (1,)), ((), ())), preferred_element_type=F32) for x in thirds(s.wide[...]))
    for r in range(rank):
        for j in range(cols):
            spatial_next[r, j] = turned[2 * j:2 * j + 2, 128 * r:128 * r + rows]


def widen_weights(s):
    nf, frames, rank = s.raw.shape
    one = lax.broadcasted_iota(jnp.int32, (rank, rank), 0) == lax.broadcasted_iota(jnp.int32, (rank, rank), 1)

    def step(d, carry):
        for t in range(frames):
            row = jnp.broadcast_to(s.raw[d, pl.ds(t, 1)], (rank, rank))
            column = jnp.sum(jnp.where(one, row, 0.0), axis=1, keepdims=True)
            s.weights[d, t] = jnp.broadcast_to(column, (rank, 128))
        return carry

    lax.fori_loop(0, nf, step, 0, unroll=8)


def row_sems():
    return [
        pltpu.SemaphoreType.DMA((2, 2, 2)),
        pltpu.SemaphoreType.DMA((2, 2, 2)),
        pltpu.SemaphoreType.DMA((2, 2)),
        pltpu.SemaphoreType.DMA((2, 2)),
    ]


def reduce_start(part, t, xa, xd, sems):
    s1, r1, s2, r2, s3, r3 = sems
    coil, nc = lax.axis_index("coil"), lax.axis_size("coil")
    rows = part.shape[2] // nc
    far = pl.ds(pl.multiple_of(lax.rem(coil + 2, nc) * rows, 16), rows)
    for way, step in ((0, 1), (1, nc - 1)):
        to = lax.rem(coil + step, nc)
        near = pl.ds(pl.multiple_of(to * rows, 16), rows)
        remote(part.at[t, way, far], xa.at[t, way], s1.at[t, way], r1.at[t, way], {"coil": to}).start()
        remote(part.at[t, 1 - way, near], xd.at[t, way], s2.at[t, way], r2.at[t, way], {"coil": to}).start()


def reduce_forward(part, t, xa, xsum, xs, sems):
    s1, r1, s2, r2, s3, r3 = sems
    coil, nc = lax.axis_index("coil"), lax.axis_size("coil")
    rows = part.shape[2] // nc
    for way, step in ((0, 1), (1, nc - 1)):
        to = lax.rem(coil + step, nc)
        near = pl.ds(pl.multiple_of(to * rows, 16), rows)
        wait_bytes(xa.at[t, way], r1.at[t, way])
        xsum[t, way] = xa[t, way] + part[t, way, near]
        remote(xsum.at[t, way], xs.at[t, way], s3.at[t, way], r3.at[t, way], {"coil": to}).start()


def reduce_finish(part, t, xd, xs, total, sems):
    s1, r1, s2, r2, s3, r3 = sems
    coil, nc = lax.axis_index("coil"), lax.axis_size("coil")
    size = part.shape[3]
    rows = part.shape[2] // nc
    mine = pl.ds(pl.multiple_of(coil * rows, 16), rows)
    for way in range(2):
        wait_bytes(xs.at[t, way], r3.at[t, way])
        wait_bytes(xd.at[t, 1 - way], r2.at[t, 1 - way])
        total[t, way, :, pl.ds(0, size)] = part[t, way, mine] + xs[t, way] + xd[t, 1 - way]


def send_columns(total, t, send_buf, recv_buf, sems, cols):
    frame, nf = lax.axis_index("frame"), lax.axis_size("frame")
    rows = total.shape[2]
    blocks = rows // 16
    lane = lax.broadcasted_iota(jnp.int32, (16, 128), 1)
    for f in range(nf):
        value = jnp.zeros((16, 128), F32)
        for c in range(2):
            for rb in range(blocks):
                for tile, at, off, count in moves(f, cols, c * blocks + rb):
                    inside = (lane >= off) & (lane < off + count)
                    value = jnp.where(inside, roll(total[t, c, pl.ds(16 * rb, 16), pl.ds(128 * tile, 128)], off - at), value)
        send_buf[t, f] = value

    def step(i, carry):
        d = lax.rem(frame + i, nf)
        remote(send_buf.at[t, d], recv_buf.at[t, frame], sems.at[0, t], sems.at[1, t], {"frame": d}).start()
        return carry

    lax.fori_loop(1, nf, step, 0)
    recv_buf[t, frame] = send_buf[t, frame]


def gradient_step(weights, recv_buf, t, grad):
    nf = lax.axis_size("frame")
    rank = grad.shape[0]

    def step(f, acc):
        value = recv_buf[t, f]
        return tuple(acc[r] + weights[f, t, pl.ds(r, 1)] * value for r in range(rank))

    acc = lax.fori_loop(0, nf, step, tuple(jnp.zeros((16, 128), F32) for _ in range(rank)))
    for r in range(rank):
        grad[r] = acc[r] if t == 0 else grad[r] + acc[r]


LOCAL = ("spatial", "spread", "index", "sens", "data") + TABLES[:-1]


def whole_kernel(weight, level, *refs, **scratch):
    s = types.SimpleNamespace(**scratch)
    sources, (spatial_next, image) = refs[:len(LOCAL)], refs[len(LOCAL):]
    frame, nf = lax.axis_index("frame"), lax.axis_size("frame")
    cols = spatial_next.shape[1]
    copies = {}
    for n, (name, source) in enumerate(zip(LOCAL, sources)):
        copies[name] = pltpu.make_async_copy(source, scratch[name], s.lsem.at[n])
        copies[name].start()

    def ready(*names):
        for name in names:
            copies[name].wait()

    enter(None)

    def exchange(i, carry):
        remote(weight, s.raw.at[frame], s.wsem.at[0], s.wsem.at[1], {"frame": lax.rem(frame + i, nf)}).start()
        return carry

    lax.fori_loop(1, nf, exchange, 0)
    s.raw[frame] = weight[...]
    ready("spatial", "spread")
    pack_factors(s)
    wait_bytes(s.raw.at[pl.ds(0, nf - 1)], s.wsem.at[1])
    widen_weights(s)
    for t in range(2):
        mix_and_send(s.weights, s.factors, t, s.send1, s.recv1, s.asem)
    ready("index", *TABLES[:-1])
    kernel_quads(s, level, 0)
    ready("sens", "data")
    for c in range(s.sens.shape[0]):
        for h in range(2):
            s.sf[c, h] = folded(s, s.sens[c, h])
    rows1 = (s.p0, s.p1, s.p2, s.p3)
    wait_frames(s.recv1, 0, s.asem.at[1, 0])
    place_rows(s.recv1, s.old, 0, cols)
    spread_rows(s.old, 0, rows1)
    wait_frames(s.recv1, 1, s.asem.at[1, 1])
    place_rows(s.recv1, s.old, 1, cols)
    kernel_quads(s, level, 1)
    forward_rows(s.old, 0, rows1)
    spread_rows(s.old, 1, rows1)
    fold_data(s, 0)
    fold_data(s, 1)
    finish_rows(s.old, 0, rows1)
    for h in range(2):
        s.imf[0, h] = folded(s, s.old[0, h])
    sems = (s.s1, s.r1, s.s2, s.r2, s.s3, s.r3)
    coils = s.sens.shape[0]

    def pair(q, carry):
        run_pair(s, q // coils, q % coils)

        @pl.when(q == 0)
        def _():
            forward_rows(s.old, 1, rows1)

        @pl.when(q == coils - 1)
        def _():
            unfold(s, 0)
            reduce_start(s.part, 0, s.xa, s.xd, sems)
            finish_rows(s.old, 1, rows1)
            for h in range(2):
                s.imf[1, h] = folded(s, s.old[1, h])

        @pl.when(q == coils)
        def _():
            reduce_forward(s.part, 0, s.xa, s.xsum, s.xs, sems)

        return carry

    lax.fori_loop(0, 2 * coils, pair, 0)
    unfold(s, 1)
    reduce_start(s.part, 1, s.xa, s.xd, sems)
    reduce_finish(s.part, 0, s.xd, s.xs, s.total, sems)
    send_columns(s.total, 0, s.rsend, s.rrecv, s.rsem, cols)
    reduce_forward(s.part, 1, s.xa, s.xsum, s.xs, sems)
    wait_bytes(s.rrecv.at[0, pl.ds(0, nf - 1)], s.rsem.at[1, 0])
    gradient_step(s.weights, s.rrecv, 0, s.grad)
    reduce_finish(s.part, 1, s.xd, s.xs, s.total, sems)
    send_columns(s.total, 1, s.rsend, s.rrecv, s.rsem, cols)
    wait_bytes(s.rrecv.at[1, pl.ds(0, nf - 1)], s.rsem.at[1, 1])
    gradient_step(s.weights, s.rrecv, 1, s.grad)
    for r in range(s.factors.shape[0]):
        s.factors[r] = s.factors[r] - STEP_SIZE * s.grad[r]
    share_images(s, image, cols, (s.q0, s.q1, s.q2, s.q3), lambda: unpack_factors(s, spatial_next))
    wait_bytes(s.raw.at[pl.ds(0, nf - 1)], s.wsem.at[0])
    for t in range(2):
        wait_frames(s.send1, t, s.asem.at[0, t])
    for t in range(2):
        wait_bytes(s.rrecv.at[t, pl.ds(0, nf - 1)], s.rsem.at[0, t])
        for way in range(2):
            for sem in (s.s1, s.s2, s.s3):
                wait_bytes(s.xa.at[t, way], sem.at[t, way])


def settle_kernel(result, images, result_out, images_out, small, large, sems):
    frames, parts = images.shape[:2]
    legs = [(result, small, result_out)]
    legs += [(images.at[t, h], large.at[t, h], images_out.at[t, h]) for t in range(frames) for h in range(parts)]
    into = [pltpu.make_async_copy(src, mid, sems.at[0, n]) for n, (src, mid, _) in enumerate(legs)]
    out = [pltpu.make_async_copy(mid, dst, sems.at[1, n]) for n, (_, mid, dst) in enumerate(legs)]
    for copy in into:
        copy.start()
    for first, second in zip(into, out):
        first.wait()
        second.start()
    for copy in out:
        copy.wait()


def settle(result, images):
    anywhere = pl.BlockSpec(memory_space=pl.ANY)
    return pl.pallas_call(
        settle_kernel,
        out_shape=(jax.ShapeDtypeStruct(result.shape, result.dtype), jax.ShapeDtypeStruct(images.shape, images.dtype)),
        in_specs=[anywhere, anywhere],
        out_specs=(anywhere, anywhere),
        scratch_shapes=[
            pltpu.VMEM(result.shape, result.dtype),
            pltpu.VMEM(images.shape, images.dtype),
            pltpu.SemaphoreType.DMA((2, 1 + images.shape[0] * images.shape[1])),
        ],
    )(result, images)


def body(spatial, temporal, sensitivity, coil_data, kernel_index, kernel_level):
    size = sensitivity.shape[2]
    rank, _, rows_mine, cols = spatial.shape
    frames, coils = coil_data.shape[:2]
    nf = lax.axis_size("frame")
    tables = make_tables(size, rows_mine // 16, cols)
    half = size // 2
    wide = tables["place"].shape[1] // 2
    rows = tables["f2c"].shape[0]
    slots = tables["mirror"].shape[1]
    chunks = slots // 128
    operands = dict(spatial=spatial.transpose(0, 3, 1, 2), index=kernel_index, sens=sensitivity, data=coil_data)
    operands.update({n: jnp.asarray(tables[n]) for n in TABLES})
    vm = pl.BlockSpec(memory_space=pltpu.VMEM)
    block = pltpu.VMEM((frames, 2, rows_mine, size), F32)
    dma = pltpu.SemaphoreType.DMA
    scratch = {n: pltpu.VMEM(x.shape, x.dtype) for n, x in operands.items()}
    scratch.update(
        kq=pltpu.VMEM((frames, 4, rows, slots), F32),
        sf=pltpu.VMEM((coils, 2, size, 2 * wide), F32),
        imf=pltpu.VMEM((frames, 2, size, 2 * wide), F32),
        res=pltpu.VMEM((frames, 2, size, 2 * wide), F32),
        lc=pltpu.VMEM((2, 4 * half, half), BF),
        ls=pltpu.VMEM((2, 4 * half, half), BF),
        ge=pltpu.VMEM((chunks, 3 * half, 512), BF),
        go=pltpu.VMEM((chunks, 3 * half, 512), BF),
        za=pltpu.VMEM((chunks, 3 * rows, 512), BF),
        zb=pltpu.VMEM((chunks, 3 * rows, 512), BF),
        lhc=pltpu.VMEM((4 * half, 3 * slots), BF),
        lhs=pltpu.VMEM((4 * half, 3 * slots), BF),
        oc=pltpu.VMEM((4 * half, half), F32),
        osn=pltpu.VMEM((4 * half, half), F32),
        part=pltpu.VMEM((frames, 2, size, size), F32),
        old=pltpu.VMEM((frames, 2, size, size), BF),
        raw=pltpu.VMEM((nf, frames, rank), F32),
        flat=pltpu.VMEM((32, 128 * rank), F32),
        wide=pltpu.VMEM((128 * rank, 128), F32),
        weights=pltpu.VMEM((nf, frames, rank, 128), F32),
        factors=pltpu.VMEM((rank, 16, 128), F32),
        grad=pltpu.VMEM((rank, 16, 128), F32),
        send1=pltpu.VMEM((frames, nf, 16, 128), BF),
        recv1=pltpu.VMEM((frames, nf, 16, 128), BF),
        send2=pltpu.VMEM((frames, nf, 16, 128), BF),
        recv2=pltpu.VMEM((frames, nf, 16, 128), BF),
        rsend=pltpu.VMEM((frames, nf, 16, 128), F32),
        rrecv=pltpu.VMEM((frames, nf, 16, 128), F32),
        xa=block, xd=block, xsum=block, xs=block,
        total=pltpu.VMEM((frames, 2, rows_mine, -(-size // 128) * 128), F32),
        lsem=dma((len(LOCAL),)),
        wsem=dma((2,)), asem=dma((2, 2)), bsem=dma((2, 2)), rsem=dma((2, 2)),
        s1=dma((2, 2)), r1=dma((2, 2)), s2=dma((2, 2)), r2=dma((2, 2)), s3=dma((2, 2)), r3=dma((2, 2)),
    )
    for first in "pq":
        scratch.update({first + str(n): sem for n, sem in enumerate(row_sems())})
    result, images = settle(*pl.pallas_call(
        whole_kernel,
        out_shape=(jax.ShapeDtypeStruct((rank, cols, 2, rows_mine), F32), jax.ShapeDtypeStruct((frames, 2, size, size), BF)),
        in_specs=[vm, pl.BlockSpec(memory_space=pltpu.SMEM)] + [pl.BlockSpec(memory_space=pl.ANY)] * len(LOCAL),
        out_specs=(vm, vm),
        scratch_shapes=scratch,
        compiler_params=pltpu.CompilerParams(vmem_limit_bytes=60 * 2**20, collective_id=0, has_side_effects=True),
    )(temporal, kernel_level, *[operands[n] for n in LOCAL]))
    return result.transpose(0, 2, 3, 1), images


def solution(mesh):
    placed = (
        P(None, None, "coil", "frame"),
        P("frame", None),
        P("coil", None, None, None),
        P("frame", "coil", None, None, None),
        P("frame", None, None),
        P("frame", None),
    )
    return jax.shard_map(
        body,
        mesh=mesh,
        in_specs=placed,
        out_specs=(P(None, None, "coil", "frame"), P("frame", None, None, None)),
        check_vma=False,
    )
```

```python
import types

import jax
import jax.numpy as jnp
import ml_dtypes
import numpy as np
from jax import lax
from jax.experimental import pallas as pl
from jax.experimental.pallas import tpu as pltpu
from jax.sharding import PartitionSpec as P

STEP_SIZE = 0.15
BF = jnp.bfloat16
F32 = jnp.float32


def halves(table):
    high = table.astype(ml_dtypes.bfloat16)
    low = (table - high.astype(np.float64)).astype(ml_dtypes.bfloat16)
    return high, low


def make_tables(size, blocks, cols):
    half = size // 2
    slots = -(-(size + 1) // 128) * 128
    rows = -(-(size + 1) // 16) * 16
    p = np.arange(half) + 0.5
    k = np.arange(slots)
    valid = (k <= size).astype(np.float64)
    angle = np.pi / size * np.outer(p, k)
    cos, sin = np.cos(angle) * valid, np.sin(angle) * valid
    cos[:, size] = 0.0
    sin[:, 0] = 0.0
    weight = np.where((k == 0) | (k == size), 0.5, 1.0)
    out = {}
    for name, tab in (("c", cos), ("s", sin)):
        hi, lo = halves(tab)
        out["f1" + name] = np.concatenate([hi, lo], axis=1)
        rhi, rlo = hi[:, :rows].T, lo[:, :rows].T
        out["f2" + name] = np.concatenate([rhi, rhi, rlo], axis=1)
        whi, wlo = halves(tab * weight)
        out["i1" + name] = np.concatenate([whi[:, :rows], whi[:, :rows], wlo[:, :rows]], axis=1)
        parts = []
        for j in range(0, slots, 128):
            parts += [whi.T[j:j + 128], whi.T[j:j + 128], wlo.T[j:j + 128]]
        out["i2" + name] = np.concatenate(parts, axis=0)
    wide = -(-half // 128) * 128
    place = np.zeros((size, 2 * wide))
    q = np.arange(half)
    place[half + q, q] = 1
    place[half - 1 - q, wide + q] = 1
    out["place"] = place.astype(ml_dtypes.bfloat16)
    out["unplace"] = place.T.astype(ml_dtypes.bfloat16)
    out["flip"] = np.eye(half)[::-1].astype(ml_dtypes.bfloat16)
    mirror = np.zeros((2 * size, slots))
    kk = np.arange(size + 1)
    mirror[(2 * size - kk) % (2 * size), kk] = 1
    out["mirror"] = mirror.astype(ml_dtypes.bfloat16)
    out["mirror_rows"] = mirror.T[:rows].astype(ml_dtypes.bfloat16)
    spread = np.zeros((32, 128))
    for c in range(2):
        for rb in range(blocks):
            for j in range(cols):
                spread[2 * j + c, (c * blocks + rb) * cols + j] = 1
    out["spread"] = spread.astype(ml_dtypes.bfloat16)
    return out


TABLES = ("f1c", "f1s", "f2c", "f2s", "i1c", "i1s", "i2c", "i2s", "place", "unplace", "flip", "mirror", "mirror_rows", "spread")


def mm(a, b):
    return jnp.dot(a, b, preferred_element_type=F32)


def split(x):
    high = x.astype(BF)
    low = (x - high.astype(F32)).astype(BF)
    return high, low


def kernel_quads(s, level, t):
    rows = s.f2c.shape[0]
    slots = s.mirror.shape[1]
    size = 2 * s.flip.shape[0]
    values = [level[t, m] * (0.25 / (size * size)) for m in range(level.shape[1])]
    ib = s.index[t].astype(F32).astype(BF)
    flipped = mm(ib, s.mirror[...]).astype(BF)
    low = mm(s.mirror_rows[...], jnp.concatenate([ib[:, :slots], flipped], axis=1))
    quads = (ib[:rows, :slots].astype(F32), flipped[:rows].astype(F32), low[:, :slots], low[:, slots:])
    for n, quad in enumerate(quads):
        value = jnp.full(quad.shape, values[0], F32)
        for m in range(1, len(values)):
            value = jnp.where(quad > m - 0.5, values[m], value)
        s.kq[t, n] = value


def folded(s, x):
    half = s.flip.shape[0]
    left = mm(s.flip[...], x[:half]).astype(BF)
    return mm(jnp.concatenate([x[half:], left], axis=0), s.place[...])


def fold_data(s, t):
    for c in range(s.sens.shape[0]):
        dr, di = folded(s, s.data[t, c, 0]), folded(s, s.data[t, c, 1])
        sr, si = s.sf[c, 0], s.sf[c, 1]
        gr, gi = -(sr * dr + si * di), si * dr - sr * di
        if c:
            gr, gi = s.res[t, 0] + gr, s.res[t, 1] + gi
        s.res[t, 0] = gr
        s.res[t, 1] = gi


def unfold(s, t):
    half = s.flip.shape[0]
    for h in range(2):
        high, low = split(s.res[t, h])
        cols = mm(high, s.unplace[...]) + mm(low, s.unplace[...])
        s.part[t, h, pl.ds(half, half)] = cols[:half]
        high, low = split(cols[half:])
        s.part[t, h, pl.ds(0, half)] = mm(s.flip[...], high) + mm(s.flip[...], low)


def run_pair(s, t, c):
    half = s.flip.shape[0]
    wide = s.place.shape[1] // 2
    rows = s.f2c.shape[0]
    slots = s.mirror.shape[1]
    chunks = slots // 128
    for r in range(0, half, 16):
        parts = {}
        for a, row in (("R", r), ("L", half + r)):
            for b, col in (("R", 0), ("L", wide)):
                sl = (pl.ds(row, 16), pl.ds(col, half))
                sr, si = s.sf[c, 0, sl[0], sl[1]], s.sf[c, 1, sl[0], sl[1]]
                ir, ii = s.imf[t, 0, sl[0], sl[1]], s.imf[t, 1, sl[0], sl[1]]
                parts[a + b] = (sr * ir - si * ii, sr * ii + si * ir)
        for h in range(2):
            rr, rl, lr, ll = (parts[n][h] for n in ("RR", "RL", "LR", "LL"))
            re, ro, le, lo = rr + rl, rr - rl, lr + ll, lr - ll
            for k, (xc, xs) in enumerate(((re + le, ro + lo), (re - le, ro - lo))):
                at = (2 * k + h) * half + r
                hc, wc = split(xc)
                hs, ws = split(xs)
                s.lc[0, pl.ds(at, 16)] = hc
                s.lc[1, pl.ds(at, 16)] = wc
                s.ls[0, pl.ds(at, 16)] = hs
                s.ls[1, pl.ds(at, 16)] = ws
    for n, (lref, tab) in enumerate(((s.lc, s.f1c), (s.ls, s.f1s))):
        both = mm(lref[0], tab[...])
        first = both[:, :slots] + both[:, slots:] + mm(lref[1], tab[:, :slots])
        for k, dest in enumerate((s.ge, s.go)):
            for h in range(2):
                part = first[(2 * k + h) * half:(2 * k + h + 1) * half]
                high, low = split(part)
                for j in range(chunks):
                    lanes = pl.ds((2 * n + h) * 128, 128)
                    dest[j, pl.ds(0, half), lanes] = high[:, j * 128:(j + 1) * 128]
                    dest[j, pl.ds(half, half), lanes] = low[:, j * 128:(j + 1) * 128]
                    dest[j, pl.ds(2 * half, half), lanes] = high[:, j * 128:(j + 1) * 128]
    even = [mm(s.f2c[...], s.ge[j]) for j in range(chunks)]
    odd = [mm(s.f2s[...], s.go[j]) for j in range(chunks)]
    for j in range(chunks):
        for r in range(0, rows, 16):
            rs = pl.ds(r, 16)
            aar, aai, abr, abi = (even[j][r:r + 16, 128 * m:128 * m + 128] for m in range(4))
            bar, bai, bbr, bbi = (odd[j][r:r + 16, 128 * m:128 * m + 128] for m in range(4))
            kpp, kpm, kmp, kmm = (s.kq[t, m, rs, pl.ds(128 * j, 128)] for m in range(4))
            ur, ui, vr, vi = aar - bbr, aai - bbi, aar + bbr, aai + bbi
            wr, wi, qr, qi = abr + bar, abi + bai, abr - bar, abi - bai
            ppr, ppi = kpp * (ur + wi), kpp * (ui - wr)
            mmr, mmi = kmm * (ur - wi), kmm * (ui + wr)
            pmr, pmi = kpm * (vr - qi), kpm * (vi + qr)
            mpr, mpi = kmp * (vr + qi), kmp * (vi - qr)
            s1r, s1i, s2r, s2i = ppr + mmr, ppi + mmi, pmr + mpr, pmi + mpi
            d1r, d1i, d2r, d2i = ppr - mmr, ppi - mmi, pmr - mpr, pmi - mpi
            for dest, vals in ((s.za, (s1r + s2r, s1i + s2i, d2i - d1i, d1r - d2r)), (s.zb, (-(d1i + d2i), d1r + d2r, s2r - s1r, s2i - s1i))):
                for m, value in enumerate(vals):
                    high, low = split(value)
                    lanes = pl.ds(128 * m, 128)
                    dest[j, pl.ds(r, 16), lanes] = high
                    dest[j, pl.ds(rows + r, 16), lanes] = low
                    dest[j, pl.ds(2 * rows + r, 16), lanes] = high
    for j in range(chunks):
        for n, (tab, src) in enumerate(((s.i1c, s.za), (s.i1s, s.zb))):
            high, low = split(mm(tab[...], src[j]))
            for m in range(4):
                dest = s.lhc if m < 2 else s.lhs
                rs = pl.ds((2 * n + m % 2) * half, half)
                for place_at, value in enumerate((high, low, high)):
                    dest[rs, pl.ds(j * 384 + place_at * 128, 128)] = value[:, 128 * m:128 * (m + 1)]
    s.oc[...] = mm(s.lhc[...], s.i2c[...])
    s.osn[...] = mm(s.lhs[...], s.i2s[...])
    for r in range(0, half, 16):
        quad = {}
        for h in range(2):
            ee, oe = s.oc[pl.ds(h * half + r, 16)], s.oc[pl.ds((2 + h) * half + r, 16)]
            eo, oo = s.osn[pl.ds(h * half + r, 16)], s.osn[pl.ds((2 + h) * half + r, 16)]
            quad["RR", h] = (ee + oe) + (eo + oo)
            quad["RL", h] = (ee + oe) - (eo + oo)
            quad["LR", h] = (ee - oe) + (eo - oo)
            quad["LL", h] = (ee - oe) - (eo - oo)
        for a, row in (("R", r), ("L", half + r)):
            for b, col in (("R", 0), ("L", wide)):
                sl = (pl.ds(row, 16), pl.ds(col, half))
                sr, si = s.sf[c, 0, sl[0], sl[1]], s.sf[c, 1, sl[0], sl[1]]
                yr, yi = quad[a + b, 0], quad[a + b, 1]
                s.res[t, 0, sl[0], sl[1]] += sr * yr + si * yi
                s.res[t, 1, sl[0], sl[1]] += sr * yi - si * yr


def plane_shape(sp):
    rank, _, rows, cols = sp.shape
    return rank, rows, rows // 16, cols


def lane_masks(cols, groups):
    lane = lax.broadcasted_iota(jnp.int32, (16, 128), 1)
    return lane


def moves(block, cols, group):
    off, start = group * cols, block * cols
    tile, at = start // 128, start % 128
    first = min(cols, 128 - at)
    out = [(tile, at, off, first)]
    if first < cols:
        out.append((tile + 1, 0, off + first, cols - first))
    return out


def roll(x, shift):
    shift = shift % 128
    return pltpu.roll(x, shift, 1) if shift else x


def enter(peers):
    barrier = pltpu.get_barrier_semaphore()
    frame, coil = lax.axis_index("frame"), lax.axis_index("coil")
    nf, nc = lax.axis_size("frame"), lax.axis_size("coil")

    def greet(i, carry):
        pl.semaphore_signal(barrier, inc=1, device_id={"frame": lax.rem(frame + i, nf)}, device_id_type=pl.DeviceIdType.MESH)
        return carry

    lax.fori_loop(1, nf, greet, 0)
    for step in (1, nc - 1):
        pl.semaphore_signal(barrier, inc=1, device_id={"coil": lax.rem(coil + step, nc)}, device_id_type=pl.DeviceIdType.MESH)
    pl.semaphore_wait(barrier, nf + 1)


def remote(src, dst, send, recv, where):
    return pltpu.make_async_remote_copy(src_ref=src, dst_ref=dst, send_sem=send, recv_sem=recv, device_id=where, device_id_type=pl.DeviceIdType.MESH)


def wait_bytes(ref, sem):
    pltpu.make_async_copy(ref, ref, sem).wait()


def mix_and_send(weights, factors, t, send_buf, recv_buf, sems):
    frame, nf = lax.axis_index("frame"), lax.axis_size("frame")
    rank = factors.shape[0]

    def piece(d):
        total = weights[d, t, pl.ds(0, 1)] * factors[0]
        for r in range(1, rank):
            total += weights[d, t, pl.ds(r, 1)] * factors[r]
        return total.astype(BF)

    def prepare(d, carry):
        send_buf[t, d] = piece(d)
        return carry

    lax.fori_loop(0, nf, prepare, 0, unroll=8)

    def step(i, carry):
        d = lax.rem(frame + i, nf)
        remote(send_buf.at[t, d], recv_buf.at[t, frame], sems.at[0, t], sems.at[1, t], {"frame": d}).start()
        return carry

    lax.fori_loop(1, nf, step, 0)
    recv_buf[t, frame] = send_buf[t, frame]


def wait_frames(buf, t, sem):
    wait_bytes(buf.at[t, pl.ds(0, buf.shape[1] - 1)], sem)


def place_rows(recv_buf, image, t, cols):
    coil, nf = lax.axis_index("coil"), lax.axis_size("frame")
    size = image.shape[2]
    rows = size // lax.axis_size("coil")
    lane = lax.broadcasted_iota(jnp.int32, (16, 128), 1)
    blocks = rows // 16
    for c in range(2):
        for rb in range(blocks):
            tiles = [jnp.zeros((16, 128), F32) for _ in range(-(-size // 128))]
            for f in range(nf):
                value = recv_buf[t, f].astype(F32)
                for tile, at, off, count in moves(f, cols, c * blocks + rb):
                    inside = (lane >= at) & (lane < at + count)
                    tiles[tile] = jnp.where(inside, roll(value, at - off), tiles[tile])
            at_row = pl.multiple_of(coil * rows + rb * 16, 16)
            for n, value in enumerate(tiles):
                width = min(128, size - 128 * n)
                image[t, c, pl.ds(at_row, 16), pl.ds(128 * n, width)] = value.astype(BF)[:, :width]


def spread_rows(image, t, sems):
    send, recv, _, _ = sems
    coil, nc = lax.axis_index("coil"), lax.axis_size("coil")
    rows = image.shape[2] // nc
    mine = pl.ds(pl.multiple_of(coil * rows, 16), rows)
    for way, step in ((0, 1), (1, nc - 1)):
        for c in (way, 1 - way):
            part = image.at[t, c, mine]
            remote(part, part, send.at[t, way, c], recv.at[t, way, c], {"coil": lax.rem(coil + step, nc)}).start()


def forward_rows(image, t, sems):
    send, recv, send2, recv2 = sems
    coil, nc = lax.axis_index("coil"), lax.axis_size("coil")
    rows = image.shape[2] // nc
    for way, step in ((0, 1), (1, nc - 1)):
        source = lax.rem(coil + nc - step, nc)
        part = image.at[t, way, pl.ds(pl.multiple_of(source * rows, 16), rows)]
        wait_bytes(part, recv.at[t, way, way])
        remote(part, part, send2.at[t, way], recv2.at[t, way], {"coil": lax.rem(coil + step, nc)}).start()


def finish_rows(image, t, sems):
    send, recv, send2, recv2 = sems
    coil, nc = lax.axis_index("coil"), lax.axis_size("coil")
    rows = image.shape[2] // nc
    part = image.at[t, 0, pl.ds(0, rows)]
    for way in range(2):
        wait_bytes(part, recv.at[t, way, 1 - way])
        wait_bytes(part, recv2.at[t, way])
        wait_bytes(part, send2.at[t, way])
        for c in range(2):
            wait_bytes(part, send.at[t, way, c])


def share_images(s, image, cols, sems, between):
    for t in range(2):
        mix_and_send(s.weights, s.factors, t, s.send2, s.recv2, s.bsem)
    between()
    for t in range(2):
        wait_frames(s.recv2, t, s.bsem.at[1, t])
        place_rows(s.recv2, image, t, cols)
        spread_rows(image, t, sems)
    for t in range(2):
        forward_rows(image, t, sems)
    for t in range(2):
        finish_rows(image, t, sems)
        wait_frames(s.send2, t, s.bsem.at[0, t])


def thirds(x):
    high, low = split(x)
    rest = (x - high.astype(F32)) - low.astype(F32)
    return high, low, rest.astype(BF)


def group_mask(rb, blocks, cols):
    lane = lax.broadcasted_iota(jnp.int32, (16, 128), 1)
    first, second = rb * cols, (blocks + rb) * cols
    return ((lane >= first) & (lane < first + cols)) | ((lane >= second) & (lane < second + cols))


def pack_factors(s):
    rank, cols, _, rows = s.spatial.shape
    blocks = rows // 16
    s.flat[...] = jnp.zeros(s.flat.shape, F32)
    for r in range(rank):
        for j in range(cols):
            s.flat[pl.ds(2 * j, 2), pl.ds(128 * r, rows)] = s.spatial[r, j]
    turned = sum(lax.dot_general(x, s.spread[...], (((0,), (0,)), ((), ())), preferred_element_type=F32) for x in thirds(s.flat[...]))
    for r in range(rank):
        total = jnp.zeros((16, 128), F32)
        for rb in range(blocks):
            at = 128 * r + 16 * rb
            total = jnp.where(group_mask(rb, blocks, cols), turned[at:at + 16], total)
        s.factors[r] = total


def unpack_factors(s, spatial_next):
    rank, cols, _, rows = spatial_next.shape
    blocks = rows // 16
    s.wide[...] = jnp.zeros(s.wide.shape, F32)
    for r in range(rank):
        value = s.factors[r]
        for rb in range(blocks):
            s.wide[pl.ds(128 * r + 16 * rb, 16)] = jnp.where(group_mask(rb, blocks, cols), value, 0.0)
    turned = sum(lax.dot_general(s.spread[...], x, (((1,), (1,)), ((), ())), preferred_element_type=F32) for x in thirds(s.wide[...]))
    for r in range(rank):
        for j in range(cols):
            spatial_next[r, j] = turned[2 * j:2 * j + 2, 128 * r:128 * r + rows]


def widen_weights(s):
    nf, frames, rank = s.raw.shape
    one = lax.broadcasted_iota(jnp.int32, (rank, rank), 0) == lax.broadcasted_iota(jnp.int32, (rank, rank), 1)

    def step(d, carry):
        for t in range(frames):
            row = jnp.broadcast_to(s.raw[d, pl.ds(t, 1)], (rank, rank))
            column = jnp.sum(jnp.where(one, row, 0.0), axis=1, keepdims=True)
            s.weights[d, t] = jnp.broadcast_to(column, (rank, 128))
        return carry

    lax.fori_loop(0, nf, step, 0, unroll=8)


def row_sems():
    return [
        pltpu.SemaphoreType.DMA((2, 2, 2)),
        pltpu.SemaphoreType.DMA((2, 2, 2)),
        pltpu.SemaphoreType.DMA((2, 2)),
        pltpu.SemaphoreType.DMA((2, 2)),
    ]


def reduce_start(part, t, xa, xd, sems):
    s1, r1, s2, r2, s3, r3 = sems
    coil, nc = lax.axis_index("coil"), lax.axis_size("coil")
    rows = part.shape[2] // nc
    far = pl.ds(pl.multiple_of(lax.rem(coil + 2, nc) * rows, 16), rows)
    for way, step in ((0, 1), (1, nc - 1)):
        to = lax.rem(coil + step, nc)
        near = pl.ds(pl.multiple_of(to * rows, 16), rows)
        remote(part.at[t, way, far], xa.at[t, way], s1.at[t, way], r1.at[t, way], {"coil": to}).start()
        remote(part.at[t, 1 - way, near], xd.at[t, way], s2.at[t, way], r2.at[t, way], {"coil": to}).start()


def reduce_forward(part, t, xa, xsum, xs, sems):
    s1, r1, s2, r2, s3, r3 = sems
    coil, nc = lax.axis_index("coil"), lax.axis_size("coil")
    rows = part.shape[2] // nc
    for way, step in ((0, 1), (1, nc - 1)):
        to = lax.rem(coil + step, nc)
        near = pl.ds(pl.multiple_of(to * rows, 16), rows)
        wait_bytes(xa.at[t, way], r1.at[t, way])
        xsum[t, way] = xa[t, way] + part[t, way, near]
        remote(xsum.at[t, way], xs.at[t, way], s3.at[t, way], r3.at[t, way], {"coil": to}).start()


def reduce_finish(part, t, xd, xs, total, sems):
    s1, r1, s2, r2, s3, r3 = sems
    coil, nc = lax.axis_index("coil"), lax.axis_size("coil")
    size = part.shape[3]
    rows = part.shape[2] // nc
    mine = pl.ds(pl.multiple_of(coil * rows, 16), rows)
    for way in range(2):
        wait_bytes(xs.at[t, way], r3.at[t, way])
        wait_bytes(xd.at[t, 1 - way], r2.at[t, 1 - way])
        total[t, way, :, pl.ds(0, size)] = part[t, way, mine] + xs[t, way] + xd[t, 1 - way]


def send_columns(total, t, send_buf, recv_buf, sems, cols):
    frame, nf = lax.axis_index("frame"), lax.axis_size("frame")
    rows = total.shape[2]
    blocks = rows // 16
    lane = lax.broadcasted_iota(jnp.int32, (16, 128), 1)
    for f in range(nf):
        value = jnp.zeros((16, 128), F32)
        for c in range(2):
            for rb in range(blocks):
                for tile, at, off, count in moves(f, cols, c * blocks + rb):
                    inside = (lane >= off) & (lane < off + count)
                    value = jnp.where(inside, roll(total[t, c, pl.ds(16 * rb, 16), pl.ds(128 * tile, 128)], off - at), value)
        send_buf[t, f] = value

    def step(i, carry):
        d = lax.rem(frame + i, nf)
        remote(send_buf.at[t, d], recv_buf.at[t, frame], sems.at[0, t], sems.at[1, t], {"frame": d}).start()
        return carry

    lax.fori_loop(1, nf, step, 0)
    recv_buf[t, frame] = send_buf[t, frame]


def gradient_step(weights, recv_buf, t, grad):
    nf = lax.axis_size("frame")
    rank = grad.shape[0]

    def step(f, acc):
        value = recv_buf[t, f]
        return tuple(acc[r] + weights[f, t, pl.ds(r, 1)] * value for r in range(rank))

    acc = lax.fori_loop(0, nf, step, tuple(jnp.zeros((16, 128), F32) for _ in range(rank)))
    for r in range(rank):
        grad[r] = acc[r] if t == 0 else grad[r] + acc[r]


LOCAL = ("spatial", "spread", "index", "sens", "data") + TABLES[:-1]


def whole_kernel(weight, level, *refs, **scratch):
    s = types.SimpleNamespace(**scratch)
    sources, (spatial_next, image) = refs[:len(LOCAL)], refs[len(LOCAL):]
    frame, nf = lax.axis_index("frame"), lax.axis_size("frame")
    cols = spatial_next.shape[1]
    copies = {}
    for n, (name, source) in enumerate(zip(LOCAL, sources)):
        copies[name] = pltpu.make_async_copy(source, scratch[name], s.lsem.at[n])
        copies[name].start()

    def ready(*names):
        for name in names:
            copies[name].wait()

    enter(None)

    def exchange(i, carry):
        remote(weight, s.raw.at[frame], s.wsem.at[0], s.wsem.at[1], {"frame": lax.rem(frame + i, nf)}).start()
        return carry

    lax.fori_loop(1, nf, exchange, 0)
    s.raw[frame] = weight[...]
    ready("spatial", "spread")
    pack_factors(s)
    wait_bytes(s.raw.at[pl.ds(0, nf - 1)], s.wsem.at[1])
    widen_weights(s)
    for t in range(2):
        mix_and_send(s.weights, s.factors, t, s.send1, s.recv1, s.asem)
    ready("index", *TABLES[:-1])
    kernel_quads(s, level, 0)
    ready("sens", "data")
    for c in range(s.sens.shape[0]):
        for h in range(2):
            s.sf[c, h] = folded(s, s.sens[c, h])
    rows1 = (s.p0, s.p1, s.p2, s.p3)
    wait_frames(s.recv1, 0, s.asem.at[1, 0])
    place_rows(s.recv1, s.old, 0, cols)
    spread_rows(s.old, 0, rows1)
    wait_frames(s.recv1, 1, s.asem.at[1, 1])
    place_rows(s.recv1, s.old, 1, cols)
    kernel_quads(s, level, 1)
    forward_rows(s.old, 0, rows1)
    spread_rows(s.old, 1, rows1)
    fold_data(s, 0)
    fold_data(s, 1)
    finish_rows(s.old, 0, rows1)
    for h in range(2):
        s.imf[0, h] = folded(s, s.old[0, h])
    sems = (s.s1, s.r1, s.s2, s.r2, s.s3, s.r3)
    coils = s.sens.shape[0]

    def pair(q, carry):
        run_pair(s, q // coils, q % coils)

        @pl.when(q == 0)
        def _():
            forward_rows(s.old, 1, rows1)

        @pl.when(q == coils - 1)
        def _():
            unfold(s, 0)
            reduce_start(s.part, 0, s.xa, s.xd, sems)
            finish_rows(s.old, 1, rows1)
            for h in range(2):
                s.imf[1, h] = folded(s, s.old[1, h])

        @pl.when(q == coils)
        def _():
            reduce_forward(s.part, 0, s.xa, s.xsum, s.xs, sems)

        return carry

    lax.fori_loop(0, 2 * coils, pair, 0)
    unfold(s, 1)
    reduce_start(s.part, 1, s.xa, s.xd, sems)
    reduce_finish(s.part, 0, s.xd, s.xs, s.total, sems)
    send_columns(s.total, 0, s.rsend, s.rrecv, s.rsem, cols)
    reduce_forward(s.part, 1, s.xa, s.xsum, s.xs, sems)
    wait_bytes(s.rrecv.at[0, pl.ds(0, nf - 1)], s.rsem.at[1, 0])
    gradient_step(s.weights, s.rrecv, 0, s.grad)
    reduce_finish(s.part, 1, s.xd, s.xs, s.total, sems)
    send_columns(s.total, 1, s.rsend, s.rrecv, s.rsem, cols)
    wait_bytes(s.rrecv.at[1, pl.ds(0, nf - 1)], s.rsem.at[1, 1])
    gradient_step(s.weights, s.rrecv, 1, s.grad)
    for r in range(s.factors.shape[0]):
        s.factors[r] = s.factors[r] - STEP_SIZE * s.grad[r]
    share_images(s, image, cols, (s.q0, s.q1, s.q2, s.q3), lambda: unpack_factors(s, spatial_next))
    wait_bytes(s.raw.at[pl.ds(0, nf - 1)], s.wsem.at[0])
    for t in range(2):
        wait_frames(s.send1, t, s.asem.at[0, t])
    for t in range(2):
        wait_bytes(s.rrecv.at[t, pl.ds(0, nf - 1)], s.rsem.at[0, t])
        for way in range(2):
            for sem in (s.s1, s.s2, s.s3):
                wait_bytes(s.xa.at[t, way], sem.at[t, way])


def settle_kernel(result, images, result_out, images_out, small, large, sems):
    frames, parts = images.shape[:2]
    legs = [(result, small, result_out)]
    legs += [(images.at[t, h], large.at[t, h], images_out.at[t, h]) for t in range(frames) for h in range(parts)]
    into = [pltpu.make_async_copy(src, mid, sems.at[0, n]) for n, (src, mid, _) in enumerate(legs)]
    out = [pltpu.make_async_copy(mid, dst, sems.at[1, n]) for n, (_, mid, dst) in enumerate(legs)]
    for copy in into:
        copy.start()
    for first, second in zip(into, out):
        first.wait()
        second.start()
    for copy in out:
        copy.wait()


def settle(result, images):
    anywhere = pl.BlockSpec(memory_space=pl.ANY)
    return pl.pallas_call(
        settle_kernel,
        out_shape=(jax.ShapeDtypeStruct(result.shape, result.dtype), jax.ShapeDtypeStruct(images.shape, images.dtype)),
        in_specs=[anywhere, anywhere],
        out_specs=(anywhere, anywhere),
        scratch_shapes=[
            pltpu.VMEM(result.shape, result.dtype),
            pltpu.VMEM(images.shape, images.dtype),
            pltpu.SemaphoreType.DMA((2, 1 + images.shape[0] * images.shape[1])),
        ],
    )(result, images)


def body(spatial, temporal, sensitivity, coil_data, kernel_index, kernel_level):
    size = sensitivity.shape[2]
    rank, _, rows_mine, cols = spatial.shape
    frames, coils = coil_data.shape[:2]
    nf = lax.axis_size("frame")
    tables = make_tables(size, rows_mine // 16, cols)
    half = size // 2
    wide = tables["place"].shape[1] // 2
    rows = tables["f2c"].shape[0]
    slots = tables["mirror"].shape[1]
    chunks = slots // 128
    operands = dict(spatial=spatial.transpose(0, 3, 1, 2), index=kernel_index, sens=sensitivity, data=coil_data)
    operands.update({n: jnp.asarray(tables[n]) for n in TABLES})
    vm = pl.BlockSpec(memory_space=pltpu.VMEM)
    block = pltpu.VMEM((frames, 2, rows_mine, size), F32)
    dma = pltpu.SemaphoreType.DMA
    scratch = {n: pltpu.VMEM(x.shape, x.dtype) for n, x in operands.items()}
    scratch.update(
        kq=pltpu.VMEM((frames, 4, rows, slots), F32),
        sf=pltpu.VMEM((coils, 2, size, 2 * wide), F32),
        imf=pltpu.VMEM((frames, 2, size, 2 * wide), F32),
        res=pltpu.VMEM((frames, 2, size, 2 * wide), F32),
        lc=pltpu.VMEM((2, 4 * half, half), BF),
        ls=pltpu.VMEM((2, 4 * half, half), BF),
        ge=pltpu.VMEM((chunks, 3 * half, 512), BF),
        go=pltpu.VMEM((chunks, 3 * half, 512), BF),
        za=pltpu.VMEM((chunks, 3 * rows, 512), BF),
        zb=pltpu.VMEM((chunks, 3 * rows, 512), BF),
        lhc=pltpu.VMEM((4 * half, 3 * slots), BF),
        lhs=pltpu.VMEM((4 * half, 3 * slots), BF),
        oc=pltpu.VMEM((4 * half, half), F32),
        osn=pltpu.VMEM((4 * half, half), F32),
        part=pltpu.VMEM((frames, 2, size, size), F32),
        old=pltpu.VMEM((frames, 2, size, size), BF),
        raw=pltpu.VMEM((nf, frames, rank), F32),
        flat=pltpu.VMEM((32, 128 * rank), F32),
        wide=pltpu.VMEM((128 * rank, 128), F32),
        weights=pltpu.VMEM((nf, frames, rank, 128), F32),
        factors=pltpu.VMEM((rank, 16, 128), F32),
        grad=pltpu.VMEM((rank, 16, 128), F32),
        send1=pltpu.VMEM((frames, nf, 16, 128), BF),
        recv1=pltpu.VMEM((frames, nf, 16, 128), BF),
        send2=pltpu.VMEM((frames, nf, 16, 128), BF),
        recv2=pltpu.VMEM((frames, nf, 16, 128), BF),
        rsend=pltpu.VMEM((frames, nf, 16, 128), F32),
        rrecv=pltpu.VMEM((frames, nf, 16, 128), F32),
        xa=block, xd=block, xsum=block, xs=block,
        total=pltpu.VMEM((frames, 2, rows_mine, -(-size // 128) * 128), F32),
        lsem=dma((len(LOCAL),)),
        wsem=dma((2,)), asem=dma((2, 2)), bsem=dma((2, 2)), rsem=dma((2, 2)),
        s1=dma((2, 2)), r1=dma((2, 2)), s2=dma((2, 2)), r2=dma((2, 2)), s3=dma((2, 2)), r3=dma((2, 2)),
    )
    for first in "pq":
        scratch.update({first + str(n): sem for n, sem in enumerate(row_sems())})
    result, images = settle(*pl.pallas_call(
        whole_kernel,
        out_shape=(jax.ShapeDtypeStruct((rank, cols, 2, rows_mine), F32), jax.ShapeDtypeStruct((frames, 2, size, size), BF)),
        in_specs=[vm, pl.BlockSpec(memory_space=pltpu.SMEM)] + [pl.BlockSpec(memory_space=pl.ANY)] * len(LOCAL),
        out_specs=(vm, vm),
        scratch_shapes=scratch,
        compiler_params=pltpu.CompilerParams(vmem_limit_bytes=60 * 2**20, collective_id=0, has_side_effects=True),
    )(temporal, kernel_level, *[operands[n] for n in LOCAL]))
    return result.transpose(0, 2, 3, 1), images


def solution(mesh):
    placed = (
        P(None, None, "coil", "frame"),
        P("frame", None),
        P("coil", None, None, None),
        P("frame", "coil", None, None, None),
        P("frame", None, None),
        P("frame", None),
    )
    return jax.shard_map(
        body,
        mesh=mesh,
        in_specs=placed,
        out_specs=(P(None, None, "coil", "frame"), P("frame", None, None, None)),
        check_vma=False,
    )
```
